256 devices in a mesh: dp: 32 (over x, y, core), tensor: 8 (over z).
Axes of the slice: x: 4, y: 4, z: 8, core: 2. Of those that a mesh axis runs over, the one named last changes fastest.
Arguments:
- activations: bfloat16 [4096, 16384], P('dp', 'tensor'), may hold values from -1 to 1
- weight: bfloat16 [16384, 12288], P('dp', 'tensor'), may hold values from -0.046875 to 0.046875
- grad_out: bfloat16 [4096, 12288], P('dp', 'tensor'), may hold values from -6 to 6
Outputs:
- grad_input: bfloat16 [4096, 16384], P('dp', 'tensor')
- grad_weight: float32 [16384, 12288], P('dp', 'tensor')
The draws below stay inside these ranges and needn't reach their ends.
All inputs are finite; a program needn't handle non-finite values.
Results may differ from the reference program's by a relative error of at most 0.02.
Values may be sent and summed in bfloat16 or wider, within the bound.
No kernel may reach another device: no remote copies, remote signals or barrier semaphores. Data moves between devices by JAX's collectives and lax.ppermute only.
A program may use at most 128 MiB of HBM per device.

```python
import math
import jax
import jax.numpy as jnp
from jax import lax

BLOCK = 1024
WIDTH = 16384
OUT_COLS = 12288
TOKENS = 4096
N_TENSOR = 8


def draw_activations(key, part):
    key = jax.random.fold_in(key, 11)
    subkeys = jax.random.split(key, 3)
    entries = jnp.clip(jax.random.normal(subkeys[0], (TOKENS, WIDTH), jnp.float32), -5.0, 5.0)
    row_low = 0.3
    row_high = 3.0
    row_scale = jnp.exp(jax.random.uniform(subkeys[1], (TOKENS, 1), jnp.float32, math.log(row_low), math.log(row_high)))
    column_scale = jnp.exp(jax.random.uniform(subkeys[2], (1, WIDTH), jnp.float32, 0.0, math.log(10.0))) / 4.0
    return (entries * row_scale * column_scale / 64.0).astype(jnp.bfloat16)


def level_of(rng, dims, cuts, low, largest):
    gain, own = 1.0, jax.random.fold_in(rng, 6)
    for dim, blocks in cuts:
        heights = jnp.exp(jax.random.uniform(jax.random.fold_in(own, dim), (blocks,), jnp.float32, low / len(cuts), largest / len(cuts)))
        gain = gain * jnp.repeat(heights, dims[dim] // blocks).reshape([-1 if axis == dim else 1 for axis in range(len(dims))])
    return gain


def bell_draw(rng, extent, width, most, cuts=(), held_as=jnp.bfloat16):
    array = jax.random.normal(rng, extent, jnp.float32) * width
    if len(cuts) > 0:
        array = level_of(rng, extent, cuts, -0.22, 0.18) * array
    return jnp.clip(array, min=-most, max=most).astype(held_as)


def setup_inputs(seed: int = 0) -> dict:
    keys = jax.random.split(jax.random.key(seed), 4)
    return {
        "activations": draw_activations(jax.random.fold_in(keys[3], 71), 0),
        "weight": bell_draw(keys[1], (WIDTH, OUT_COLS), WIDTH ** -0.5, 0.046875, ((0, 32), (1, 8))),
        "grad_out": bell_draw(keys[2], (TOKENS, OUT_COLS), 1.0, 6.0, ((0, 32), (1, 8))),
    }


levels = 127.0
ripple = 0.5
epsilon = 1e-06

def hadamard_table(length, number_type):
    row_ids = lax.broadcasted_iota(jnp.int32, (length, length), 0)
    column_ids = lax.broadcasted_iota(jnp.int32, (length, length), 1)
    common = jnp.bitwise_and(row_ids, column_ids)
    parity = jnp.zeros((length, length), jnp.int32)
    for bit_index in range(length.bit_length() - 1):
        parity = parity + jnp.bitwise_and(jnp.right_shift(common, bit_index), 1)
    parity = parity % 2
    return (1 - 2 * parity).astype(number_type)

def transform(values):
    row_count = values.shape[0]
    blocks = WIDTH // BLOCK
    inner = jnp.dot(values.reshape(row_count * blocks, BLOCK), hadamard_table(BLOCK, jnp.bfloat16), preferred_element_type=jnp.float32)
    inner = inner.reshape(row_count, blocks, BLOCK)
    combined = jnp.einsum('ab,rbf->raf', hadamard_table(blocks, jnp.float32), inner, precision=lax.Precision.HIGHEST)
    return combined.reshape(row_count, WIDTH) * (1.0 / math.sqrt(WIDTH))

def reference(activations, weight, grad_out):
    transformed = transform(activations)
    peak = lax.optimization_barrier(jnp.max(jnp.abs(transformed), axis=1, keepdims=True))
    scale = (peak + epsilon) / levels
    phase = 2.0 * math.pi * (transformed / scale)
    quantized = (transformed - ripple / (2.0 * math.pi) * scale * jnp.sin(phase)).astype(jnp.bfloat16)
    slope = 1.0 - ripple * jnp.cos(phase)
    grad_weight = jnp.dot(quantized.T, grad_out, preferred_element_type=jnp.float32)
    column_share = OUT_COLS // N_TENSOR
    summed = jnp.zeros(transformed.shape, jnp.float32)
    for member in range(N_TENSOR):
        lower_edge = member * column_share
        share_term = jnp.dot(grad_out[:, lower_edge:lower_edge + column_share], weight[:, lower_edge:lower_edge + column_share].T, preferred_element_type=jnp.float32)
        rounded = lax.optimization_barrier(share_term.astype(jnp.bfloat16))
        summed = summed + rounded.astype(jnp.float32)
    upstream = (summed * slope).astype(jnp.bfloat16)
    grad_input = transform(upstream).astype(jnp.bfloat16)
    return (grad_input, grad_weight)
```

```python
import math

import jax
import jax.numpy as jnp
import numpy as np
from jax import lax
from jax.experimental import pallas as pl
from jax.experimental.pallas import tpu as pltpu
from jax.sharding import PartitionSpec as P

BLOCK = 1024
WIDTH = 16384
BLOCKS = WIDTH // BLOCK
LANES = 128
NORM = 1.0 / math.sqrt(WIDTH)

levels = 127.0
ripple = 0.5
epsilon = 1e-06


def hadamard_table(length):
    table = np.ones((1, 1), np.float32)
    while table.shape[0] < length:
        table = np.block([[table, table], [table, -table]])
    return jnp.asarray(table, jnp.bfloat16)


def fit(odd, terms):
    nodes = 0.5 * np.cos(np.pi * (np.arange(400) + 0.5) / 800.0)
    squares = nodes * nodes
    values = np.sin(2.0 * np.pi * nodes) / nodes if odd else np.cos(2.0 * np.pi * nodes)
    scaled = np.polynomial.chebyshev.Chebyshev.fit(squares, values, terms - 1, domain=[0.0, 0.25])
    return [float(c) for c in scaled.convert(kind=np.polynomial.Polynomial).coef]


SINE = fit(True, 8)
COSINE = fit(False, 9)


def horner(coefficients, square):
    total = jnp.full_like(square, coefficients[-1])
    for coefficient in coefficients[-2::-1]:
        total = total * square + coefficient
    return total


def butterfly(parts):
    distance = 1
    while distance < len(parts):
        mixed = list(parts)
        for low in range(len(parts)):
            if not low & distance:
                mixed[low] = parts[low] + parts[low | distance]
                mixed[low | distance] = parts[low] - parts[low | distance]
        parts = mixed
        distance *= 2
    return parts


def quantize_kernel(place, rows_ref, table_ref, quantized_ref, slope_ref, inner, mixed):
    tokens = rows_ref.shape[1]
    per_shard = rows_ref.shape[2] // BLOCK
    stacked = jnp.concatenate(
        [
            rows_ref[b // per_shard, :, (b % per_shard) * BLOCK : (b % per_shard + 1) * BLOCK]
            for b in range(BLOCKS)
        ],
        axis=0,
    )
    inner[...] = jnp.dot(stacked, table_ref[...], preferred_element_type=jnp.float32)
    largest = jnp.zeros((tokens, LANES), jnp.float32)
    for chunk in range(BLOCK // LANES):
        lanes = slice(chunk * LANES, (chunk + 1) * LANES)
        parts = butterfly([inner[b * tokens : (b + 1) * tokens, lanes] for b in range(BLOCKS)])
        for b in range(BLOCKS):
            value = parts[b] * NORM
            mixed[b * tokens : (b + 1) * tokens, lanes] = value
            largest = jnp.maximum(largest, jnp.abs(value))
    peak = jnp.max(largest, axis=1, keepdims=True)
    scale = (peak + epsilon) / levels
    inverse = 1.0 / scale
    depth = (ripple / (2.0 * math.pi)) * scale
    width = quantized_ref.shape[2]
    per_block = BLOCK // width

    def remainder(value):
        turns = value * inverse
        return turns - jnp.round(turns)

    for b in range(BLOCKS):
        value = mixed[b * tokens : (b + 1) * tokens, :]
        rest = remainder(value)
        sine = rest * horner(SINE, rest * rest)
        result = (value - depth * sine).astype(jnp.bfloat16)
        for k in range(per_block):
            quantized_ref[b * per_block + k] = result[:, k * width : (k + 1) * width]

    @pl.when(pl.program_id(0) == place[0])
    def _():
        for b in range(BLOCKS):
            rest = remainder(mixed[b * tokens : (b + 1) * tokens, :])
            slope = 1.0 - ripple * horner(COSINE, rest * rest)
            for k in range(per_block):
                slope_ref[b * per_block + k] = slope[:, k * width : (k + 1) * width]


def quantize(rows, table, place, dp, width):
    shards, tokens, features = rows.shape
    step = tokens // shards
    return pl.pallas_call(
        quantize_kernel,
        grid_spec=pltpu.PrefetchScalarGridSpec(
            num_scalar_prefetch=1,
            grid=(shards,),
            in_specs=[
                pl.BlockSpec((shards, step, features), lambda i, place: (0, i, 0)),
                pl.BlockSpec((BLOCK, BLOCK), lambda i, place: (0, 0)),
            ],
            out_specs=[
                pl.BlockSpec((dp, step, width), lambda i, place: (0, i, 0)),
                pl.BlockSpec((dp, step, width), lambda i, place: (0, 0, 0)),
            ],
            scratch_shapes=[
                pltpu.VMEM((BLOCKS * step, BLOCK), jnp.float32),
                pltpu.VMEM((BLOCKS * step, BLOCK), jnp.float32),
            ],
        ),
        out_shape=[
            jax.ShapeDtypeStruct((dp, tokens, width), jnp.bfloat16),
            jax.ShapeDtypeStruct((dp, step, width), jnp.float32),
        ],
        compiler_params=pltpu.CompilerParams(vmem_limit_bytes=32 * 1024 * 1024),
        cost_estimate=pl.CostEstimate(
            flops=2 * tokens * WIDTH * BLOCK, bytes_accessed=4 * tokens * WIDTH, transcendentals=0
        ),
    )(place, rows, table)


def product_kernel(rows_ref, weight_ref, out_ref):
    devices, tokens, depth = rows_ref.shape
    out_ref[0] = lax.dot_general(
        rows_ref[...].reshape(devices * tokens, depth),
        weight_ref[...],
        (((1,), (1,)), ((), ())),
        preferred_element_type=jnp.float32,
    ).astype(out_ref.dtype)


def product(rows, weight, shards):
    devices, tokens, depth = rows.shape
    step = tokens // shards
    width = weight.shape[0]
    return pl.pallas_call(
        product_kernel,
        grid=(shards,),
        in_specs=[
            pl.BlockSpec((devices, step, depth), lambda i: (0, i, 0)),
            pl.BlockSpec((width, depth), lambda i: (0, 0)),
        ],
        out_specs=pl.BlockSpec((1, devices * step, width), lambda i: (i, 0, 0)),
        out_shape=jax.ShapeDtypeStruct((shards, devices * step, width), jnp.bfloat16),
        compiler_params=pltpu.CompilerParams(vmem_limit_bytes=32 * 1024 * 1024),
        cost_estimate=pl.CostEstimate(
            flops=2 * devices * tokens * depth * width,
            bytes_accessed=2 * devices * tokens * (depth + width),
            transcendentals=0,
        ),
    )(rows, weight)


def finish_kernel(summed_ref, slope_ref, table_ref, out_ref, inner):
    tokens, width = summed_ref.shape[1:]
    per_block = BLOCK // width
    per_shard = out_ref.shape[2] // BLOCK
    upstream = (summed_ref[...].astype(jnp.float32) * slope_ref[...]).astype(jnp.bfloat16)
    stacked = jnp.concatenate(
        [
            jnp.concatenate([upstream[b * per_block + k] for k in range(per_block)], axis=1)
            for b in range(BLOCKS)
        ],
        axis=0,
    )
    inner[...] = jnp.dot(stacked, table_ref[...], preferred_element_type=jnp.float32)
    for chunk in range(BLOCK // LANES):
        lanes = slice(chunk * LANES, (chunk + 1) * LANES)
        parts = butterfly([inner[b * tokens : (b + 1) * tokens, lanes] for b in range(BLOCKS)])
        for b in range(BLOCKS):
            start = (b % per_shard) * BLOCK + chunk * LANES
            out_ref[b // per_shard, :, start : start + LANES] = (parts[b] * NORM).astype(
                out_ref.dtype
            )


def finish(summed, slope, table, shards):
    devices, tokens, width = summed.shape
    return pl.pallas_call(
        finish_kernel,
        out_shape=jax.ShapeDtypeStruct((shards, tokens, WIDTH // shards), jnp.bfloat16),
        scratch_shapes=[pltpu.VMEM((BLOCKS * tokens, BLOCK), jnp.float32)],
        compiler_params=pltpu.CompilerParams(vmem_limit_bytes=32 * 1024 * 1024),
        cost_estimate=pl.CostEstimate(
            flops=2 * tokens * WIDTH * BLOCK, bytes_accessed=8 * tokens * WIDTH, transcendentals=0
        ),
    )(summed, slope, table)


def shards(activations, weight, grad_out):
    dp = lax.axis_size("dp")
    members = lax.axis_size("tensor")
    tokens, features = activations.shape
    width, depth = weight.shape
    place = lax.axis_index("tensor").astype(jnp.int32).reshape(1)
    table = hadamard_table(BLOCK)
    wide_rows = lax.all_gather(activations, "tensor", axis=0, tiled=False)
    all_rows = lax.all_gather(grad_out, "dp", axis=0, tiled=False)
    quantized, slope = quantize(wide_rows, table, place, dp, width)
    q_block = lax.all_to_all(quantized, "dp", split_axis=0, concat_axis=0, tiled=True)
    partial_rows = product(all_rows, weight, members)
    summed = lax.psum_scatter(partial_rows, "tensor", scatter_dimension=0, tiled=False)
    homed = lax.all_to_all(
        summed.reshape(dp, tokens // members, width), "dp", split_axis=0, concat_axis=0, tiled=True
    )
    mixed = finish(homed, slope, table, members)
    grad_input = lax.all_to_all(mixed, "tensor", split_axis=0, concat_axis=0, tiled=True)
    weight_sum = lax.dot_general(
        q_block.reshape(dp * tokens, width),
        all_rows.reshape(dp * tokens, depth),
        (((0,), (0,)), ((), ())),
        preferred_element_type=jnp.float32,
    )
    return (grad_input.reshape(tokens, features), weight_sum)


def solution(mesh):
    return jax.shard_map(
        shards,
        mesh=mesh,
        in_specs=(P("dp", "tensor"), P("dp", "tensor"), P("dp", "tensor")),
        out_specs=(P("dp", "tensor"), P("dp", "tensor")),
        check_vma=False,
    )
```

```python
import math

import jax
import jax.numpy as jnp
import numpy as np
from jax import lax
from jax.experimental import pallas as pl
from jax.experimental.pallas import tpu as pltpu
from jax.sharding import PartitionSpec as P

BLOCK = 1024
WIDTH = 16384
BLOCKS = WIDTH // BLOCK
LANES = 128
NORM = 1.0 / math.sqrt(WIDTH)
SIDE = 4
PIECES = 4
OFFSETS = (0, -1, 1, -2)

levels = 127.0
ripple = 0.5
epsilon = 1e-06


def hadamard_table(length):
    table = np.ones((1, 1), np.float32)
    while table.shape[0] < length:
        table = np.block([[table, table], [table, -table]])
    return jnp.asarray(table, jnp.bfloat16)


def fit(odd, terms):
    nodes = 0.5 * np.cos(np.pi * (np.arange(400) + 0.5) / 800.0)
    squares = nodes * nodes
    values = np.sin(2.0 * np.pi * nodes) / nodes if odd else np.cos(2.0 * np.pi * nodes)
    scaled = np.polynomial.chebyshev.Chebyshev.fit(squares, values, terms - 1, domain=[0.0, 0.25])
    return [float(c) for c in scaled.convert(kind=np.polynomial.Polynomial).coef]


SINE = fit(True, 8)
COSINE = fit(False, 9)


def horner(coefficients, square):
    total = jnp.full_like(square, coefficients[-1])
    for coefficient in coefficients[-2::-1]:
        total = total * square + coefficient
    return total


def butterfly(parts):
    distance = 1
    while distance < len(parts):
        mixed = list(parts)
        for low in range(len(parts)):
            if not low & distance:
                mixed[low] = parts[low] + parts[low | distance]
                mixed[low | distance] = parts[low] - parts[low | distance]
        parts = mixed
        distance *= 2
    return parts


def quantize_kernel(place, rows_ref, table_ref, quantized_ref, slope_ref, inner, mixed):
    tokens = rows_ref.shape[1]
    per_shard = rows_ref.shape[2] // BLOCK
    stacked = jnp.concatenate(
        [
            rows_ref[b // per_shard, :, (b % per_shard) * BLOCK : (b % per_shard + 1) * BLOCK]
            for b in range(BLOCKS)
        ],
        axis=0,
    )
    inner[...] = jnp.dot(stacked, table_ref[...], preferred_element_type=jnp.float32)
    largest = jnp.zeros((tokens, LANES), jnp.float32)
    for chunk in range(BLOCK // LANES):
        lanes = slice(chunk * LANES, (chunk + 1) * LANES)
        parts = butterfly([inner[b * tokens : (b + 1) * tokens, lanes] for b in range(BLOCKS)])
        for b in range(BLOCKS):
            value = parts[b] * NORM
            mixed[b * tokens : (b + 1) * tokens, lanes] = value
            largest = jnp.maximum(largest, jnp.abs(value))
    peak = jnp.max(largest, axis=1, keepdims=True)
    scale = (peak + epsilon) / levels
    inverse = 1.0 / scale
    depth = (ripple / (2.0 * math.pi)) * scale
    width = quantized_ref.shape[2]
    per_block = BLOCK // width

    def remainder(value):
        turns = value * inverse
        return turns - jnp.round(turns)

    for b in range(BLOCKS):
        value = mixed[b * tokens : (b + 1) * tokens, :]
        rest = remainder(value)
        sine = rest * horner(SINE, rest * rest)
        result = (value - depth * sine).astype(jnp.bfloat16)
        for k in range(per_block):
            quantized_ref[b * per_block + k] = result[:, k * width : (k + 1) * width]

    @pl.when(pl.program_id(0) == place[0])
    def _():
        for b in range(BLOCKS):
            rest = remainder(mixed[b * tokens : (b + 1) * tokens, :])
            slope = 1.0 - ripple * horner(COSINE, rest * rest)
            for k in range(per_block):
                slope_ref[b * per_block + k] = slope[:, k * width : (k + 1) * width]


def quantize(rows, table, place, dp, width):
    shards, tokens, features = rows.shape
    step = tokens // shards
    return pl.pallas_call(
        quantize_kernel,
        grid_spec=pltpu.PrefetchScalarGridSpec(
            num_scalar_prefetch=1,
            grid=(shards,),
            in_specs=[
                pl.BlockSpec((shards, step, features), lambda i, place: (0, i, 0)),
                pl.BlockSpec((BLOCK, BLOCK), lambda i, place: (0, 0)),
            ],
            out_specs=[
                pl.BlockSpec((dp, step, width), lambda i, place: (0, i, 0)),
                pl.BlockSpec((dp, step, width), lambda i, place: (0, 0, 0)),
            ],
            scratch_shapes=[
                pltpu.VMEM((BLOCKS * step, BLOCK), jnp.float32),
                pltpu.VMEM((BLOCKS * step, BLOCK), jnp.float32),
            ],
        ),
        out_shape=[
            jax.ShapeDtypeStruct((dp, tokens, width), jnp.bfloat16),
            jax.ShapeDtypeStruct((dp, step, width), jnp.float32),
        ],
        compiler_params=pltpu.CompilerParams(vmem_limit_bytes=32 * 1024 * 1024),
        cost_estimate=pl.CostEstimate(
            flops=2 * tokens * WIDTH * BLOCK, bytes_accessed=4 * tokens * WIDTH, transcendentals=0
        ),
    )(place, rows, table)


def product_kernel(*refs):
    weight_ref, out_ref = refs[-2:]
    pieces = [ref for ref in refs[:-2] if len(ref.shape) == 2]
    members, step = out_ref.shape[0], out_ref.shape[1] // PIECES // 2
    done = 0
    for piece_ref in pieces:
        rows, depth = piece_ref.shape
        result = lax.dot_general(
            piece_ref[...],
            weight_ref[...],
            (((1,), (1,)), ((), ())),
            preferred_element_type=jnp.float32,
        ).astype(out_ref.dtype)
        for k in range(rows // (members * step)):
            for t in range(members):
                start = (k * members + t) * step
                out_ref[t, done * step : (done + 1) * step, :] = result[start : start + step]
            done += 1


def product(held, pieces, weight, position, members):
    rows = sum(piece.shape[0] for piece in pieces)
    width, depth = weight.shape
    whole = [pl.BlockSpec(memory_space=pltpu.VMEM)] * (len(pieces) + 1)
    earlier = [] if held is None else [held]
    return pl.pallas_call(
        product_kernel,
        grid=(1,),
        in_specs=[pl.BlockSpec(memory_space=pl.ANY)] * len(earlier) + whole,
        out_specs=pl.BlockSpec((members, rows // members, width), lambda i: (0, position, 0)),
        out_shape=jax.ShapeDtypeStruct((members, 4 * rows // members, width), jnp.bfloat16),
        input_output_aliases={0: 0} if earlier else {},
        compiler_params=pltpu.CompilerParams(vmem_limit_bytes=32 * 1024 * 1024),
        cost_estimate=pl.CostEstimate(
            flops=2 * rows * depth * width,
            bytes_accessed=2 * rows * (depth + width),
            transcendentals=0,
        ),
    )(*earlier, *pieces, weight)


def order_kernel(sources, rows_ref, out_ref):
    for slot in range(rows_ref.shape[0]):
        out_ref[sources[slot]] = rows_ref[slot]


def order(rows, sources):
    return pl.pallas_call(
        order_kernel,
        in_specs=[
            pl.BlockSpec(memory_space=pltpu.SMEM),
            pl.BlockSpec(memory_space=pltpu.VMEM),
        ],
        out_specs=pl.BlockSpec(memory_space=pltpu.VMEM),
        out_shape=jax.ShapeDtypeStruct(rows.shape, rows.dtype),
    )(sources, rows)


def gradient_kernel(sources, quantized_ref, *refs):
    out_ref = refs[-1]
    pieces = refs[:-1]
    tokens = quantized_ref.shape[1]
    slot = 0
    for number, piece_ref in enumerate(pieces):
        count = piece_ref.shape[0] // tokens
        block = jnp.concatenate(
            [quantized_ref[sources[slot + k]] for k in range(count)], axis=0
        )
        slot += count
        term = lax.dot_general(
            block, piece_ref[...], (((0,), (0,)), ((), ())), preferred_element_type=jnp.float32
        )
        out_ref[...] = term if number == 0 else out_ref[...] + term


def gradient(sources, quantized, pieces):
    width, depth = quantized.shape[2], pieces[0].shape[1]
    rows = sum(piece.shape[0] for piece in pieces)
    return pl.pallas_call(
        gradient_kernel,
        in_specs=[pl.BlockSpec(memory_space=pltpu.SMEM)]
        + [pl.BlockSpec(memory_space=pltpu.VMEM)] * (len(pieces) + 1),
        out_specs=pl.BlockSpec(memory_space=pltpu.VMEM),
        out_shape=jax.ShapeDtypeStruct((width, depth), jnp.float32),
        compiler_params=pltpu.CompilerParams(vmem_limit_bytes=48 * 1024 * 1024),
        cost_estimate=pl.CostEstimate(
            flops=2 * rows * depth * width,
            bytes_accessed=2 * rows * (depth + width) + 4 * width * depth,
            transcendentals=0,
        ),
    )(sources, quantized, *pieces)


def chip_core(x, y, core):
    return (x % SIDE * SIDE + y % SIDE) * 2 + core


def route(turn, sign):
    pairs = []
    for x in range(SIDE):
        for y in range(SIDE):
            for core in range(2):
                along = (sign, 0) if core == turn else (0, sign)
                pairs.append(
                    (chip_core(x, y, core), chip_core(x + along[0], y + along[1], core))
                )
    return pairs


def around(block, turn):
    half = block.shape[0] // 2
    below = lax.ppermute(block, "dp", route(turn, 1))
    above = lax.ppermute(block, "dp", route(turn, -1))
    first = lax.ppermute(below[:half], "dp", route(turn, 1))
    second = lax.ppermute(above[half:], "dp", route(turn, -1))
    return below, above, first, second


def other_core(block):
    return lax.ppermute(block, "dp", [(d, d ^ 1) for d in range(2 * SIDE * SIDE)])


def sources_of(device):
    x, y, core = device // (2 * SIDE), device // 2 % SIDE, device % 2
    found = []
    for outer in OFFSETS:
        for chain in range(2):
            sender = core ^ chain
            for inner in OFFSETS:
                at_x = (x + jnp.where(sender == 0, inner, outer) + SIDE) % SIDE
                at_y = (y + jnp.where(sender == 0, outer, inner) + SIDE) % SIDE
                found.append((at_x * SIDE + at_y) * 2 + sender)
    return jnp.stack(found).astype(jnp.int32)


def finish_kernel(summed_ref, slope_ref, table_ref, out_ref, inner):
    tokens, width = summed_ref.shape[1:]
    per_block = BLOCK // width
    per_shard = out_ref.shape[2] // BLOCK
    upstream = (summed_ref[...].astype(jnp.float32) * slope_ref[...]).astype(jnp.bfloat16)
    stacked = jnp.concatenate(
        [
            jnp.concatenate([upstream[b * per_block + k] for k in range(per_block)], axis=1)
            for b in range(BLOCKS)
        ],
        axis=0,
    )
    inner[...] = jnp.dot(stacked, table_ref[...], preferred_element_type=jnp.float32)
    for chunk in range(BLOCK // LANES):
        lanes = slice(chunk * LANES, (chunk + 1) * LANES)
        parts = butterfly([inner[b * tokens : (b + 1) * tokens, lanes] for b in range(BLOCKS)])
        for b in range(BLOCKS):
            start = (b % per_shard) * BLOCK + chunk * LANES
            out_ref[b // per_shard, :, start : start + LANES] = (parts[b] * NORM).astype(
                out_ref.dtype
            )


def finish(summed, slope, table, shards):
    devices, tokens, width = summed.shape
    return pl.pallas_call(
        finish_kernel,
        out_shape=jax.ShapeDtypeStruct((shards, tokens, WIDTH // shards), jnp.bfloat16),
        scratch_shapes=[pltpu.VMEM((BLOCKS * tokens, BLOCK), jnp.float32)],
        compiler_params=pltpu.CompilerParams(vmem_limit_bytes=32 * 1024 * 1024),
        cost_estimate=pl.CostEstimate(
            flops=2 * tokens * WIDTH * BLOCK, bytes_accessed=8 * tokens * WIDTH, transcendentals=0
        ),
    )(summed, slope, table)


def shards(activations, weight, grad_out):
    dp = lax.axis_size("dp")
    members = lax.axis_size("tensor")
    tokens, features = activations.shape
    width = weight.shape[0]
    place = lax.axis_index("tensor").astype(jnp.int32).reshape(1)
    sources = sources_of(lax.axis_index("dp").astype(jnp.int32))
    table = hadamard_table(BLOCK)
    wide_rows = lax.all_gather(activations, "tensor", axis=0, tiled=False)
    near = jnp.concatenate([grad_out, *around(grad_out, 0)], axis=0)
    below, above, first, second = around(near, 1)
    groups = []
    for block in (near, below, above):
        groups.append([block, other_core(block)])
    groups.append([first, second, other_core(first), other_core(second)])
    partial_rows = None
    for position, group in enumerate(groups):
        partial_rows = product(partial_rows, group, weight, position, members)
    summed = lax.psum_scatter(partial_rows, "tensor", scatter_dimension=0, tiled=False)
    quantized, slope = quantize(wide_rows, table, place, dp, width)
    q_block = lax.all_to_all(quantized, "dp", split_axis=0, concat_axis=0, tiled=True)
    ordered = order(summed.reshape(dp, tokens // members, width), sources)
    homed = lax.all_to_all(ordered, "dp", split_axis=0, concat_axis=0, tiled=True)
    mixed = finish(homed, slope, table, members)
    grad_input = lax.all_to_all(mixed, "tensor", split_axis=0, concat_axis=0, tiled=True)
    weight_sum = gradient(sources, q_block, [block for group in groups for block in group])
    return (grad_input.reshape(tokens, features), weight_sum)


def solution(mesh):
    return jax.shard_map(
        shards,
        mesh=mesh,
        in_specs=(P("dp", "tensor"), P("dp", "tensor"), P("dp", "tensor")),
        out_specs=(P("dp", "tensor"), P("dp", "tensor")),
        check_vma=False,
    )
```

```python
import math

import jax
import jax.numpy as jnp
import numpy as np
from jax import lax
from jax.experimental import pallas as pl
from jax.experimental.pallas import tpu as pltpu
from jax.sharding import PartitionSpec as P

BLOCK = 1024
WIDTH = 16384
BLOCKS = WIDTH // BLOCK
LANES = 128
NORM = 1.0 / math.sqrt(WIDTH)
SIDE = 4
PIECES = 4
OFFSETS = (0, -1, 1, -2)

levels = 127.0
ripple = 0.5
epsilon = 1e-06


def hadamard_table(length):
    table = np.ones((1, 1), np.float32)
    while table.shape[0] < length:
        table = np.block([[table, table], [table, -table]])
    return jnp.asarray(table, jnp.bfloat16)


def fit(odd, terms):
    nodes = 0.5 * np.cos(np.pi * (np.arange(400) + 0.5) / 800.0)
    squares = nodes * nodes
    values = np.sin(2.0 * np.pi * nodes) / nodes if odd else np.cos(2.0 * np.pi * nodes)
    scaled = np.polynomial.chebyshev.Chebyshev.fit(squares, values, terms - 1, domain=[0.0, 0.25])
    return [float(c) for c in scaled.convert(kind=np.polynomial.Polynomial).coef]


SINE = fit(True, 8)
COSINE = fit(False, 9)


def horner(coefficients, square):
    total = jnp.full_like(square, coefficients[-1])
    for coefficient in coefficients[-2::-1]:
        total = total * square + coefficient
    return total


def butterfly(parts):
    distance = 1
    while distance < len(parts):
        mixed = list(parts)
        for low in range(len(parts)):
            if not low & distance:
                mixed[low] = parts[low] + parts[low | distance]
                mixed[low | distance] = parts[low] - parts[low | distance]
        parts = mixed
        distance *= 2
    return parts


def quantize_kernel(place, rows_ref, table_ref, quantized_ref, slope_ref, inner, mixed):
    tokens = rows_ref.shape[1]
    per_shard = rows_ref.shape[2] // BLOCK
    stacked = jnp.concatenate(
        [
            rows_ref[b // per_shard, :, (b % per_shard) * BLOCK : (b % per_shard + 1) * BLOCK]
            for b in range(BLOCKS)
        ],
        axis=0,
    )
    inner[...] = jnp.dot(stacked, table_ref[...], preferred_element_type=jnp.float32)
    largest = jnp.zeros((tokens, LANES), jnp.float32)
    for chunk in range(BLOCK // LANES):
        lanes = slice(chunk * LANES, (chunk + 1) * LANES)
        parts = butterfly([inner[b * tokens : (b + 1) * tokens, lanes] for b in range(BLOCKS)])
        for b in range(BLOCKS):
            value = parts[b] * NORM
            mixed[b * tokens : (b + 1) * tokens, lanes] = value
            largest = jnp.maximum(largest, jnp.abs(value))
    peak = jnp.max(largest, axis=1, keepdims=True)
    scale = (peak + epsilon) / levels
    inverse = 1.0 / scale
    depth = (ripple / (2.0 * math.pi)) * scale
    width = quantized_ref.shape[2]
    per_block = BLOCK // width

    def remainder(value):
        turns = value * inverse
        return turns - jnp.round(turns)

    for b in range(BLOCKS):
        value = mixed[b * tokens : (b + 1) * tokens, :]
        rest = remainder(value)
        sine = rest * horner(SINE, rest * rest)
        result = (value - depth * sine).astype(jnp.bfloat16)
        for k in range(per_block):
            quantized_ref[b * per_block + k] = result[:, k * width : (k + 1) * width]

    @pl.when(pl.program_id(0) == place[0])
    def _():
        for b in range(BLOCKS):
            rest = remainder(mixed[b * tokens : (b + 1) * tokens, :])
            slope = 1.0 - ripple * horner(COSINE, rest * rest)
            for k in range(per_block):
                slope_ref[b * per_block + k] = slope[:, k * width : (k + 1) * width]


def quantize(rows, table, place, dp, width):
    shards, tokens, features = rows.shape
    step = tokens // shards
    return pl.pallas_call(
        quantize_kernel,
        grid_spec=pltpu.PrefetchScalarGridSpec(
            num_scalar_prefetch=1,
            grid=(shards,),
            in_specs=[
                pl.BlockSpec((shards, step, features), lambda i, place: (0, i, 0)),
                pl.BlockSpec((BLOCK, BLOCK), lambda i, place: (0, 0)),
            ],
            out_specs=[
                pl.BlockSpec((dp, step, width), lambda i, place: (0, i, 0)),
                pl.BlockSpec((dp, step, width), lambda i, place: (0, 0, 0)),
            ],
            scratch_shapes=[
                pltpu.VMEM((BLOCKS * step, BLOCK), jnp.float32),
                pltpu.VMEM((BLOCKS * step, BLOCK), jnp.float32),
            ],
        ),
        out_shape=[
            jax.ShapeDtypeStruct((dp, tokens, width), jnp.bfloat16),
            jax.ShapeDtypeStruct((dp, step, width), jnp.float32),
        ],
        compiler_params=pltpu.CompilerParams(vmem_limit_bytes=32 * 1024 * 1024),
        cost_estimate=pl.CostEstimate(
            flops=2 * tokens * WIDTH * BLOCK, bytes_accessed=4 * tokens * WIDTH, transcendentals=0
        ),
    )(place, rows, table)


def product_kernel(*refs):
    weight_ref, out_ref = refs[-2:]
    pieces = [ref for ref in refs[:-2] if len(ref.shape) == 2]
    members, step = out_ref.shape[0], out_ref.shape[1] // PIECES // 2
    done = 0
    for piece_ref in pieces:
        rows, depth = piece_ref.shape
        result = lax.dot_general(
            piece_ref[...],
            weight_ref[...],
            (((1,), (1,)), ((), ())),
            preferred_element_type=jnp.float32,
        ).astype(out_ref.dtype)
        for k in range(rows // (members * step)):
            for t in range(members):
                start = (k * members + t) * step
                out_ref[t, done * step : (done + 1) * step, :] = result[start : start + step]
            done += 1


def product(held, pieces, weight, position, members):
    rows = sum(piece.shape[0] for piece in pieces)
    width, depth = weight.shape
    whole = [pl.BlockSpec(memory_space=pltpu.VMEM)] * (len(pieces) + 1)
    earlier = [] if held is None else [held]
    return pl.pallas_call(
        product_kernel,
        grid=(1,),
        in_specs=[pl.BlockSpec(memory_space=pl.ANY)] * len(earlier) + whole,
        out_specs=pl.BlockSpec((members, rows // members, width), lambda i: (0, position, 0)),
        out_shape=jax.ShapeDtypeStruct((members, 4 * rows // members, width), jnp.bfloat16),
        input_output_aliases={0: 0} if earlier else {},
        compiler_params=pltpu.CompilerParams(vmem_limit_bytes=32 * 1024 * 1024),
        cost_estimate=pl.CostEstimate(
            flops=2 * rows * depth * width,
            bytes_accessed=2 * rows * (depth + width),
            transcendentals=0,
        ),
    )(*earlier, *pieces, weight)


def order_kernel(sources, rows_ref, out_ref):
    for slot in range(rows_ref.shape[0]):
        out_ref[sources[slot]] = rows_ref[slot]


def order(rows, sources):
    return pl.pallas_call(
        order_kernel,
        in_specs=[
            pl.BlockSpec(memory_space=pltpu.SMEM),
            pl.BlockSpec(memory_space=pltpu.VMEM),
        ],
        out_specs=pl.BlockSpec(memory_space=pltpu.VMEM),
        out_shape=jax.ShapeDtypeStruct(rows.shape, rows.dtype),
    )(sources, rows)


def gradient_kernel(sources, quantized_ref, *refs):
    out_ref = refs[-1]
    pieces = refs[:-1]
    tokens = quantized_ref.shape[1]
    slot = 0
    for number, piece_ref in enumerate(pieces):
        count = piece_ref.shape[0] // tokens
        block = jnp.concatenate(
            [quantized_ref[sources[slot + k]] for k in range(count)], axis=0
        )
        slot += count
        term = lax.dot_general(
            block, piece_ref[...], (((0,), (0,)), ((), ())), preferred_element_type=jnp.float32
        )
        out_ref[...] = term if number == 0 else out_ref[...] + term


def gradient(sources, quantized, pieces):
    width, depth = quantized.shape[2], pieces[0].shape[1]
    rows = sum(piece.shape[0] for piece in pieces)
    return pl.pallas_call(
        gradient_kernel,
        in_specs=[pl.BlockSpec(memory_space=pltpu.SMEM)]
        + [pl.BlockSpec(memory_space=pltpu.VMEM)] * (len(pieces) + 1),
        out_specs=pl.BlockSpec(memory_space=pltpu.VMEM),
        out_shape=jax.ShapeDtypeStruct((width, depth), jnp.float32),
        compiler_params=pltpu.CompilerParams(vmem_limit_bytes=48 * 1024 * 1024),
        cost_estimate=pl.CostEstimate(
            flops=2 * rows * depth * width,
            bytes_accessed=2 * rows * (depth + width) + 4 * width * depth,
            transcendentals=0,
        ),
    )(sources, quantized, *pieces)


def chip_core(x, y, core):
    return (x % SIDE * SIDE + y % SIDE) * 2 + core


def route(turn, sign):
    pairs = []
    for x in range(SIDE):
        for y in range(SIDE):
            for core in range(2):
                along = (sign, 0) if core == turn else (0, sign)
                pairs.append(
                    (chip_core(x, y, core), chip_core(x + along[0], y + along[1], core))
                )
    return pairs


def around(block, turn):
    half = block.shape[0] // 2
    below = lax.ppermute(block, "dp", route(turn, 1))
    above = lax.ppermute(block, "dp", route(turn, -1))
    first = lax.ppermute(below[:half], "dp", route(turn, 1))
    second = lax.ppermute(above[half:], "dp", route(turn, -1))
    return below, above, first, second


def other_core(block):
    return lax.ppermute(block, "dp", [(d, d ^ 1) for d in range(2 * SIDE * SIDE)])


def sources_table():
    table = []
    for x in range(SIDE):
        for y in range(SIDE):
            for core in range(2):
                found = []
                for outer in OFFSETS:
                    for sender in (core, 1 - core):
                        for inner in OFFSETS:
                            along = (inner, outer) if sender == 0 else (outer, inner)
                            found.append(chip_core(x + along[0], y + along[1], sender))
                table.append(found)
    return np.asarray(table, np.int32)


def finish_kernel(summed_ref, slope_ref, table_ref, out_ref, inner):
    tokens, width = summed_ref.shape[1:]
    per_block = BLOCK // width
    per_shard = out_ref.shape[2] // BLOCK
    upstream = (summed_ref[...].astype(jnp.float32) * slope_ref[...]).astype(jnp.bfloat16)
    stacked = jnp.concatenate(
        [
            jnp.concatenate([upstream[b * per_block + k] for k in range(per_block)], axis=1)
            for b in range(BLOCKS)
        ],
        axis=0,
    )
    inner[...] = jnp.dot(stacked, table_ref[...], preferred_element_type=jnp.float32)
    for chunk in range(BLOCK // LANES):
        lanes = slice(chunk * LANES, (chunk + 1) * LANES)
        parts = butterfly([inner[b * tokens : (b + 1) * tokens, lanes] for b in range(BLOCKS)])
        for b in range(BLOCKS):
            start = (b % per_shard) * BLOCK + chunk * LANES
            out_ref[b // per_shard, :, start : start + LANES] = (parts[b] * NORM).astype(
                out_ref.dtype
            )


def finish(summed, slope, table, shards):
    devices, tokens, width = summed.shape
    return pl.pallas_call(
        finish_kernel,
        out_shape=jax.ShapeDtypeStruct((shards, tokens, WIDTH // shards), jnp.bfloat16),
        scratch_shapes=[pltpu.VMEM((BLOCKS * tokens, BLOCK), jnp.float32)],
        compiler_params=pltpu.CompilerParams(vmem_limit_bytes=32 * 1024 * 1024),
        cost_estimate=pl.CostEstimate(
            flops=2 * tokens * WIDTH * BLOCK, bytes_accessed=8 * tokens * WIDTH, transcendentals=0
        ),
    )(summed, slope, table)


def shards(activations, weight, grad_out):
    dp = lax.axis_size("dp")
    members = lax.axis_size("tensor")
    tokens, features = activations.shape
    width = weight.shape[0]
    place = lax.axis_index("tensor").astype(jnp.int32).reshape(1)
    sources = jnp.asarray(sources_table())[lax.axis_index("dp")]
    table = hadamard_table(BLOCK)
    wide_rows = lax.all_gather(activations, "tensor", axis=0, tiled=False)
    near = jnp.concatenate([grad_out, *around(grad_out, 0)], axis=0)
    below, above, first, second = around(near, 1)
    groups = []
    for block in (near, below, above):
        groups.append([block, other_core(block)])
    groups.append([first, second, other_core(first), other_core(second)])
    partial_rows = None
    for position, group in enumerate(groups):
        partial_rows = product(partial_rows, group, weight, position, members)
    partial_rows, wide_rows = lax.optimization_barrier((partial_rows, wide_rows))
    summed = lax.psum_scatter(partial_rows, "tensor", scatter_dimension=0, tiled=False)
    quantized, slope = quantize(wide_rows, table, place, dp, width)
    q_block = lax.all_to_all(quantized, "dp", split_axis=0, concat_axis=0, tiled=True)
    ordered = order(summed.reshape(dp, tokens // members, width), sources)
    homed = lax.all_to_all(ordered, "dp", split_axis=0, concat_axis=0, tiled=True)
    mixed = finish(homed, slope, table, members)
    grad_input = lax.all_to_all(mixed, "tensor", split_axis=0, concat_axis=0, tiled=True)
    weight_sum = gradient(sources, q_block, [block for group in groups for block in group])
    return (grad_input.reshape(tokens, features), weight_sum)


def solution(mesh):
    return jax.shard_map(
        shards,
        mesh=mesh,
        in_specs=(P("dp", "tensor"), P("dp", "tensor"), P("dp", "tensor")),
        out_specs=(P("dp", "tensor"), P("dp", "tensor")),
        check_vma=False,
    )
```

```python
import math

import jax
import jax.numpy as jnp
import numpy as np
from jax import lax
from jax.experimental import pallas as pl
from jax.experimental.pallas import tpu as pltpu
from jax.sharding import PartitionSpec as P

BLOCK = 1024
WIDTH = 16384
TABLE = 256
LANES = 128
VMEM_BYTES = 60 * 1024 * 1024
NORM = 1.0 / math.sqrt(WIDTH)
SIDE = 4
PIECES = 4
OFFSETS = (0, -1, 1, -2)

levels = 127.0
ripple = 0.5
epsilon = 1e-06


def hadamard_table(length):
    table = np.ones((1, 1), np.float32)
    while table.shape[0] < length:
        table = np.block([[table, table], [table, -table]])
    return jnp.asarray(table, jnp.bfloat16)


def fit(odd, terms):
    nodes = 0.5 * np.cos(np.pi * (np.arange(400) + 0.5) / 800.0)
    squares = nodes * nodes
    values = np.sin(2.0 * np.pi * nodes) / nodes if odd else np.cos(2.0 * np.pi * nodes)
    scaled = np.polynomial.chebyshev.Chebyshev.fit(squares, values, terms - 1, domain=[0.0, 0.25])
    return [float(c) for c in scaled.convert(kind=np.polynomial.Polynomial).coef]


SINE = fit(True, 6)
COSINE = fit(False, 7)


def horner(coefficients, square):
    total = jnp.full_like(square, coefficients[-1])
    for coefficient in coefficients[-2::-1]:
        total = total * square + coefficient
    return total


def butterfly(parts):
    distance = 1
    while distance < len(parts):
        mixed = list(parts)
        for low in range(len(parts)):
            if not low & distance:
                mixed[low] = parts[low] + parts[low | distance]
                mixed[low | distance] = parts[low] - parts[low | distance]
        parts = mixed
        distance *= 2
    return parts


def quantize_kernel(place, rows_ref, table_ref, quantized_ref, slope_ref, inner, mixed):
    members, count, features = rows_ref.shape
    step, width = slope_ref.shape[1:]
    chunks, per_shard, per_width = features // TABLE, features // width, width // TABLE
    rows = rows_ref[...].reshape(members * count, features)
    for c in range(chunks):
        inner[c] = jnp.dot(
            rows[:, c * TABLE : (c + 1) * TABLE],
            table_ref[...],
            preferred_element_type=jnp.float32,
        )
    halves = [slice(l * LANES, (l + 1) * LANES) for l in range(TABLE // LANES)]
    for group in range(count // step):
        spans = [
            slice(t * count + group * step, t * count + (group + 1) * step)
            for t in range(members)
        ]
        here = slice(group * step, (group + 1) * step)
        for span in spans:
            for lanes in halves:
                parts = butterfly([inner[c, span, lanes] for c in range(chunks)])
                for c in range(chunks):
                    inner[c, span, lanes] = parts[c]
        largest = jnp.zeros((step, LANES), jnp.float32)
        for c in range(chunks):
            for lanes in halves:
                parts = butterfly([inner[c, span, lanes] for span in spans])
                for span, part in zip(spans, parts):
                    mixed[c, span, lanes] = part
                    largest = jnp.maximum(largest, jnp.abs(part))
        peak = jnp.max(largest, axis=1, keepdims=True) * NORM
        scale = (peak + epsilon) / levels
        inverse = jnp.broadcast_to(NORM / scale, (step, LANES))
        depth = jnp.broadcast_to((ripple / (2.0 * math.pi)) * scale, (step, LANES))

        def remainder(value):
            turns = value * inverse
            return turns - jnp.round(turns)

        def places():
            for t, span in enumerate(spans):
                for c in range(chunks):
                    for l, lanes in enumerate(halves):
                        start = (c % per_width) * TABLE + l * LANES
                        yield t * per_shard + c // per_width, start, mixed[c, span, lanes]

        for block, start, value in places():
            rest = remainder(value)
            sine = rest * horner(SINE, rest * rest)
            quantized_ref[block, here, start : start + LANES] = (
                value * NORM - depth * sine
            ).astype(jnp.bfloat16)

        @pl.when(pl.program_id(0) * (count // step) + group == place[0])
        def _():
            for block, start, value in places():
                rest = remainder(value)
                slope_ref[block, :, start : start + LANES] = 1.0 - ripple * horner(
                    COSINE, rest * rest
                )


def quantize(rows, table, place, dp, width):
    members, tokens, features = rows.shape
    step = tokens // members
    count = 2 * step
    return pl.pallas_call(
        quantize_kernel,
        grid_spec=pltpu.PrefetchScalarGridSpec(
            num_scalar_prefetch=1,
            grid=(tokens // count,),
            in_specs=[
                pl.BlockSpec((members, count, features), lambda i, place: (0, i, 0)),
                pl.BlockSpec((TABLE, TABLE), lambda i, place: (0, 0)),
            ],
            out_specs=[
                pl.BlockSpec((dp, count, width), lambda i, place: (0, i, 0)),
                pl.BlockSpec((dp, step, width), lambda i, place: (0, 0, 0)),
            ],
            scratch_shapes=[
                pltpu.VMEM((features // TABLE, members * count, TABLE), jnp.float32),
                pltpu.VMEM((features // TABLE, members * count, TABLE), jnp.float32),
            ],
        ),
        out_shape=[
            jax.ShapeDtypeStruct((dp, tokens, width), jnp.bfloat16),
            jax.ShapeDtypeStruct((dp, step, width), jnp.float32),
        ],
        compiler_params=pltpu.CompilerParams(vmem_limit_bytes=VMEM_BYTES),
        cost_estimate=pl.CostEstimate(
            flops=2 * tokens * WIDTH * BLOCK, bytes_accessed=4 * tokens * WIDTH, transcendentals=0
        ),
    )(place, rows, table)


def product_kernel(*refs):
    weight_ref, out_ref = refs[-2:]
    pieces = [ref for ref in refs[:-2] if len(ref.shape) == 2]
    members, step = out_ref.shape[0], out_ref.shape[1] // PIECES // 2
    done = 0
    for piece_ref in pieces:
        rows, depth = piece_ref.shape
        result = lax.dot_general(
            piece_ref[...],
            weight_ref[...],
            (((1,), (1,)), ((), ())),
            preferred_element_type=jnp.float32,
        ).astype(out_ref.dtype)
        for k in range(rows // (members * step)):
            for t in range(members):
                start = (k * members + t) * step
                out_ref[t, done * step : (done + 1) * step, :] = result[start : start + step]
            done += 1


def product(held, pieces, weight, position, members):
    rows = sum(piece.shape[0] for piece in pieces)
    width, depth = weight.shape
    whole = [pl.BlockSpec(memory_space=pltpu.VMEM)] * (len(pieces) + 1)
    earlier = [] if held is None else [held]
    return pl.pallas_call(
        product_kernel,
        grid=(1,),
        in_specs=[pl.BlockSpec(memory_space=pl.ANY)] * len(earlier) + whole,
        out_specs=pl.BlockSpec((members, rows // members, width), lambda i: (0, position, 0)),
        out_shape=jax.ShapeDtypeStruct((members, 4 * rows // members, width), jnp.bfloat16),
        input_output_aliases={0: 0} if earlier else {},
        compiler_params=pltpu.CompilerParams(vmem_limit_bytes=VMEM_BYTES),
        cost_estimate=pl.CostEstimate(
            flops=2 * rows * depth * width,
            bytes_accessed=2 * rows * (depth + width),
            transcendentals=0,
        ),
    )(*earlier, *pieces, weight)


def order_kernel(sources, rows_ref, out_ref):
    for slot in range(rows_ref.shape[0]):
        out_ref[sources[slot]] = rows_ref[slot]


def order(rows, sources):
    return pl.pallas_call(
        order_kernel,
        in_specs=[
            pl.BlockSpec(memory_space=pltpu.SMEM),
            pl.BlockSpec(memory_space=pltpu.VMEM),
        ],
        out_specs=pl.BlockSpec(memory_space=pltpu.VMEM),
        out_shape=jax.ShapeDtypeStruct(rows.shape, rows.dtype),
        compiler_params=pltpu.CompilerParams(vmem_limit_bytes=VMEM_BYTES),
    )(sources, rows)


def gradient_kernel(sources, quantized_ref, *refs):
    out_ref = refs[-1]
    pieces = refs[:-1]
    tokens = quantized_ref.shape[1]
    slot = 0
    for number, piece_ref in enumerate(pieces):
        count = piece_ref.shape[0] // tokens
        block = jnp.concatenate(
            [quantized_ref[sources[slot + k]] for k in range(count)], axis=0
        )
        slot += count
        term = lax.dot_general(
            block, piece_ref[...], (((0,), (0,)), ((), ())), preferred_element_type=jnp.float32
        )
        out_ref[...] = term if number == 0 else out_ref[...] + term


def gradient(sources, quantized, pieces):
    width, depth = quantized.shape[2], pieces[0].shape[1]
    rows = sum(piece.shape[0] for piece in pieces)
    return pl.pallas_call(
        gradient_kernel,
        in_specs=[pl.BlockSpec(memory_space=pltpu.SMEM)]
        + [pl.BlockSpec(memory_space=pltpu.VMEM)] * (len(pieces) + 1),
        out_specs=pl.BlockSpec(memory_space=pltpu.VMEM),
        out_shape=jax.ShapeDtypeStruct((width, depth), jnp.float32),
        compiler_params=pltpu.CompilerParams(vmem_limit_bytes=VMEM_BYTES),
        cost_estimate=pl.CostEstimate(
            flops=2 * rows * depth * width,
            bytes_accessed=2 * rows * (depth + width) + 4 * width * depth,
            transcendentals=0,
        ),
    )(sources, quantized, *pieces)


def chip_core(x, y, core):
    return (x % SIDE * SIDE + y % SIDE) * 2 + core


def route(turn, sign):
    pairs = []
    for x in range(SIDE):
        for y in range(SIDE):
            for core in range(2):
                along = (sign, 0) if core == turn else (0, sign)
                pairs.append(
                    (chip_core(x, y, core), chip_core(x + along[0], y + along[1], core))
                )
    return pairs


def hops(block, turn):
    below = lax.ppermute(block, "dp", route(turn, 1))
    above = lax.ppermute(block, "dp", route(turn, -1))
    return below, above


def far_hops(below, above, turn):
    half = below.shape[0] // 2
    first = lax.ppermute(below[:half], "dp", route(turn, 1))
    second = lax.ppermute(above[half:], "dp", route(turn, -1))
    return first, second


def other_core(block):
    return lax.ppermute(block, "dp", [(d, d ^ 1) for d in range(2 * SIDE * SIDE)])


def sources_table():
    table = []
    for x in range(SIDE):
        for y in range(SIDE):
            for core in range(2):
                found = []
                for outer in OFFSETS:
                    for sender in (core, 1 - core):
                        for inner in OFFSETS:
                            along = (inner, outer) if sender == 0 else (outer, inner)
                            found.append(chip_core(x + along[0], y + along[1], sender))
                table.append(found)
    return np.asarray(table, np.int32)


def finish_kernel(summed_ref, slope_ref, table_ref, out_ref, inner):
    devices, step, width = summed_ref.shape
    members, per_width = out_ref.shape[0], width // TABLE
    per_shard = devices // members
    upstream = (summed_ref[...].astype(jnp.float32) * slope_ref[...]).astype(jnp.bfloat16)
    upstream = upstream.reshape(devices * step, width)
    for c in range(per_width):
        inner[c] = jnp.dot(
            upstream[:, c * TABLE : (c + 1) * TABLE],
            table_ref[...],
            preferred_element_type=jnp.float32,
        )
    span = lambda d: slice(d * step, (d + 1) * step)
    for l in range(TABLE // LANES):
        lanes = slice(l * LANES, (l + 1) * LANES)
        for t in range(members):
            near = [(c, span(t * per_shard + k)) for k in range(per_shard) for c in range(per_width)]
            parts = butterfly([inner[c, rows, lanes] for c, rows in near])
            for (c, rows), part in zip(near, parts):
                inner[c, rows, lanes] = part
        for k in range(per_shard):
            for c in range(per_width):
                far = [span(t * per_shard + k) for t in range(members)]
                parts = butterfly([inner[c, rows, lanes] for rows in far])
                start = (k * per_width + c) * TABLE + l * LANES
                for t in range(members):
                    out_ref[t, :, start : start + LANES] = (parts[t] * NORM).astype(out_ref.dtype)


def finish(summed, slope, table, members):
    devices, step, width = summed.shape
    return pl.pallas_call(
        finish_kernel,
        out_shape=jax.ShapeDtypeStruct((members, step, WIDTH // members), jnp.bfloat16),
        scratch_shapes=[pltpu.VMEM((width // TABLE, devices * step, TABLE), jnp.float32)],
        compiler_params=pltpu.CompilerParams(vmem_limit_bytes=VMEM_BYTES),
        cost_estimate=pl.CostEstimate(
            flops=2 * step * WIDTH * BLOCK, bytes_accessed=8 * step * WIDTH, transcendentals=0
        ),
    )(summed, slope, table)


def shards(activations, weight, grad_out):
    dp = lax.axis_size("dp")
    members = lax.axis_size("tensor")
    tokens, features = activations.shape
    width = weight.shape[0]
    place = lax.axis_index("tensor").astype(jnp.int32).reshape(1)
    sources = jnp.asarray(sources_table())[lax.axis_index("dp")]
    table = hadamard_table(TABLE)
    wide_rows = lax.all_gather(activations, "tensor", axis=0, tiled=False)
    below, above = hops(grad_out, 0)
    near = jnp.concatenate([grad_out, below, above, *far_hops(below, above, 0)], axis=0)
    below, above = hops(near, 1)
    near_pair = [near, other_core(near)]
    partial_rows = product(None, near_pair, weight, 0, members)
    below, above, partial_rows = lax.optimization_barrier((below, above, partial_rows))
    first, second = far_hops(below, above, 1)
    below_pair = [below, other_core(below)]
    above_pair = [above, other_core(above)]
    partial_rows = product(partial_rows, below_pair, weight, 1, members)
    partial_rows = product(partial_rows, above_pair, weight, 2, members)
    first, second, partial_rows = lax.optimization_barrier((first, second, partial_rows))
    far_pair = [first, second, other_core(first), other_core(second)]
    partial_rows = product(partial_rows, far_pair, weight, 3, members)
    partial_rows, wide_rows = lax.optimization_barrier((partial_rows, wide_rows))
    summed = lax.psum_scatter(partial_rows, "tensor", scatter_dimension=0, tiled=False)
    quantized, slope = quantize(wide_rows, table, place, dp, width)
    q_block = lax.all_to_all(quantized, "dp", split_axis=0, concat_axis=0, tiled=True)
    summed, q_block = lax.optimization_barrier((summed, q_block))
    ordered = order(summed.reshape(dp, tokens // members, width), sources)
    homed = lax.all_to_all(ordered, "dp", split_axis=0, concat_axis=0, tiled=True)
    mixed = finish(homed, slope, table, members)
    grad_input = lax.all_to_all(mixed, "tensor", split_axis=0, concat_axis=0, tiled=True)
    weight_sum = gradient(sources, q_block, near_pair + below_pair + above_pair + far_pair)
    return (grad_input.reshape(tokens, features), weight_sum)


def solution(mesh):
    return jax.shard_map(
        shards,
        mesh=mesh,
        in_specs=(P("dp", "tensor"), P("dp", "tensor"), P("dp", "tensor")),
        out_specs=(P("dp", "tensor"), P("dp", "tensor")),
        check_vma=False,
    )
```

```python
import math

import jax
import jax.numpy as jnp
import numpy as np
from jax import lax
from jax.experimental import pallas as pl
from jax.experimental.pallas import tpu as pltpu
from jax.sharding import PartitionSpec as P

BLOCK = 1024
WIDTH = 16384
TABLE = 256
LANES = 128
VMEM_BYTES = 60 * 1024 * 1024
NORM = 1.0 / math.sqrt(WIDTH)
SIDE = 4
PIECES = 4
OFFSETS = (0, -1, 1, -2)
RING = (0, 1, 2, -1)

levels = 127.0
ripple = 0.5
epsilon = 1e-06


def hadamard_table(length):
    table = np.ones((1, 1), np.float32)
    while table.shape[0] < length:
        table = np.block([[table, table], [table, -table]])
    return jnp.asarray(table, jnp.bfloat16)


def fit(odd, terms):
    nodes = 0.5 * np.cos(np.pi * (np.arange(400) + 0.5) / 800.0)
    squares = nodes * nodes
    values = np.sin(2.0 * np.pi * nodes) / nodes if odd else np.cos(2.0 * np.pi * nodes)
    scaled = np.polynomial.chebyshev.Chebyshev.fit(squares, values, terms - 1, domain=[0.0, 0.25])
    return [float(c) for c in scaled.convert(kind=np.polynomial.Polynomial).coef]


SINE = fit(True, 6)
COSINE = fit(False, 7)


def horner(coefficients, square):
    total = jnp.full_like(square, coefficients[-1])
    for coefficient in coefficients[-2::-1]:
        total = total * square + coefficient
    return total


def butterfly(parts):
    distance = 1
    while distance < len(parts):
        mixed = list(parts)
        for low in range(len(parts)):
            if not low & distance:
                mixed[low] = parts[low] + parts[low | distance]
                mixed[low | distance] = parts[low] - parts[low | distance]
        parts = mixed
        distance *= 2
    return parts


def quantize_kernel(
    place, targets, rows_ref, table_ref, stay_ref, up_ref, down_ref, slope_ref, inner, mixed
):
    members, count, features = rows_ref.shape
    step, width = slope_ref.shape[1:]
    chunks, per_shard, per_width = features // TABLE, features // width, width // TABLE
    rows = rows_ref[...].reshape(members * count, features)
    for c in range(chunks):
        inner[c] = jnp.dot(
            rows[:, c * TABLE : (c + 1) * TABLE],
            table_ref[...],
            preferred_element_type=jnp.float32,
        )
    halves = [slice(l * LANES, (l + 1) * LANES) for l in range(TABLE // LANES)]
    for group in range(count // step):
        spans = [
            slice(t * count + group * step, t * count + (group + 1) * step)
            for t in range(members)
        ]
        here = slice(group * step, (group + 1) * step)
        for span in spans:
            for lanes in halves:
                parts = butterfly([inner[c, span, lanes] for c in range(chunks)])
                for c in range(chunks):
                    inner[c, span, lanes] = parts[c]
        largest = jnp.zeros((step, LANES), jnp.float32)
        for c in range(chunks):
            for lanes in halves:
                parts = butterfly([inner[c, span, lanes] for span in spans])
                for t, part in enumerate(parts):
                    mixed[c, t, here, lanes] = part
                    largest = jnp.maximum(largest, jnp.abs(part))
        peak = jnp.max(largest, axis=1, keepdims=True) * NORM
        scale = (peak + epsilon) / levels
        inverse = jnp.broadcast_to(NORM / scale, (step, LANES))
        depth = jnp.broadcast_to((ripple / (2.0 * math.pi)) * scale, (step, LANES))

        def remainder(value):
            turns = value * inverse
            return turns - jnp.round(turns)

        sent = [
            (ref, slot) for ref in (stay_ref, up_ref, down_ref) for slot in range(ref.shape[0])
        ]
        for number, (ref, slot) in enumerate(sent):
            block = targets[number]
            t, c = block // per_shard, block % per_shard * per_width
            for k in range(per_width):
                for l, lanes in enumerate(halves):
                    value = mixed[c + k, t, here, lanes]
                    rest = remainder(value)
                    sine = rest * horner(SINE, rest * rest)
                    start = k * TABLE + l * LANES
                    ref[slot, here, start : start + LANES] = (
                        value * NORM - depth * sine
                    ).astype(jnp.bfloat16)

        @pl.when(pl.program_id(0) * (count // step) + group == place[0])
        def _():
            for t in range(members):
                for c in range(chunks):
                    for l, lanes in enumerate(halves):
                        rest = remainder(mixed[c, t, here, lanes])
                        start = (c % per_width) * TABLE + l * LANES
                        slope_ref[t * per_shard + c // per_width, :, start : start + LANES] = (
                            1.0 - ripple * horner(COSINE, rest * rest)
                        )


def quantize(rows, table, place, targets, dp, width):
    members, tokens, features = rows.shape
    step = tokens // members
    count = 2 * step
    sizes = (dp // SIDE, dp * 3 // (2 * SIDE), dp * 3 // (2 * SIDE))
    return pl.pallas_call(
        quantize_kernel,
        grid_spec=pltpu.PrefetchScalarGridSpec(
            num_scalar_prefetch=2,
            grid=(tokens // count,),
            in_specs=[
                pl.BlockSpec((members, count, features), lambda i, *_: (0, i, 0)),
                pl.BlockSpec((TABLE, TABLE), lambda i, *_: (0, 0)),
            ],
            out_specs=[pl.BlockSpec((n, count, width), lambda i, *_: (0, i, 0)) for n in sizes]
            + [pl.BlockSpec((dp, step, width), lambda i, *_: (0, 0, 0))],
            scratch_shapes=[
                pltpu.VMEM((features // TABLE, members * count, TABLE), jnp.float32),
                pltpu.VMEM((features // TABLE, members, count, TABLE), jnp.float32),
            ],
        ),
        out_shape=[jax.ShapeDtypeStruct((n, tokens, width), jnp.bfloat16) for n in sizes]
        + [jax.ShapeDtypeStruct((dp, step, width), jnp.float32)],
        compiler_params=pltpu.CompilerParams(vmem_limit_bytes=VMEM_BYTES),
        cost_estimate=pl.CostEstimate(
            flops=2 * tokens * WIDTH * BLOCK, bytes_accessed=4 * tokens * WIDTH, transcendentals=0
        ),
    )(place, targets, rows, table)


def product_kernel(*refs):
    weight_ref, out_ref = refs[-2:]
    pieces = [ref for ref in refs[:-2] if len(ref.shape) == 2]
    members, step = out_ref.shape[0], out_ref.shape[1] // PIECES // 2
    done = 0
    for piece_ref in pieces:
        rows, depth = piece_ref.shape
        result = lax.dot_general(
            piece_ref[...],
            weight_ref[...],
            (((1,), (1,)), ((), ())),
            preferred_element_type=jnp.float32,
        ).astype(out_ref.dtype)
        for k in range(rows // (members * step)):
            for t in range(members):
                start = (k * members + t) * step
                out_ref[t, done * step : (done + 1) * step, :] = result[start : start + step]
            done += 1


def product(held, pieces, weight, position, members):
    rows = sum(piece.shape[0] for piece in pieces)
    width, depth = weight.shape
    whole = [pl.BlockSpec(memory_space=pltpu.VMEM)] * (len(pieces) + 1)
    earlier = [] if held is None else [held]
    return pl.pallas_call(
        product_kernel,
        grid=(1,),
        in_specs=[pl.BlockSpec(memory_space=pl.ANY)] * len(earlier) + whole,
        out_specs=pl.BlockSpec((members, rows // members, width), lambda i: (0, position, 0)),
        out_shape=jax.ShapeDtypeStruct((members, 4 * rows // members, width), jnp.bfloat16),
        input_output_aliases={0: 0} if earlier else {},
        compiler_params=pltpu.CompilerParams(vmem_limit_bytes=VMEM_BYTES),
        cost_estimate=pl.CostEstimate(
            flops=2 * rows * depth * width,
            bytes_accessed=2 * rows * (depth + width),
            transcendentals=0,
        ),
    )(*earlier, *pieces, weight)


def order_kernel(sources, rows_ref, out_ref):
    for slot in range(rows_ref.shape[0]):
        out_ref[sources[slot]] = rows_ref[slot]


def order(rows, sources):
    return pl.pallas_call(
        order_kernel,
        in_specs=[
            pl.BlockSpec(memory_space=pltpu.SMEM),
            pl.BlockSpec(memory_space=pltpu.VMEM),
        ],
        out_specs=pl.BlockSpec(memory_space=pltpu.VMEM),
        out_shape=jax.ShapeDtypeStruct(rows.shape, rows.dtype),
        compiler_params=pltpu.CompilerParams(vmem_limit_bytes=VMEM_BYTES),
    )(sources, rows)


def gradient_kernel(*refs):
    out_ref = refs[-1]
    quantized_ref = refs[-2]
    pieces = [ref for ref in refs[:-2] if ref.dtype == quantized_ref.dtype]
    held = [ref for ref in refs[:-2] if ref.dtype != quantized_ref.dtype]
    tokens = quantized_ref.shape[1]
    total = held[0][...] if held else None
    slot = 0
    for piece_ref in pieces:
        count = piece_ref.shape[0] // tokens
        block = quantized_ref[slot : slot + count].reshape(count * tokens, quantized_ref.shape[2])
        slot += count
        term = lax.dot_general(
            block, piece_ref[...], (((0,), (0,)), ((), ())), preferred_element_type=jnp.float32
        )
        total = term if total is None else total + term
    out_ref[...] = total


def gradient(held, quantized, pieces):
    width, depth = quantized.shape[2], pieces[0].shape[1]
    rows = sum(piece.shape[0] for piece in pieces)
    earlier = [] if held is None else [held]
    return pl.pallas_call(
        gradient_kernel,
        in_specs=[pl.BlockSpec(memory_space=pltpu.VMEM)] * (len(earlier) + len(pieces) + 1),
        out_specs=pl.BlockSpec(memory_space=pltpu.VMEM),
        out_shape=jax.ShapeDtypeStruct((width, depth), jnp.float32),
        compiler_params=pltpu.CompilerParams(vmem_limit_bytes=VMEM_BYTES),
        cost_estimate=pl.CostEstimate(
            flops=2 * rows * depth * width,
            bytes_accessed=2 * rows * (depth + width) + 4 * width * depth,
            transcendentals=0,
        ),
    )(*earlier, *pieces, quantized)


def chip_core(x, y, core):
    return (x % SIDE * SIDE + y % SIDE) * 2 + core


def route(turn, sign):
    pairs = []
    for x in range(SIDE):
        for y in range(SIDE):
            for core in range(2):
                along = (sign, 0) if core == turn else (0, sign)
                pairs.append(
                    (chip_core(x, y, core), chip_core(x + along[0], y + along[1], core))
                )
    return pairs


def hops(block, turn):
    below = lax.ppermute(block, "dp", route(turn, 1))
    above = lax.ppermute(block, "dp", route(turn, -1))
    return below, above


def far_hops(below, above, turn):
    half = below.shape[0] // 2
    first = lax.ppermute(below[:half], "dp", route(turn, 1))
    second = lax.ppermute(above[half:], "dp", route(turn, -1))
    return first, second


def other_core(block):
    return lax.ppermute(block, "dp", [(d, d ^ 1) for d in range(2 * SIDE * SIDE)])


def sources_table():
    table = []
    for x in range(SIDE):
        for y in range(SIDE):
            for core in range(2):
                found = []
                for outer in OFFSETS:
                    for sender in (core, 1 - core):
                        for inner in OFFSETS:
                            along = (inner, outer) if sender == 0 else (outer, inner)
                            found.append(chip_core(x + along[0], y + along[1], sender))
                table.append(found)
    return np.asarray(table, np.int32)


def targets_table():
    table = []
    for x in range(SIDE):
        for y in range(SIDE):
            for core in range(2):
                def block(first, second, swap):
                    along = (first, second) if core == 0 else (second, first)
                    return chip_core(x + along[0], y + along[1], core ^ swap)

                pairs = [(0, s) for s in RING] + [(1, s) for s in RING]
                pairs += [(2, s) for s in RING] + [(-1, s) for s in RING]
                table.append([block(p, s, swap) for p, s in pairs for swap in range(2)])
    return np.asarray(table, np.int32)


def spread_once(up, down, turn):
    below = lax.ppermute(up, "dp", route(turn, 1))
    above = lax.ppermute(down, "dp", route(turn, -1))
    return below, above


def spread_far(below, above, turn):
    half = below.shape[0] // 3
    first = lax.ppermute(below[2 * half :], "dp", route(turn, 1))
    second = lax.ppermute(above[:half], "dp", route(turn, -1))
    return first, second


def finish_kernel(summed_ref, slope_ref, table_ref, out_ref, inner):
    devices, step, width = summed_ref.shape
    members, per_width = out_ref.shape[0], width // TABLE
    per_shard = devices // members
    upstream = (summed_ref[...].astype(jnp.float32) * slope_ref[...]).astype(jnp.bfloat16)
    upstream = upstream.reshape(devices * step, width)
    for c in range(per_width):
        inner[c] = jnp.dot(
            upstream[:, c * TABLE : (c + 1) * TABLE],
            table_ref[...],
            preferred_element_type=jnp.float32,
        )
    span = lambda d: slice(d * step, (d + 1) * step)
    for l in range(TABLE // LANES):
        lanes = slice(l * LANES, (l + 1) * LANES)
        for t in range(members):
            near = [(c, span(t * per_shard + k)) for k in range(per_shard) for c in range(per_width)]
            parts = butterfly([inner[c, rows, lanes] for c, rows in near])
            for (c, rows), part in zip(near, parts):
                inner[c, rows, lanes] = part
        for k in range(per_shard):
            for c in range(per_width):
                far = [span(t * per_shard + k) for t in range(members)]
                parts = butterfly([inner[c, rows, lanes] for rows in far])
                start = (k * per_width + c) * TABLE + l * LANES
                for t in range(members):
                    out_ref[t, :, start : start + LANES] = (parts[t] * NORM).astype(out_ref.dtype)


def finish(summed, slope, table, members):
    devices, step, width = summed.shape
    return pl.pallas_call(
        finish_kernel,
        out_shape=jax.ShapeDtypeStruct((members, step, WIDTH // members), jnp.bfloat16),
        scratch_shapes=[pltpu.VMEM((width // TABLE, devices * step, TABLE), jnp.float32)],
        compiler_params=pltpu.CompilerParams(vmem_limit_bytes=VMEM_BYTES),
        cost_estimate=pl.CostEstimate(
            flops=2 * step * WIDTH * BLOCK, bytes_accessed=8 * step * WIDTH, transcendentals=0
        ),
    )(summed, slope, table)


def shards(activations, weight, grad_out):
    dp = lax.axis_size("dp")
    members = lax.axis_size("tensor")
    tokens, features = activations.shape
    width = weight.shape[0]
    place = lax.axis_index("tensor").astype(jnp.int32).reshape(1)
    sources = jnp.asarray(sources_table())[lax.axis_index("dp")]
    targets = jnp.asarray(targets_table())[lax.axis_index("dp")]
    table = hadamard_table(TABLE)
    wide_rows = lax.all_gather(activations, "tensor", axis=0, tiled=False)
    below, above = hops(grad_out, 0)
    near = jnp.concatenate([grad_out, below, above, *far_hops(below, above, 0)], axis=0)
    below, above = hops(near, 1)
    near_pair = [near, other_core(near)]
    partial_rows = product(None, near_pair, weight, 0, members)
    below, above, partial_rows = lax.optimization_barrier((below, above, partial_rows))
    first, second = far_hops(below, above, 1)
    below_pair = [below, other_core(below)]
    above_pair = [above, other_core(above)]
    partial_rows = product(partial_rows, below_pair, weight, 1, members)
    partial_rows = product(partial_rows, above_pair, weight, 2, members)
    first, second, partial_rows = lax.optimization_barrier((first, second, partial_rows))
    far_pair = [first, second, other_core(first), other_core(second)]
    partial_rows = product(partial_rows, far_pair, weight, 3, members)
    partial_rows, wide_rows = lax.optimization_barrier((partial_rows, wide_rows))
    summed = lax.psum_scatter(partial_rows, "tensor", scatter_dimension=0, tiled=False)
    stay, up, down, slope = quantize(wide_rows, table, place, targets, dp, width)
    below, above = spread_once(up, down, 0)
    first, second = spread_far(below, above, 0)
    lines = [stay, below[:8], above[4:], jnp.concatenate([first, second], axis=0)]
    up = jnp.concatenate([line[2:4] for line in lines] + [lines[0][4:6], lines[1][4:6]], axis=0)
    down = jnp.concatenate([lines[2][4:6], lines[3][4:6]] + [line[6:] for line in lines], axis=0)
    below, above = spread_once(up, down, 1)
    ordered = order(summed.reshape(dp, tokens // members, width), sources)
    homed = lax.all_to_all(ordered, "dp", split_axis=0, concat_axis=0, tiled=True)
    below, above, homed = lax.optimization_barrier((below, above, homed))
    first, second = spread_far(below, above, 1)
    mixed = finish(homed, slope, table, members)
    grad_input = lax.all_to_all(mixed, "tensor", split_axis=0, concat_axis=0, tiled=True)
    arrived = jnp.concatenate(
        [line[:2] for line in lines] + [below[:8], above[4:], first, second], axis=0
    ).reshape(dp // 2, 2, tokens, width)
    crossed = other_core(arrived[:, 1])
    own = [near_pair[0], below_pair[0], above_pair[0], *far_pair[:2]]
    other = [near_pair[1], below_pair[1], above_pair[1], *far_pair[2:]]
    weight_sum = gradient(None, arrived[:, 0], own)
    weight_sum = gradient(weight_sum, crossed, other)
    return (grad_input.reshape(tokens, features), weight_sum)


def solution(mesh):
    return jax.shard_map(
        shards,
        mesh=mesh,
        in_specs=(P("dp", "tensor"), P("dp", "tensor"), P("dp", "tensor")),
        out_specs=(P("dp", "tensor"), P("dp", "tensor")),
        check_vma=False,
    )
```

```python
import math

import jax
import jax.numpy as jnp
import numpy as np
from jax import lax
from jax.experimental import pallas as pl
from jax.experimental.pallas import tpu as pltpu
from jax.sharding import PartitionSpec as P

BLOCK = 1024
WIDTH = 16384
TABLE = 256
LANES = 128
VMEM_BYTES = 60 * 1024 * 1024
NORM = 1.0 / math.sqrt(WIDTH)
SIDE = 4
PIECES = 4
OFFSETS = (0, -1, 1, -2)

levels = 127.0
ripple = 0.5
epsilon = 1e-06


def hadamard_table(length):
    table = np.ones((1, 1), np.float32)
    while table.shape[0] < length:
        table = np.block([[table, table], [table, -table]])
    return jnp.asarray(table, jnp.bfloat16)


def fit(odd, terms):
    nodes = 0.5 * np.cos(np.pi * (np.arange(400) + 0.5) / 800.0)
    squares = nodes * nodes
    values = np.sin(2.0 * np.pi * nodes) / nodes if odd else np.cos(2.0 * np.pi * nodes)
    scaled = np.polynomial.chebyshev.Chebyshev.fit(squares, values, terms - 1, domain=[0.0, 0.25])
    return [float(c) for c in scaled.convert(kind=np.polynomial.Polynomial).coef]


SINE = fit(True, 6)
COSINE = fit(False, 7)


def horner(coefficients, square):
    total = jnp.full_like(square, coefficients[-1])
    for coefficient in coefficients[-2::-1]:
        total = total * square + coefficient
    return total


def butterfly(parts):
    distance = 1
    while distance < len(parts):
        mixed = list(parts)
        for low in range(len(parts)):
            if not low & distance:
                mixed[low] = parts[low] + parts[low | distance]
                mixed[low | distance] = parts[low] - parts[low | distance]
        parts = mixed
        distance *= 2
    return parts


def quantize_kernel(place, rows_ref, table_ref, quantized_ref, slope_ref, inner, mixed):
    members, count, features = rows_ref.shape
    step, width = slope_ref.shape[1:]
    chunks, per_shard, per_width = features // TABLE, features // width, width // TABLE
    rows = rows_ref[...].reshape(members * count, features)
    for c in range(chunks):
        inner[c] = jnp.dot(
            rows[:, c * TABLE : (c + 1) * TABLE],
            table_ref[...],
            preferred_element_type=jnp.float32,
        )
    halves = [slice(l * LANES, (l + 1) * LANES) for l in range(TABLE // LANES)]
    for group in range(count // step):
        spans = [
            slice(t * count + group * step, t * count + (group + 1) * step)
            for t in range(members)
        ]
        here = slice(group * step, (group + 1) * step)
        for span in spans:
            for lanes in halves:
                parts = butterfly([inner[c, span, lanes] for c in range(chunks)])
                for c in range(chunks):
                    inner[c, span, lanes] = parts[c]
        largest = jnp.zeros((step, LANES), jnp.float32)
        for c in range(chunks):
            for lanes in halves:
                parts = butterfly([inner[c, span, lanes] for span in spans])
                for span, part in zip(spans, parts):
                    mixed[c, span, lanes] = part
                    largest = jnp.maximum(largest, jnp.abs(part))
        peak = jnp.max(largest, axis=1, keepdims=True) * NORM
        scale = (peak + epsilon) / levels
        inverse = jnp.broadcast_to(NORM / scale, (step, LANES))
        depth = jnp.broadcast_to((ripple / (2.0 * math.pi)) * scale, (step, LANES))

        def remainder(value):
            turns = value * inverse
            return turns - jnp.round(turns)

        def places():
            for t, span in enumerate(spans):
                for c in range(chunks):
                    for l, lanes in enumerate(halves):
                        start = (c % per_width) * TABLE + l * LANES
                        yield t * per_shard + c // per_width, start, mixed[c, span, lanes]

        for block, start, value in places():
            rest = remainder(value)
            sine = rest * horner(SINE, rest * rest)
            quantized_ref[block, here, start : start + LANES] = (
                value * NORM - depth * sine
            ).astype(jnp.bfloat16)

        @pl.when(pl.program_id(0) * (count // step) + group == place[0])
        def _():
            for block, start, value in places():
                rest = remainder(value)
                slope_ref[block, :, start : start + LANES] = 1.0 - ripple * horner(
                    COSINE, rest * rest
                )


def quantize(rows, table, place, dp, step, width):
    members, tokens, features = rows.shape
    count = 2 * step
    return pl.pallas_call(
        quantize_kernel,
        grid_spec=pltpu.PrefetchScalarGridSpec(
            num_scalar_prefetch=1,
            grid=(tokens // count,),
            in_specs=[
                pl.BlockSpec((members, count, features), lambda i, place: (0, i, 0)),
                pl.BlockSpec((TABLE, TABLE), lambda i, place: (0, 0)),
            ],
            out_specs=[
                pl.BlockSpec((dp, count, width), lambda i, place: (0, i, 0)),
                pl.BlockSpec((dp, step, width), lambda i, place: (0, 0, 0)),
            ],
            scratch_shapes=[
                pltpu.VMEM((features // TABLE, members * count, TABLE), jnp.float32),
                pltpu.VMEM((features // TABLE, members * count, TABLE), jnp.float32),
            ],
        ),
        out_shape=[
            jax.ShapeDtypeStruct((dp, tokens, width), jnp.bfloat16),
            jax.ShapeDtypeStruct((dp, step, width), jnp.float32),
        ],
        compiler_params=pltpu.CompilerParams(vmem_limit_bytes=VMEM_BYTES),
        cost_estimate=pl.CostEstimate(
            flops=2 * tokens * WIDTH * BLOCK, bytes_accessed=4 * tokens * WIDTH, transcendentals=0
        ),
    )(place, rows, table)


def product_kernel(*refs):
    weight_ref, out_ref = refs[-2:]
    pieces = [ref for ref in refs[:-2] if len(ref.shape) == 2]
    members, step = out_ref.shape[0], out_ref.shape[1] // PIECES // 2
    done = 0
    for piece_ref in pieces:
        rows, depth = piece_ref.shape
        result = lax.dot_general(
            piece_ref[...],
            weight_ref[...],
            (((1,), (1,)), ((), ())),
            preferred_element_type=jnp.float32,
        ).astype(out_ref.dtype)
        for k in range(rows // (members * step)):
            for t in range(members):
                start = (k * members + t) * step
                out_ref[t, done * step : (done + 1) * step, :] = result[start : start + step]
            done += 1


def product(held, pieces, weight, position, members):
    rows = sum(piece.shape[0] for piece in pieces)
    width, depth = weight.shape
    whole = [pl.BlockSpec(memory_space=pltpu.VMEM)] * (len(pieces) + 1)
    earlier = [] if held is None else [held]
    return pl.pallas_call(
        product_kernel,
        grid=(1,),
        in_specs=[pl.BlockSpec(memory_space=pl.ANY)] * len(earlier) + whole,
        out_specs=pl.BlockSpec((members, rows // members, width), lambda i: (0, position, 0)),
        out_shape=jax.ShapeDtypeStruct((members, 4 * rows // members, width), jnp.bfloat16),
        input_output_aliases={0: 0} if earlier else {},
        compiler_params=pltpu.CompilerParams(vmem_limit_bytes=VMEM_BYTES),
        cost_estimate=pl.CostEstimate(
            flops=2 * rows * depth * width,
            bytes_accessed=2 * rows * (depth + width),
            transcendentals=0,
        ),
    )(*earlier, *pieces, weight)


def order_kernel(sources, rows_ref, out_ref):
    for slot in range(rows_ref.shape[0]):
        out_ref[sources[slot]] = rows_ref[slot]


def order(rows, sources):
    return pl.pallas_call(
        order_kernel,
        in_specs=[
            pl.BlockSpec(memory_space=pltpu.SMEM),
            pl.BlockSpec(memory_space=pltpu.VMEM),
        ],
        out_specs=pl.BlockSpec(memory_space=pltpu.VMEM),
        out_shape=jax.ShapeDtypeStruct(rows.shape, rows.dtype),
        compiler_params=pltpu.CompilerParams(vmem_limit_bytes=VMEM_BYTES),
    )(sources, rows)


def gradient_kernel(sources, early_ref, late_ref, *refs):
    out_ref = refs[-1]
    pieces = refs[:-1]
    tokens = early_ref.shape[1] + late_ref.shape[1]
    slot = 0
    for number, piece_ref in enumerate(pieces):
        count = piece_ref.shape[0] // tokens
        block = jnp.concatenate(
            [
                ref[sources[slot + k]] for k in range(count) for ref in (early_ref, late_ref)
            ],
            axis=0,
        )
        slot += count
        term = lax.dot_general(
            block, piece_ref[...], (((0,), (0,)), ((), ())), preferred_element_type=jnp.float32
        )
        out_ref[...] = term if number == 0 else out_ref[...] + term


def gradient(sources, early, late, pieces):
    width, depth = early.shape[2], pieces[0].shape[1]
    rows = sum(piece.shape[0] for piece in pieces)
    return pl.pallas_call(
        gradient_kernel,
        in_specs=[pl.BlockSpec(memory_space=pltpu.SMEM)]
        + [pl.BlockSpec(memory_space=pltpu.VMEM)] * (len(pieces) + 2),
        out_specs=pl.BlockSpec(memory_space=pltpu.VMEM),
        out_shape=jax.ShapeDtypeStruct((width, depth), jnp.float32),
        compiler_params=pltpu.CompilerParams(vmem_limit_bytes=VMEM_BYTES),
        cost_estimate=pl.CostEstimate(
            flops=2 * rows * depth * width,
            bytes_accessed=2 * rows * (depth + width) + 4 * width * depth,
            transcendentals=0,
        ),
    )(sources, early, late, *pieces)


def chip_core(x, y, core):
    return (x % SIDE * SIDE + y % SIDE) * 2 + core


def route(turn, sign):
    pairs = []
    for x in range(SIDE):
        for y in range(SIDE):
            for core in range(2):
                along = (sign, 0) if core == turn else (0, sign)
                pairs.append(
                    (chip_core(x, y, core), chip_core(x + along[0], y + along[1], core))
                )
    return pairs


def hops(block, turn):
    below = lax.ppermute(block, "dp", route(turn, 1))
    above = lax.ppermute(block, "dp", route(turn, -1))
    return below, above


def far_hops(below, above, turn):
    half = below.shape[0] // 2
    first = lax.ppermute(below[:half], "dp", route(turn, 1))
    second = lax.ppermute(above[half:], "dp", route(turn, -1))
    return first, second


def other_core(block):
    return lax.ppermute(block, "dp", [(d, d ^ 1) for d in range(2 * SIDE * SIDE)])


def sources_table():
    table = []
    for x in range(SIDE):
        for y in range(SIDE):
            for core in range(2):
                found = []
                for outer in OFFSETS:
                    for sender in (core, 1 - core):
                        for inner in OFFSETS:
                            along = (inner, outer) if sender == 0 else (outer, inner)
                            found.append(chip_core(x + along[0], y + along[1], sender))
                table.append(found)
    return np.asarray(table, np.int32)


def finish_kernel(summed_ref, slope_ref, table_ref, out_ref, inner):
    devices, step, width = summed_ref.shape
    members, per_width = out_ref.shape[0], width // TABLE
    per_shard = devices // members
    upstream = (summed_ref[...].astype(jnp.float32) * slope_ref[...]).astype(jnp.bfloat16)
    upstream = upstream.reshape(devices * step, width)
    for c in range(per_width):
        inner[c] = jnp.dot(
            upstream[:, c * TABLE : (c + 1) * TABLE],
            table_ref[...],
            preferred_element_type=jnp.float32,
        )
    span = lambda d: slice(d * step, (d + 1) * step)
    for l in range(TABLE // LANES):
        lanes = slice(l * LANES, (l + 1) * LANES)
        for t in range(members):
            near = [(c, span(t * per_shard + k)) for k in range(per_shard) for c in range(per_width)]
            parts = butterfly([inner[c, rows, lanes] for c, rows in near])
            for (c, rows), part in zip(near, parts):
                inner[c, rows, lanes] = part
        for k in range(per_shard):
            for c in range(per_width):
                far = [span(t * per_shard + k) for t in range(members)]
                parts = butterfly([inner[c, rows, lanes] for rows in far])
                start = (k * per_width + c) * TABLE + l * LANES
                for t in range(members):
                    out_ref[t, :, start : start + LANES] = (parts[t] * NORM).astype(out_ref.dtype)


def finish(summed, slope, table, members):
    devices, step, width = summed.shape
    return pl.pallas_call(
        finish_kernel,
        out_shape=jax.ShapeDtypeStruct((members, step, WIDTH // members), jnp.bfloat16),
        scratch_shapes=[pltpu.VMEM((width // TABLE, devices * step, TABLE), jnp.float32)],
        compiler_params=pltpu.CompilerParams(vmem_limit_bytes=VMEM_BYTES),
        cost_estimate=pl.CostEstimate(
            flops=2 * step * WIDTH * BLOCK, bytes_accessed=8 * step * WIDTH, transcendentals=0
        ),
    )(summed, slope, table)


def shards(activations, weight, grad_out):
    dp = lax.axis_size("dp")
    members = lax.axis_size("tensor")
    tokens, features = activations.shape
    width = weight.shape[0]
    place = lax.axis_index("tensor").astype(jnp.int32).reshape(1)
    sources = jnp.asarray(sources_table())[lax.axis_index("dp")]
    table = hadamard_table(TABLE)
    step, half = tokens // members, tokens // 2
    early_rows, late_rows, grad_out = lax.optimization_barrier(
        (activations[:half], activations[half:], grad_out)
    )
    wide_early = lax.all_gather(early_rows, "tensor", axis=0, tiled=False)
    wide_late = lax.all_gather(late_rows, "tensor", axis=0, tiled=False)
    below, above = hops(grad_out, 0)
    near = jnp.concatenate([grad_out, below, above, *far_hops(below, above, 0)], axis=0)
    below, above = hops(near, 1)
    near_pair = [near, other_core(near)]
    partial_rows = product(None, near_pair, weight, 0, members)
    below, above, partial_rows = lax.optimization_barrier((below, above, partial_rows))
    first, second = far_hops(below, above, 1)
    below_pair = [below, other_core(below)]
    above_pair = [above, other_core(above)]
    early, early_slope = quantize(wide_early, table, place, dp, step, width)
    q_early = lax.all_to_all(early, "dp", split_axis=0, concat_axis=0, tiled=True)
    partial_rows, early_slope = lax.optimization_barrier((partial_rows, early_slope))
    partial_rows = product(partial_rows, below_pair, weight, 1, members)
    partial_rows = product(partial_rows, above_pair, weight, 2, members)
    first, second, partial_rows = lax.optimization_barrier((first, second, partial_rows))
    far_pair = [first, second, other_core(first), other_core(second)]
    partial_rows = product(partial_rows, far_pair, weight, 3, members)
    partial_rows, wide_late = lax.optimization_barrier((partial_rows, wide_late))
    summed = lax.psum_scatter(partial_rows, "tensor", scatter_dimension=0, tiled=False)
    late, late_slope = quantize(wide_late, table, place - members // 2, dp, step, width)
    slope = jnp.where(place[0] < members // 2, early_slope, late_slope)
    q_late = lax.all_to_all(late, "dp", split_axis=0, concat_axis=0, tiled=True)
    summed, q_early, q_late = lax.optimization_barrier((summed, q_early, q_late))
    ordered = order(summed.reshape(dp, step, width), sources)
    homed = lax.all_to_all(ordered, "dp", split_axis=0, concat_axis=0, tiled=True)
    mixed = finish(homed, slope, table, members)
    grad_input = lax.all_to_all(mixed, "tensor", split_axis=0, concat_axis=0, tiled=True)
    weight_sum = gradient(
        sources, q_early, q_late, near_pair + below_pair + above_pair + far_pair
    )
    return (grad_input.reshape(tokens, features), weight_sum)


def solution(mesh):
    return jax.shard_map(
        shards,
        mesh=mesh,
        in_specs=(P("dp", "tensor"), P("dp", "tensor"), P("dp", "tensor")),
        out_specs=(P("dp", "tensor"), P("dp", "tensor")),
        check_vma=False,
    )
```

```python
import math

import jax
import jax.numpy as jnp
import numpy as np
from jax import lax
from jax.experimental import pallas as pl
from jax.experimental.pallas import tpu as pltpu
from jax.sharding import PartitionSpec as P

BLOCK = 1024
WIDTH = 16384
TABLE = 256
LANES = 128
VMEM_BYTES = 60 * 1024 * 1024
NORM = 1.0 / math.sqrt(WIDTH)
SIDE = 4
STEP = 16
OFFSETS = (0, -1, 1, -2)

levels = 127.0
ripple = 0.5
epsilon = 1e-06


def hadamard_table(length):
    table = np.ones((1, 1), np.float32)
    while table.shape[0] < length:
        table = np.block([[table, table], [table, -table]])
    return jnp.asarray(table, jnp.bfloat16)


def fit(odd, terms):
    nodes = 0.5 * np.cos(np.pi * (np.arange(400) + 0.5) / 800.0)
    squares = nodes * nodes
    values = np.sin(2.0 * np.pi * nodes) / nodes if odd else np.cos(2.0 * np.pi * nodes)
    scaled = np.polynomial.chebyshev.Chebyshev.fit(squares, values, terms - 1, domain=[0.0, 0.25])
    return [float(c) for c in scaled.convert(kind=np.polynomial.Polynomial).coef]


SINE = fit(True, 6)
COSINE = fit(False, 7)


def horner(coefficients, square):
    total = jnp.full_like(square, coefficients[-1])
    for coefficient in coefficients[-2::-1]:
        total = total * square + coefficient
    return total


def butterfly(parts):
    distance = 1
    while distance < len(parts):
        mixed = list(parts)
        for low in range(len(parts)):
            if not low & distance:
                mixed[low] = parts[low] + parts[low | distance]
                mixed[low | distance] = parts[low] - parts[low | distance]
        parts = mixed
        distance *= 2
    return parts


def quantize_kernel(place, rows_ref, table_ref, quantized_ref, slope_ref, inner, mixed):
    members, count, features = rows_ref.shape
    step, width = slope_ref.shape[1:]
    chunks, per_shard, per_width = features // TABLE, features // width, width // TABLE
    rows = rows_ref[...].reshape(members * count, features)
    for c in range(chunks):
        inner[c] = jnp.dot(
            rows[:, c * TABLE : (c + 1) * TABLE],
            table_ref[...],
            preferred_element_type=jnp.float32,
        )
    halves = [slice(l * LANES, (l + 1) * LANES) for l in range(TABLE // LANES)]
    for group in range(count // step):
        spans = [
            slice(t * count + group * step, t * count + (group + 1) * step)
            for t in range(members)
        ]
        here = slice(group * step, (group + 1) * step)
        for span in spans:
            for lanes in halves:
                parts = butterfly([inner[c, span, lanes] for c in range(chunks)])
                for c in range(chunks):
                    inner[c, span, lanes] = parts[c]
        largest = jnp.zeros((step, LANES), jnp.float32)
        for c in range(chunks):
            for lanes in halves:
                parts = butterfly([inner[c, span, lanes] for span in spans])
                for span, part in zip(spans, parts):
                    mixed[c, span, lanes] = part
                    largest = jnp.maximum(largest, jnp.abs(part))
        peak = jnp.max(largest, axis=1, keepdims=True) * NORM
        scale = (peak + epsilon) / levels
        inverse = jnp.broadcast_to(NORM / scale, (step, LANES))
        depth = jnp.broadcast_to((ripple / (2.0 * math.pi)) * scale, (step, LANES))

        def remainder(value):
            turns = value * inverse
            return turns - jnp.round(turns)

        def places():
            for t, span in enumerate(spans):
                for c in range(chunks):
                    for l, lanes in enumerate(halves):
                        start = (c % per_width) * TABLE + l * LANES
                        yield t * per_shard + c // per_width, start, mixed[c, span, lanes]

        for block, start, value in places():
            rest = remainder(value)
            sine = rest * horner(SINE, rest * rest)
            quantized_ref[block, here, start : start + LANES] = (
                value * NORM - depth * sine
            ).astype(jnp.bfloat16)

        @pl.when(pl.program_id(0) * (count // step) + group == place[0])
        def _():
            for block, start, value in places():
                rest = remainder(value)
                slope_ref[block, :, start : start + LANES] = 1.0 - ripple * horner(
                    COSINE, rest * rest
                )


def quantize(rows, table, place, dp, width):
    members, tokens, features = rows.shape
    step = tokens // members
    count = 2 * step
    return pl.pallas_call(
        quantize_kernel,
        grid_spec=pltpu.PrefetchScalarGridSpec(
            num_scalar_prefetch=1,
            grid=(tokens // count,),
            in_specs=[
                pl.BlockSpec((members, count, features), lambda i, place: (0, i, 0)),
                pl.BlockSpec((TABLE, TABLE), lambda i, place: (0, 0)),
            ],
            out_specs=[
                pl.BlockSpec((dp, count, width), lambda i, place: (0, i, 0)),
                pl.BlockSpec((dp, step, width), lambda i, place: (0, 0, 0)),
            ],
            scratch_shapes=[
                pltpu.VMEM((features // TABLE, members * count, TABLE), jnp.float32),
                pltpu.VMEM((features // TABLE, members * count, TABLE), jnp.float32),
            ],
        ),
        out_shape=[
            jax.ShapeDtypeStruct((dp, tokens, width), jnp.bfloat16),
            jax.ShapeDtypeStruct((dp, step, width), jnp.float32),
        ],
        compiler_params=pltpu.CompilerParams(vmem_limit_bytes=VMEM_BYTES),
        cost_estimate=pl.CostEstimate(
            flops=2 * tokens * WIDTH * BLOCK, bytes_accessed=4 * tokens * WIDTH, transcendentals=0
        ),
    )(place, rows, table)


def product_kernel(*refs):
    weight_ref, out_ref = refs[-2:]
    pieces = [ref for ref in refs[:-2] if len(ref.shape) == 2]
    members, step = out_ref.shape[0], STEP
    done = 0
    for piece_ref in pieces:
        rows, depth = piece_ref.shape
        result = lax.dot_general(
            piece_ref[...],
            weight_ref[...],
            (((1,), (1,)), ((), ())),
            preferred_element_type=jnp.float32,
        ).astype(out_ref.dtype)
        for k in range(rows // (members * step)):
            for t in range(members):
                start = (k * members + t) * step
                out_ref[t, done * step : (done + 1) * step, :] = result[start : start + step]
            done += 1


def product(held, pieces, weight, position, members, total):
    rows = sum(piece.shape[0] for piece in pieces)
    width, depth = weight.shape
    whole = [pl.BlockSpec(memory_space=pltpu.VMEM)] * (len(pieces) + 1)
    earlier = [] if held is None else [held]
    return pl.pallas_call(
        product_kernel,
        grid=(1,),
        in_specs=[pl.BlockSpec(memory_space=pl.ANY)] * len(earlier) + whole,
        out_specs=pl.BlockSpec((members, rows // members, width), lambda i: (0, position, 0)),
        out_shape=jax.ShapeDtypeStruct((members, total // members, width), jnp.bfloat16),
        input_output_aliases={0: 0} if earlier else {},
        compiler_params=pltpu.CompilerParams(vmem_limit_bytes=VMEM_BYTES),
        cost_estimate=pl.CostEstimate(
            flops=2 * rows * depth * width,
            bytes_accessed=2 * rows * (depth + width),
            transcendentals=0,
        ),
    )(*earlier, *pieces, weight)


def order_kernel(sources, rows_ref, out_ref):
    for slot in range(rows_ref.shape[0]):
        out_ref[sources[slot]] = rows_ref[slot]


def order(rows, sources):
    return pl.pallas_call(
        order_kernel,
        in_specs=[
            pl.BlockSpec(memory_space=pltpu.SMEM),
            pl.BlockSpec(memory_space=pltpu.VMEM),
        ],
        out_specs=pl.BlockSpec(memory_space=pltpu.VMEM),
        out_shape=jax.ShapeDtypeStruct(rows.shape, rows.dtype),
        compiler_params=pltpu.CompilerParams(vmem_limit_bytes=VMEM_BYTES),
    )(sources, rows)


def gradient_kernel(sources, quantized_ref, *refs):
    out_ref = refs[-1]
    pieces = refs[:-1]
    tokens = quantized_ref.shape[1]
    slot = 0
    for number, piece_ref in enumerate(pieces):
        count = piece_ref.shape[0] // tokens
        block = jnp.concatenate(
            [quantized_ref[sources[slot + k]] for k in range(count)], axis=0
        )
        slot += count
        term = lax.dot_general(
            block, piece_ref[...], (((0,), (0,)), ((), ())), preferred_element_type=jnp.float32
        )
        out_ref[...] = term if number == 0 else out_ref[...] + term


def gradient(sources, quantized, pieces):
    width, depth = quantized.shape[2], pieces[0].shape[1]
    rows = sum(piece.shape[0] for piece in pieces)
    return pl.pallas_call(
        gradient_kernel,
        in_specs=[pl.BlockSpec(memory_space=pltpu.SMEM)]
        + [pl.BlockSpec(memory_space=pltpu.VMEM)] * (len(pieces) + 1),
        out_specs=pl.BlockSpec(memory_space=pltpu.VMEM),
        out_shape=jax.ShapeDtypeStruct((width, depth), jnp.float32),
        compiler_params=pltpu.CompilerParams(vmem_limit_bytes=VMEM_BYTES),
        cost_estimate=pl.CostEstimate(
            flops=2 * rows * depth * width,
            bytes_accessed=2 * rows * (depth + width) + 4 * width * depth,
            transcendentals=0,
        ),
    )(sources, quantized, *pieces)


def chip_core(x, y, core):
    return (x % SIDE * SIDE + y % SIDE) * 2 + core


def route(turn, sign):
    pairs = []
    for x in range(SIDE):
        for y in range(SIDE):
            for core in range(2):
                along = (sign, 0) if core == turn else (0, sign)
                pairs.append(
                    (chip_core(x, y, core), chip_core(x + along[0], y + along[1], core))
                )
    return pairs


def send(block, turn, sign):
    return lax.ppermute(block, "dp", route(turn, sign))


def other_core(block):
    return lax.ppermute(block, "dp", [(d, d ^ 1) for d in range(2 * SIDE * SIDE)])


def sources_table():
    table = []
    for x in range(SIDE):
        for y in range(SIDE):
            for core in range(2):
                found = []
                for outer in OFFSETS:
                    for sender in (core, 1 - core):
                        for inner in OFFSETS:
                            along = (inner, outer) if sender == 0 else (outer, inner)
                            found.append(chip_core(x + along[0], y + along[1], sender))
                table.append(found)
    return np.asarray(table, np.int32)


def finish_kernel(summed_ref, slope_ref, table_ref, out_ref, inner):
    devices, step, width = summed_ref.shape
    members, per_width = out_ref.shape[0], width // TABLE
    per_shard = devices // members
    upstream = (summed_ref[...].astype(jnp.float32) * slope_ref[...]).astype(jnp.bfloat16)
    upstream = upstream.reshape(devices * step, width)
    for c in range(per_width):
        inner[c] = jnp.dot(
            upstream[:, c * TABLE : (c + 1) * TABLE],
            table_ref[...],
            preferred_element_type=jnp.float32,
        )
    span = lambda d: slice(d * step, (d + 1) * step)
    for l in range(TABLE // LANES):
        lanes = slice(l * LANES, (l + 1) * LANES)
        for t in range(members):
            near = [(c, span(t * per_shard + k)) for k in range(per_shard) for c in range(per_width)]
            parts = butterfly([inner[c, rows, lanes] for c, rows in near])
            for (c, rows), part in zip(near, parts):
                inner[c, rows, lanes] = part
        for k in range(per_shard):
            for c in range(per_width):
                far = [span(t * per_shard + k) for t in range(members)]
                parts = butterfly([inner[c, rows, lanes] for rows in far])
                start = (k * per_width + c) * TABLE + l * LANES
                for t in range(members):
                    out_ref[t, :, start : start + LANES] = (parts[t] * NORM).astype(out_ref.dtype)


def finish(summed, slope, table, members):
    devices, step, width = summed.shape
    return pl.pallas_call(
        finish_kernel,
        out_shape=jax.ShapeDtypeStruct((members, step, WIDTH // members), jnp.bfloat16),
        scratch_shapes=[pltpu.VMEM((width // TABLE, devices * step, TABLE), jnp.float32)],
        compiler_params=pltpu.CompilerParams(vmem_limit_bytes=VMEM_BYTES),
        cost_estimate=pl.CostEstimate(
            flops=2 * step * WIDTH * BLOCK, bytes_accessed=8 * step * WIDTH, transcendentals=0
        ),
    )(summed, slope, table)


def shards(activations, weight, grad_out):
    dp = lax.axis_size("dp")
    members = lax.axis_size("tensor")
    tokens, features = activations.shape
    width = weight.shape[0]
    place = lax.axis_index("tensor").astype(jnp.int32).reshape(1)
    sources = jnp.asarray(sources_table())[lax.axis_index("dp")]
    table = hadamard_table(TABLE)
    wide_rows = lax.all_gather(activations, "tensor", axis=0, tiled=False)
    total = dp * tokens

    def multiply(held, pieces, position):
        return product(held, pieces, weight, position, members, total)

    half = tokens // 2
    below, above = send(grad_out, 0, 1), send(grad_out, 0, -1)
    top = jnp.concatenate([grad_out, below], axis=0)
    below_top, above_top = send(top, 1, 1), send(top, 1, -1)
    far = [send(below[:half], 0, 1), send(above[half:], 0, -1)]
    bottom = jnp.concatenate([above, *far], axis=0)
    below_bottom, above_bottom = send(bottom, 1, 1), send(bottom, 1, -1)
    far_top = send(below_top, 1, 1)
    near = [top, bottom]
    near_other = [other_core(block) for block in near]
    held = multiply(None, near + near_other, 0)
    below_bottom, above_bottom, held = lax.optimization_barrier(
        (below_bottom, above_bottom, held)
    )
    far_bottom = send(above_bottom, 1, -1)
    below, above = [below_top, below_bottom], [above_top, above_bottom]
    below_other = [other_core(block) for block in below]
    above_other = [other_core(block) for block in above]
    held = multiply(held, below + below_other, 1)
    held = multiply(held, above + above_other, 2)
    far_top, far_bottom, held = lax.optimization_barrier((far_top, far_bottom, held))
    far = [far_top, far_bottom]
    far_other = [other_core(block) for block in far]
    held = multiply(held, far, 6)
    partial_rows = multiply(held, far_other, 7)
    partial_rows, wide_rows = lax.optimization_barrier((partial_rows, wide_rows))
    summed = lax.psum_scatter(partial_rows, "tensor", scatter_dimension=0, tiled=False)
    quantized, slope = quantize(wide_rows, table, place, dp, width)
    q_block = lax.all_to_all(quantized, "dp", split_axis=0, concat_axis=0, tiled=True)
    ordered = order(summed.reshape(dp, tokens // members, width), sources)
    ordered, q_block = lax.optimization_barrier((ordered, q_block))
    homed = lax.all_to_all(ordered, "dp", split_axis=0, concat_axis=0, tiled=True)
    mixed = finish(homed, slope, table, members)
    grad_input = lax.all_to_all(mixed, "tensor", split_axis=0, concat_axis=0, tiled=True)
    arrived = near + near_other + below + below_other + above + above_other + far + far_other
    weight_sum = gradient(sources, q_block, arrived)
    return (grad_input.reshape(tokens, features), weight_sum)


def solution(mesh):
    return jax.shard_map(
        shards,
        mesh=mesh,
        in_specs=(P("dp", "tensor"), P("dp", "tensor"), P("dp", "tensor")),
        out_specs=(P("dp", "tensor"), P("dp", "tensor")),
        check_vma=False,
    )
```

```python
import functools
import math

import jax
import jax.numpy as jnp
import numpy as np
from jax import lax
from jax.experimental import pallas as pl
from jax.experimental.pallas import tpu as pltpu
from jax.sharding import PartitionSpec as P

BLOCK = 1024
WIDTH = 16384
TABLE = 256
LANES = 128
VMEM_BYTES = 60 * 1024 * 1024
NORM = 1.0 / math.sqrt(WIDTH)
SIDE = 4
STEP = 16
OFFSETS = (0, -1, 1, -2)

levels = 127.0
ripple = 0.5
epsilon = 1e-06


def hadamard_table(length):
    table = np.ones((1, 1), np.float32)
    while table.shape[0] < length:
        table = np.block([[table, table], [table, -table]])
    return jnp.asarray(table, jnp.bfloat16)


def fit(odd, terms):
    nodes = 0.5 * np.cos(np.pi * (np.arange(400) + 0.5) / 800.0)
    squares = nodes * nodes
    values = np.sin(2.0 * np.pi * nodes) / nodes if odd else np.cos(2.0 * np.pi * nodes)
    scaled = np.polynomial.chebyshev.Chebyshev.fit(squares, values, terms - 1, domain=[0.0, 0.25])
    return [float(c) for c in scaled.convert(kind=np.polynomial.Polynomial).coef]


SINE = fit(True, 6)
COSINE = fit(False, 7)


def horner(coefficients, square):
    total = jnp.full_like(square, coefficients[-1])
    for coefficient in coefficients[-2::-1]:
        total = total * square + coefficient
    return total


def butterfly(parts):
    distance = 1
    while distance < len(parts):
        mixed = list(parts)
        for low in range(len(parts)):
            if not low & distance:
                mixed[low] = parts[low] + parts[low | distance]
                mixed[low | distance] = parts[low] - parts[low | distance]
        parts = mixed
        distance *= 2
    return parts


def levels_of(largest):
    rows = largest.shape[0]
    peak = jnp.max(largest, axis=1, keepdims=True) * NORM
    scale = (peak + epsilon) / levels
    inverse = jnp.broadcast_to(NORM / scale, (rows, LANES))
    depth = jnp.broadcast_to((ripple / (2.0 * math.pi)) * scale, (rows, LANES))
    return inverse, depth


def remainder(value, inverse):
    turns = value * inverse
    return turns - jnp.round(turns)


def quantized_of(value, inverse, depth):
    rest = remainder(value, inverse)
    return value * NORM - depth * (rest * horner(SINE, rest * rest))


def slope_of(value, inverse):
    rest = remainder(value, inverse)
    return 1.0 - ripple * horner(COSINE, rest * rest)


def quantize_kernel(place, rows_ref, table_ref, quantized_ref, slope_ref, inner, mixed):
    members, count, features = rows_ref.shape
    own, width = slope_ref.shape[1:]
    chunks, per_shard, per_width = features // TABLE, features // width, width // TABLE
    rows = rows_ref[...].reshape(members * count, features)
    for c in range(chunks):
        inner[c] = jnp.dot(
            rows[:, c * TABLE : (c + 1) * TABLE],
            table_ref[...],
            preferred_element_type=jnp.float32,
        )
    halves = [slice(l * LANES, (l + 1) * LANES) for l in range(TABLE // LANES)]
    for group in range(count // STEP):
        spans = [
            slice(t * count + group * STEP, t * count + (group + 1) * STEP)
            for t in range(members)
        ]
        here = slice(group * STEP, (group + 1) * STEP)
        for span in spans:
            for lanes in halves:
                parts = butterfly([inner[c, span, lanes] for c in range(chunks)])
                for c in range(chunks):
                    inner[c, span, lanes] = parts[c]
        largest = jnp.zeros((STEP, LANES), jnp.float32)
        for c in range(chunks):
            for lanes in halves:
                parts = butterfly([inner[c, span, lanes] for span in spans])
                for span, part in zip(spans, parts):
                    mixed[c, span, lanes] = part
                    largest = jnp.maximum(largest, jnp.abs(part))
        inverse, depth = levels_of(largest)

        def places():
            for t, span in enumerate(spans):
                for c in range(chunks):
                    for l, lanes in enumerate(halves):
                        start = (c % per_width) * TABLE + l * LANES
                        yield t * per_shard + c // per_width, start, (c, span, lanes)

        for block, start, index in places():
            quantized_ref[block, here, start : start + LANES] = quantized_of(
                mixed[index], inverse, depth
            ).astype(jnp.bfloat16)

        for part in range(STEP // own):
            mine = slice(part * own, (part + 1) * own)
            number = (pl.program_id(0) * (count // STEP) + group) * (STEP // own) + part

            @pl.when(number == place[0])
            def _():
                for block, start, (c, span, lanes) in places():
                    slope_ref[block, :, start : start + LANES] = slope_of(
                        mixed[c, span.start + mine.start : span.start + mine.stop, lanes],
                        inverse[mine],
                    )


def quantize(rows, table, place, dp, width):
    members, tokens, features = rows.shape
    own = tokens // members
    count = 2 * STEP
    return pl.pallas_call(
        quantize_kernel,
        grid_spec=pltpu.PrefetchScalarGridSpec(
            num_scalar_prefetch=1,
            grid=(tokens // count,),
            in_specs=[
                pl.BlockSpec((members, count, features), lambda i, place: (0, i, 0)),
                pl.BlockSpec((TABLE, TABLE), lambda i, place: (0, 0)),
            ],
            out_specs=[
                pl.BlockSpec((dp, count, width), lambda i, place: (0, i, 0)),
                pl.BlockSpec((dp, own, width), lambda i, place: (0, 0, 0)),
            ],
            scratch_shapes=[
                pltpu.VMEM((features // TABLE, members * count, TABLE), jnp.float32),
                pltpu.VMEM((features // TABLE, members * count, TABLE), jnp.float32),
            ],
        ),
        out_shape=[
            jax.ShapeDtypeStruct((dp, tokens, width), jnp.bfloat16),
            jax.ShapeDtypeStruct((dp, own, width), jnp.float32),
        ],
        compiler_params=pltpu.CompilerParams(vmem_limit_bytes=VMEM_BYTES),
        cost_estimate=pl.CostEstimate(
            flops=2 * tokens * WIDTH * BLOCK, bytes_accessed=4 * tokens * WIDTH, transcendentals=0
        ),
    )(place, rows, table)


def quantize_own_kernel(rows_ref, table_ref, quantized_ref, slope_ref, inner):
    devices, own, width = slope_ref.shape
    features = rows_ref.shape[1]
    members = rows_ref.shape[0] // own
    chunks, per_width = features // TABLE, width // TABLE
    for c in range(chunks):
        inner[c] = jnp.dot(
            rows_ref[:, c * TABLE : (c + 1) * TABLE],
            table_ref[...],
            preferred_element_type=jnp.float32,
        )
    halves = [slice(l * LANES, (l + 1) * LANES) for l in range(TABLE // LANES)]
    spans = [slice(t * own, (t + 1) * own) for t in range(members)]
    for span in spans:
        for lanes in halves:
            parts = butterfly([inner[c, span, lanes] for c in range(chunks)])
            for c in range(chunks):
                inner[c, span, lanes] = parts[c]
    largest = jnp.zeros((own, LANES), jnp.float32)
    for c in range(chunks):
        for lanes in halves:
            parts = butterfly([inner[c, span, lanes] for span in spans])
            for span, part in zip(spans, parts):
                inner[c, span, lanes] = part
                largest = jnp.maximum(largest, jnp.abs(part))
    inverse, depth = levels_of(largest)
    per_shard = devices // members
    for pair in range(devices // 2):
        for k in range(per_width):
            for l, lanes in enumerate(halves):
                columns = slice(k * TABLE + l * LANES, k * TABLE + (l + 1) * LANES)
                found = []
                for block in (2 * pair, 2 * pair + 1):
                    t, c = block // per_shard, block % per_shard * per_width + k
                    value = inner[c, spans[t], lanes]
                    found.append(quantized_of(value, inverse, depth))
                    slope_ref[block, :, columns] = slope_of(value, inverse)
                quantized_ref[pair * 2 * own : (pair + 1) * 2 * own, columns] = jnp.concatenate(
                    found, axis=0
                ).astype(jnp.bfloat16)


def quantize_own(rows, table, dp, width):
    members, own, features = rows.shape
    return pl.pallas_call(
        quantize_own_kernel,
        out_shape=[
            jax.ShapeDtypeStruct((dp * own, width), jnp.bfloat16),
            jax.ShapeDtypeStruct((dp, own, width), jnp.float32),
        ],
        scratch_shapes=[pltpu.VMEM((features // TABLE, members * own, TABLE), jnp.float32)],
        compiler_params=pltpu.CompilerParams(vmem_limit_bytes=VMEM_BYTES),
        cost_estimate=pl.CostEstimate(
            flops=2 * own * WIDTH * BLOCK, bytes_accessed=8 * own * WIDTH, transcendentals=0
        ),
    )(rows.reshape(members * own, features), table)


def product_kernel(count, slots, sources, *refs):
    pieces, weight_ref = refs[:count], refs[count]
    out_ref, weight, rows, results, weight_sem, in_sems, out_sems = refs[-7:]
    members = out_ref.shape[0]
    load_weight = pltpu.make_async_copy(weight_ref, weight, weight_sem)
    load_weight.start()
    loads = [pltpu.make_async_copy(pieces[n], rows.at[n], in_sems.at[n]) for n in range(count)]
    for load in loads:
        load.start()
    load_weight.wait()
    stores = []
    for n in range(count):
        loads[n].wait()
        product = lax.dot_general(
            rows[n], weight[...], (((1,), (1,)), ((), ())), preferred_element_type=jnp.float32
        )
        for k in range(2):
            for t in range(members):
                starts = [k * 16 * members + half * 8 * members + t * 8 for half in range(2)]
                results[n, k, t] = jnp.concatenate(
                    [product[start : start + 8] for start in starts], axis=0
                ).astype(results.dtype)
            place = pl.multiple_of(sources[slots[n] + k] * STEP, STEP)
            store = pltpu.make_async_copy(
                results.at[n, k], out_ref.at[:, pl.ds(place, STEP), :], out_sems.at[n, k]
            )
            store.start()
            stores.append(store)
    for store in stores:
        store.wait()


def product(held, pieces, slots, weight, sources, members, total):
    count, rows = len(pieces), pieces[0].shape[0]
    width, depth = weight.shape
    earlier = [] if held is None else [held]
    return pl.pallas_call(
        functools.partial(product_kernel, count, slots),
        in_specs=[pl.BlockSpec(memory_space=pltpu.SMEM)]
        + [pl.BlockSpec(memory_space=pl.ANY)] * (count + 1 + len(earlier)),
        out_specs=pl.BlockSpec(memory_space=pl.ANY),
        out_shape=jax.ShapeDtypeStruct((members, total // members, width), jnp.bfloat16),
        scratch_shapes=[
            pltpu.VMEM((width, depth), jnp.bfloat16),
            pltpu.VMEM((count, rows, depth), jnp.bfloat16),
            pltpu.VMEM((count, 2, members, STEP, width), jnp.bfloat16),
            pltpu.SemaphoreType.DMA,
            pltpu.SemaphoreType.DMA((count,)),
            pltpu.SemaphoreType.DMA((count, 2)),
        ],
        input_output_aliases={count + 2: 0} if earlier else {},
        compiler_params=pltpu.CompilerParams(vmem_limit_bytes=VMEM_BYTES),
        cost_estimate=pl.CostEstimate(
            flops=2 * count * rows * depth * width,
            bytes_accessed=2 * count * rows * (depth + width),
            transcendentals=0,
        ),
    )(sources, *pieces, weight, *earlier)


def gradient_kernel(half, held, sources, quantized_ref, *refs):
    out_ref = refs[-1]
    pieces = refs[1:-1] if held else refs[:-1]
    tokens = quantized_ref.shape[1]
    total = refs[0][...] if held else None
    slot = 0
    for first in range(0, len(pieces), 2):
        pair = pieces[first : first + 2]
        rows, block = [], []
        for piece_ref in pair:
            for k in range(piece_ref.shape[0] // (2 * tokens)):
                start = (2 * k + half) * tokens
                rows.append(piece_ref[start : start + tokens, :])
                block.append(quantized_ref[sources[slot]])
                slot += 1
        term = lax.dot_general(
            jnp.concatenate(block, axis=0),
            jnp.concatenate(rows, axis=0),
            (((0,), (0,)), ((), ())),
            preferred_element_type=jnp.float32,
        )
        total = term if total is None else total + term
    out_ref[...] = total


def gradient(held, half, sources, quantized, pieces):
    width, depth = quantized.shape[2], pieces[0].shape[1]
    rows = sum(piece.shape[0] for piece in pieces) // 2
    earlier = [] if held is None else [held]
    return pl.pallas_call(
        functools.partial(gradient_kernel, half, bool(earlier)),
        in_specs=[pl.BlockSpec(memory_space=pltpu.SMEM)]
        + [pl.BlockSpec(memory_space=pltpu.VMEM)] * (len(pieces) + 1 + len(earlier)),
        out_specs=pl.BlockSpec(memory_space=pltpu.VMEM),
        out_shape=jax.ShapeDtypeStruct((width, depth), jnp.float32),
        compiler_params=pltpu.CompilerParams(vmem_limit_bytes=VMEM_BYTES),
        cost_estimate=pl.CostEstimate(
            flops=2 * rows * depth * width,
            bytes_accessed=2 * rows * (depth + width) + 4 * width * depth,
            transcendentals=0,
        ),
    )(sources, quantized, *earlier, *pieces)


def chip_core(x, y, core):
    return (x % SIDE * SIDE + y % SIDE) * 2 + core


def route(turn, sign):
    pairs = []
    for x in range(SIDE):
        for y in range(SIDE):
            for core in range(2):
                along = (sign, 0) if core == turn else (0, sign)
                pairs.append(
                    (chip_core(x, y, core), chip_core(x + along[0], y + along[1], core))
                )
    return pairs


def send(block, turn, sign):
    return lax.ppermute(block, "dp", route(turn, sign))


def other_core(block):
    return lax.ppermute(block, "dp", [(d, d ^ 1) for d in range(2 * SIDE * SIDE)])


def sources_table():
    table = []
    for x in range(SIDE):
        for y in range(SIDE):
            for core in range(2):
                found = []
                for outer in OFFSETS:
                    for sender in (core, 1 - core):
                        for inner in OFFSETS:
                            along = (inner, outer) if sender == 0 else (outer, inner)
                            found.append(chip_core(x + along[0], y + along[1], sender))
                table.append(found)
    return np.asarray(table, np.int32)


def finish_kernel(summed_ref, early_ref, late_ref, table_ref, out_ref, inner):
    devices, step, width = summed_ref.shape
    members, per_width = out_ref.shape[0], width // TABLE
    per_shard = devices // members
    slope = jnp.concatenate([early_ref[...], late_ref[...]], axis=1)
    upstream = (summed_ref[...].astype(jnp.float32) * slope).astype(jnp.bfloat16)
    upstream = upstream.reshape(devices * step, width)
    for c in range(per_width):
        inner[c] = jnp.dot(
            upstream[:, c * TABLE : (c + 1) * TABLE],
            table_ref[...],
            preferred_element_type=jnp.float32,
        )
    span = lambda d: slice(d * step, (d + 1) * step)
    for l in range(TABLE // LANES):
        lanes = slice(l * LANES, (l + 1) * LANES)
        for t in range(members):
            near = [(c, span(t * per_shard + k)) for k in range(per_shard) for c in range(per_width)]
            parts = butterfly([inner[c, rows, lanes] for c, rows in near])
            for (c, rows), part in zip(near, parts):
                inner[c, rows, lanes] = part
        for k in range(per_shard):
            for c in range(per_width):
                far = [span(t * per_shard + k) for t in range(members)]
                parts = butterfly([inner[c, rows, lanes] for rows in far])
                start = (k * per_width + c) * TABLE + l * LANES
                for t in range(members):
                    out_ref[t, :, start : start + LANES] = (parts[t] * NORM).astype(out_ref.dtype)


def finish(summed, slopes, table, members):
    devices, step, width = summed.shape
    return pl.pallas_call(
        finish_kernel,
        out_shape=jax.ShapeDtypeStruct((members, step, WIDTH // members), jnp.bfloat16),
        scratch_shapes=[pltpu.VMEM((width // TABLE, devices * step, TABLE), jnp.float32)],
        compiler_params=pltpu.CompilerParams(vmem_limit_bytes=VMEM_BYTES),
        cost_estimate=pl.CostEstimate(
            flops=2 * step * WIDTH * BLOCK, bytes_accessed=8 * step * WIDTH, transcendentals=0
        ),
    )(summed, *slopes, table)


def shards(activations, weight, grad_out):
    dp = lax.axis_size("dp")
    members = lax.axis_size("tensor")
    tokens, features = activations.shape
    width = weight.shape[0]
    place = lax.axis_index("tensor").astype(jnp.int32).reshape(1)
    sources = jnp.asarray(sources_table())[lax.axis_index("dp")]
    table = hadamard_table(TABLE)
    total = dp * tokens
    own, half = STEP // 2, tokens // 2
    early_rows, late_rows = jnp.moveaxis(activations.reshape(members, 2, own, features), 1, 0)
    grad_out = jnp.moveaxis(grad_out.reshape(members, 2, own, -1), 1, 0).reshape(tokens, -1)
    early_rows, late_rows, grad_out = lax.optimization_barrier((early_rows, late_rows, grad_out))
    wide_rows = lax.all_gather(early_rows.reshape(half, features), "tensor", axis=0, tiled=False)
    late_rows = lax.all_to_all(late_rows, "tensor", split_axis=0, concat_axis=0, tiled=True)

    def multiply(held, pieces, slot):
        slots = [slot + 2 * n for n in range(len(pieces))]
        return product(held, pieces, slots, weight, sources, members, total)

    below, above = send(grad_out, 0, 1), send(grad_out, 0, -1)
    top = jnp.concatenate([grad_out, below], axis=0)
    below_top, above_top = send(top, 1, 1), send(top, 1, -1)
    far = [send(below[:half], 0, 1), send(above[half:], 0, -1)]
    bottom = jnp.concatenate([above, *far], axis=0)
    below_bottom, above_bottom = send(bottom, 1, 1), send(bottom, 1, -1)
    far_top = send(below_top, 1, 1)
    near = [top, bottom]
    near_other = [other_core(block) for block in near]
    held = multiply(None, near + near_other, 0)
    below_bottom, above_bottom, held = lax.optimization_barrier(
        (below_bottom, above_bottom, held)
    )
    far_bottom = send(above_bottom, 1, -1)
    below, above = [below_top, below_bottom], [above_top, above_bottom]
    below_other = [other_core(block) for block in below]
    above_other = [other_core(block) for block in above]
    held = multiply(held, below + below_other, 8)
    held = multiply(held, above + above_other, 16)
    late, late_slope = quantize_own(late_rows, table, dp, width)
    far_top, far_bottom, held, late = lax.optimization_barrier(
        (far_top, far_bottom, held, late)
    )
    far = [far_top, far_bottom]
    far_other = [other_core(block) for block in far]
    held = multiply(held, far, 24)
    partial_rows = multiply(held, far_other, 28)
    q_own = lax.all_to_all(
        late.reshape(dp, own, width), "dp", split_axis=0, concat_axis=0, tiled=True
    )
    partial_rows, wide_rows = lax.optimization_barrier((partial_rows, wide_rows))
    summed = lax.psum_scatter(partial_rows, "tensor", scatter_dimension=0, tiled=False)
    early, early_slope = quantize(wide_rows, table, place, dp, width)
    q_early = lax.all_to_all(early, "dp", split_axis=0, concat_axis=0, tiled=True)
    summed, q_early, q_own = lax.optimization_barrier((summed, q_early, q_own))
    homed = lax.all_to_all(
        summed.reshape(dp, STEP, width), "dp", split_axis=0, concat_axis=0, tiled=True
    )
    q_late = lax.all_gather(q_own, "tensor", axis=1, tiled=True)
    mixed = finish(homed, (early_slope, late_slope), table, members)
    grad_input = lax.all_to_all(mixed, "tensor", split_axis=0, concat_axis=0, tiled=True)
    arrived = near + near_other + below + below_other + above + above_other + far + far_other
    weight_sum = gradient(None, 0, sources, q_early, arrived)
    weight_sum = gradient(weight_sum, 1, sources, q_late, arrived)
    return (grad_input.reshape(tokens, features), weight_sum)


def solution(mesh):
    return jax.shard_map(
        shards,
        mesh=mesh,
        in_specs=(P("dp", "tensor"), P("dp", "tensor"), P("dp", "tensor")),
        out_specs=(P("dp", "tensor"), P("dp", "tensor")),
        check_vma=False,
    )
```

```python
import functools
import math

import jax
import jax.numpy as jnp
import numpy as np
from jax import lax
from jax.experimental import pallas as pl
from jax.experimental.pallas import tpu as pltpu
from jax.sharding import PartitionSpec as P

BLOCK = 1024
WIDTH = 16384
TABLE = 256
LANES = 128
VMEM_BYTES = 16 * 1024 * 1024
HELD = pltpu.HBM
NORM = 1.0 / math.sqrt(WIDTH)
SIDE = 4
STEP = 16
OFFSETS = (0, -1, 1, -2)

levels = 127.0
ripple = 0.5
epsilon = 1e-06


def hadamard_table(length):
    table = np.ones((1, 1), np.float32)
    while table.shape[0] < length:
        table = np.block([[table, table], [table, -table]])
    return jnp.asarray(table, jnp.bfloat16)


def fit(odd, terms):
    nodes = 0.5 * np.cos(np.pi * (np.arange(400) + 0.5) / 800.0)
    squares = nodes * nodes
    values = np.sin(2.0 * np.pi * nodes) / nodes if odd else np.cos(2.0 * np.pi * nodes)
    scaled = np.polynomial.chebyshev.Chebyshev.fit(squares, values, terms - 1, domain=[0.0, 0.25])
    return [float(c) for c in scaled.convert(kind=np.polynomial.Polynomial).coef]


SINE = fit(True, 6)
COSINE = fit(False, 7)


def horner(coefficients, square):
    total = jnp.full_like(square, coefficients[-1])
    for coefficient in coefficients[-2::-1]:
        total = total * square + coefficient
    return total


def butterfly(parts):
    distance = 1
    while distance < len(parts):
        mixed = list(parts)
        for low in range(len(parts)):
            if not low & distance:
                mixed[low] = parts[low] + parts[low | distance]
                mixed[low | distance] = parts[low] - parts[low | distance]
        parts = mixed
        distance *= 2
    return parts


def levels_of(largest):
    rows = largest.shape[0]
    peak = jnp.max(largest, axis=1, keepdims=True) * NORM
    scale = (peak + epsilon) / levels
    inverse = jnp.broadcast_to(NORM / scale, (rows, LANES))
    depth = jnp.broadcast_to((ripple / (2.0 * math.pi)) * scale, (rows, LANES))
    return inverse, depth


def remainder(value, inverse):
    turns = value * inverse
    return turns - jnp.round(turns)


def quantized_of(value, inverse, depth):
    rest = remainder(value, inverse)
    return value * NORM - depth * (rest * horner(SINE, rest * rest))


def slope_of(value, inverse):
    rest = remainder(value, inverse)
    return 1.0 - ripple * horner(COSINE, rest * rest)


def quantize_kernel(place, rows_ref, table_ref, quantized_ref, slope_ref, inner, mixed):
    members, count, features = rows_ref.shape
    own, width = slope_ref.shape[1:]
    chunks, per_shard, per_width = features // TABLE, features // width, width // TABLE
    rows = rows_ref[...].reshape(members * count, features)
    for c in range(chunks):
        inner[c] = jnp.dot(
            rows[:, c * TABLE : (c + 1) * TABLE],
            table_ref[...],
            preferred_element_type=jnp.float32,
        )
    halves = [slice(l * LANES, (l + 1) * LANES) for l in range(TABLE // LANES)]
    for group in range(count // STEP):
        spans = [
            slice(t * count + group * STEP, t * count + (group + 1) * STEP)
            for t in range(members)
        ]
        here = slice(group * STEP, (group + 1) * STEP)
        for span in spans:
            for lanes in halves:
                parts = butterfly([inner[c, span, lanes] for c in range(chunks)])
                for c in range(chunks):
                    inner[c, span, lanes] = parts[c]
        largest = jnp.zeros((STEP, LANES), jnp.float32)
        for c in range(chunks):
            for lanes in halves:
                parts = butterfly([inner[c, span, lanes] for span in spans])
                for span, part in zip(spans, parts):
                    mixed[c, span, lanes] = part
                    largest = jnp.maximum(largest, jnp.abs(part))
        inverse, depth = levels_of(largest)

        def places():
            for t, span in enumerate(spans):
                for c in range(chunks):
                    for l, lanes in enumerate(halves):
                        start = (c % per_width) * TABLE + l * LANES
                        yield t * per_shard + c // per_width, start, (c, span, lanes)

        for block, start, index in places():
            quantized_ref[block, here, start : start + LANES] = quantized_of(
                mixed[index], inverse, depth
            ).astype(jnp.bfloat16)

        for part in range(STEP // own):
            mine = slice(part * own, (part + 1) * own)
            number = (pl.program_id(0) * (count // STEP) + group) * (STEP // own) + part

            @pl.when(number == place[0])
            def _():
                for block, start, (c, span, lanes) in places():
                    slope_ref[block, :, start : start + LANES] = slope_of(
                        mixed[c, span.start + mine.start : span.start + mine.stop, lanes],
                        inverse[mine],
                    )


def quantize(rows, table, place, dp, width):
    members, tokens, features = rows.shape
    tokens, own, count = tokens // 2, STEP // 2, 2 * STEP
    return pl.pallas_call(
        quantize_kernel,
        grid_spec=pltpu.PrefetchScalarGridSpec(
            num_scalar_prefetch=1,
            grid=(tokens // count,),
            in_specs=[
                pl.BlockSpec((members, count, features), lambda i, place: (0, i, 0)),
                pl.BlockSpec((TABLE, TABLE), lambda i, place: (0, 0)),
            ],
            out_specs=[
                pl.BlockSpec((dp, count, width), lambda i, place: (0, i, 0)),
                pl.BlockSpec((dp, own, width), lambda i, place: (0, 0, 0)),
            ],
            scratch_shapes=[
                pltpu.VMEM((features // TABLE, members * count, TABLE), jnp.float32),
                pltpu.VMEM((features // TABLE, members * count, TABLE), jnp.float32),
            ],
        ),
        out_shape=[
            jax.ShapeDtypeStruct((dp, tokens, width), jnp.bfloat16),
            jax.ShapeDtypeStruct((dp, own, width), jnp.float32),
        ],
        compiler_params=pltpu.CompilerParams(vmem_limit_bytes=VMEM_BYTES),
        cost_estimate=pl.CostEstimate(
            flops=2 * tokens * WIDTH * BLOCK, bytes_accessed=4 * tokens * WIDTH, transcendentals=0
        ),
    )(place, rows, table)


def quantize_own_kernel(place, rows_ref, table_ref, quantized_ref, slope_ref, inner):
    devices, own, width = slope_ref.shape
    members, _, features = rows_ref.shape
    rows = rows_ref[...].reshape(members * STEP, features)
    shift = pl.multiple_of(place[0] % 2 * own, own)
    chunks, per_width = features // TABLE, width // TABLE
    for c in range(chunks):
        inner[c] = jnp.dot(
            rows[:, c * TABLE : (c + 1) * TABLE],
            table_ref[...],
            preferred_element_type=jnp.float32,
        )
    halves = [slice(l * LANES, (l + 1) * LANES) for l in range(TABLE // LANES)]
    spans = [pl.ds(pl.multiple_of(t * STEP + shift, own), own) for t in range(members)]
    for span in spans:
        for lanes in halves:
            parts = butterfly([inner[c, span, lanes] for c in range(chunks)])
            for c in range(chunks):
                inner[c, span, lanes] = parts[c]
    largest = jnp.zeros((own, LANES), jnp.float32)
    for c in range(chunks):
        for lanes in halves:
            parts = butterfly([inner[c, span, lanes] for span in spans])
            for span, part in zip(spans, parts):
                inner[c, span, lanes] = part
                largest = jnp.maximum(largest, jnp.abs(part))
    inverse, depth = levels_of(largest)
    per_shard = devices // members
    for pair in range(devices // 2):
        for k in range(per_width):
            for l, lanes in enumerate(halves):
                columns = slice(k * TABLE + l * LANES, k * TABLE + (l + 1) * LANES)
                found = []
                for block in (2 * pair, 2 * pair + 1):
                    t, c = block // per_shard, block % per_shard * per_width + k
                    value = inner[c, spans[t], lanes]
                    found.append(quantized_of(value, inverse, depth))
                    slope_ref[block, :, columns] = slope_of(value, inverse)
                quantized_ref[pair * 2 * own : (pair + 1) * 2 * own, columns] = jnp.concatenate(
                    found, axis=0
                ).astype(jnp.bfloat16)


def quantize_own(rows, table, place, dp, width):
    members, tokens, features = rows.shape
    own = STEP // 2
    first = tokens // 2 // STEP
    return pl.pallas_call(
        quantize_own_kernel,
        grid_spec=pltpu.PrefetchScalarGridSpec(
            num_scalar_prefetch=1,
            grid=(1,),
            in_specs=[
                pl.BlockSpec((members, STEP, features), lambda i, place: (0, first + place[0] // 2, 0)),
                pl.BlockSpec((TABLE, TABLE), lambda i, place: (0, 0)),
            ],
            out_specs=[
                pl.BlockSpec((dp * own, width), lambda i, place: (0, 0)),
                pl.BlockSpec((dp, own, width), lambda i, place: (0, 0, 0)),
            ],
            scratch_shapes=[pltpu.VMEM((features // TABLE, members * STEP, TABLE), jnp.float32)],
        ),
        out_shape=[
            jax.ShapeDtypeStruct((dp * own, width), jnp.bfloat16),
            jax.ShapeDtypeStruct((dp, own, width), jnp.float32),
        ],
        compiler_params=pltpu.CompilerParams(vmem_limit_bytes=VMEM_BYTES),
        cost_estimate=pl.CostEstimate(
            flops=2 * own * WIDTH * BLOCK, bytes_accessed=8 * own * WIDTH, transcendentals=0
        ),
    )(place, rows, table)


def product_kernel(count, slots, sources, *refs):
    pieces, weight_ref = refs[:count], refs[count]
    out_ref, results, out_sems = refs[-3:]
    members = out_ref.shape[0]
    stores = []
    for n in range(count):
        product = lax.dot_general(
            pieces[n][...],
            weight_ref[...],
            (((1,), (1,)), ((), ())),
            preferred_element_type=jnp.float32,
        )
        for k in range(2):
            for t in range(members):
                starts = [k * 16 * members + half * 8 * members + t * 8 for half in range(2)]
                results[n, k, t] = jnp.concatenate(
                    [product[start : start + 8] for start in starts], axis=0
                ).astype(results.dtype)
            place = pl.multiple_of(sources[slots[n] + k] * STEP, STEP)
            store = pltpu.make_async_copy(
                results.at[n, k], out_ref.at[:, pl.ds(place, STEP), :], out_sems.at[n, k]
            )
            store.start()
            stores.append(store)
    for store in stores:
        store.wait()


def product(held, pieces, slots, weight, sources, members, total):
    count, rows = len(pieces), pieces[0].shape[0]
    width, depth = weight.shape
    earlier = [] if held is None else [held]
    return pl.pallas_call(
        functools.partial(product_kernel, count, slots),
        in_specs=[pl.BlockSpec(memory_space=pltpu.SMEM)]
        + [pl.BlockSpec(memory_space=pltpu.VMEM)] * (count + 1)
        + [pl.BlockSpec(memory_space=HELD)] * len(earlier),
        out_specs=pl.BlockSpec(memory_space=HELD),
        out_shape=jax.ShapeDtypeStruct((members, total // members, width), jnp.bfloat16),
        scratch_shapes=[
            pltpu.VMEM((count, 2, members, STEP, width), jnp.bfloat16),
            pltpu.SemaphoreType.DMA((count, 2)),
        ],
        input_output_aliases={count + 2: 0} if earlier else {},
        compiler_params=pltpu.CompilerParams(vmem_limit_bytes=VMEM_BYTES),
        cost_estimate=pl.CostEstimate(
            flops=2 * count * rows * depth * width,
            bytes_accessed=2 * count * rows * (depth + width),
            transcendentals=0,
        ),
    )(sources, *pieces, weight, *earlier)


def gradient_kernel(half, held, sources, quantized_ref, *refs):
    out_ref = refs[-1]
    pieces = refs[1:-1] if held else refs[:-1]
    tokens = quantized_ref.shape[1]
    total = refs[0][...] if held else None
    slot = 0
    for first in range(0, len(pieces), 2):
        pair = pieces[first : first + 2]
        rows, block = [], []
        for piece_ref in pair:
            for k in range(piece_ref.shape[0] // (2 * tokens)):
                start = (2 * k + half) * tokens
                rows.append(piece_ref[start : start + tokens, :])
                block.append(quantized_ref[sources[slot]])
                slot += 1
        term = lax.dot_general(
            jnp.concatenate(block, axis=0),
            jnp.concatenate(rows, axis=0),
            (((0,), (0,)), ((), ())),
            preferred_element_type=jnp.float32,
        )
        total = term if total is None else total + term
    out_ref[...] = total


def gradient(held, half, sources, quantized, pieces):
    width, depth = quantized.shape[2], pieces[0].shape[1]
    rows = sum(piece.shape[0] for piece in pieces) // 2
    earlier = [] if held is None else [held]
    return pl.pallas_call(
        functools.partial(gradient_kernel, half, bool(earlier)),
        in_specs=[pl.BlockSpec(memory_space=pltpu.SMEM)]
        + [pl.BlockSpec(memory_space=pltpu.VMEM)] * (len(pieces) + 1 + len(earlier)),
        out_specs=pl.BlockSpec(memory_space=pltpu.VMEM),
        out_shape=jax.ShapeDtypeStruct((width, depth), jnp.float32),
        compiler_params=pltpu.CompilerParams(vmem_limit_bytes=2 * VMEM_BYTES),
        cost_estimate=pl.CostEstimate(
            flops=2 * rows * depth * width,
            bytes_accessed=2 * rows * (depth + width) + 4 * width * depth,
            transcendentals=0,
        ),
    )(sources, quantized, *earlier, *pieces)


def chip_core(x, y, core):
    return (x % SIDE * SIDE + y % SIDE) * 2 + core


def route(turn, sign):
    pairs = []
    for x in range(SIDE):
        for y in range(SIDE):
            for core in range(2):
                along = (sign, 0) if core == turn else (0, sign)
                pairs.append(
                    (chip_core(x, y, core), chip_core(x + along[0], y + along[1], core))
                )
    return pairs


def send(block, turn, sign):
    return lax.ppermute(block, "dp", route(turn, sign))


def other_core(block):
    return lax.ppermute(block, "dp", [(d, d ^ 1) for d in range(2 * SIDE * SIDE)])


def sources_table():
    table = []
    for x in range(SIDE):
        for y in range(SIDE):
            for core in range(2):
                found = []
                for outer in OFFSETS:
                    for sender in (core, 1 - core):
                        for inner in OFFSETS:
                            along = (inner, outer) if sender == 0 else (outer, inner)
                            found.append(chip_core(x + along[0], y + along[1], sender))
                table.append(found)
    return np.asarray(table, np.int32)


def finish_kernel(summed_ref, early_ref, late_ref, table_ref, out_ref, inner):
    devices, step, width = summed_ref.shape
    members, per_width = out_ref.shape[0], width // TABLE
    per_shard = devices // members
    slope = jnp.concatenate([early_ref[...], late_ref[...]], axis=1)
    upstream = (summed_ref[...].astype(jnp.float32) * slope).astype(jnp.bfloat16)
    upstream = upstream.reshape(devices * step, width)
    for c in range(per_width):
        inner[c] = jnp.dot(
            upstream[:, c * TABLE : (c + 1) * TABLE],
            table_ref[...],
            preferred_element_type=jnp.float32,
        )
    span = lambda d: slice(d * step, (d + 1) * step)
    for l in range(TABLE // LANES):
        lanes = slice(l * LANES, (l + 1) * LANES)
        for t in range(members):
            near = [(c, span(t * per_shard + k)) for k in range(per_shard) for c in range(per_width)]
            parts = butterfly([inner[c, rows, lanes] for c, rows in near])
            for (c, rows), part in zip(near, parts):
                inner[c, rows, lanes] = part
        for k in range(per_shard):
            for c in range(per_width):
                far = [span(t * per_shard + k) for t in range(members)]
                parts = butterfly([inner[c, rows, lanes] for rows in far])
                start = (k * per_width + c) * TABLE + l * LANES
                for t in range(members):
                    out_ref[t, :, start : start + LANES] = (parts[t] * NORM).astype(out_ref.dtype)


def finish(summed, slopes, table, members):
    devices, step, width = summed.shape
    return pl.pallas_call(
        finish_kernel,
        out_shape=jax.ShapeDtypeStruct((members, step, WIDTH // members), jnp.bfloat16),
        scratch_shapes=[pltpu.VMEM((width // TABLE, devices * step, TABLE), jnp.float32)],
        compiler_params=pltpu.CompilerParams(vmem_limit_bytes=VMEM_BYTES),
        cost_estimate=pl.CostEstimate(
            flops=2 * step * WIDTH * BLOCK, bytes_accessed=8 * step * WIDTH, transcendentals=0
        ),
    )(summed, *slopes, table)


def shards(activations, weight, grad_out):
    dp = lax.axis_size("dp")
    members = lax.axis_size("tensor")
    tokens, features = activations.shape
    width = weight.shape[0]
    place = lax.axis_index("tensor").astype(jnp.int32).reshape(1)
    sources = jnp.asarray(sources_table())[lax.axis_index("dp")]
    table = hadamard_table(TABLE)
    total = dp * tokens
    own, half = STEP // 2, tokens // 2
    activations = jnp.moveaxis(activations.reshape(members, 2, own, features), 1, 0)
    grad_out = jnp.moveaxis(grad_out.reshape(members, 2, own, -1), 1, 0).reshape(tokens, -1)
    activations, grad_out = lax.optimization_barrier((activations, grad_out))
    wide_rows = lax.all_gather(
        activations.reshape(tokens, features), "tensor", axis=0, tiled=False
    )

    def multiply(held, pieces, slot):
        slots = [slot + 2 * n for n in range(len(pieces))]
        return product(held, pieces, slots, weight, sources, members, total)

    below, above = send(grad_out, 0, 1), send(grad_out, 0, -1)
    top = jnp.concatenate([grad_out, below], axis=0)
    below_top, above_top = send(top, 1, 1), send(top, 1, -1)
    far = [send(below[:half], 0, 1), send(above[half:], 0, -1)]
    bottom = jnp.concatenate([above, *far], axis=0)
    below_bottom, above_bottom = send(bottom, 1, 1), send(bottom, 1, -1)
    far_top = send(below_top, 1, 1)
    near = [top, bottom]
    near_other = [other_core(block) for block in near]
    held = multiply(None, near + near_other, 0)
    below_bottom, above_bottom, held = lax.optimization_barrier(
        (below_bottom, above_bottom, held)
    )
    far_bottom = send(above_bottom, 1, -1)
    below, above = [below_top, below_bottom], [above_top, above_bottom]
    below_other = [other_core(block) for block in below]
    above_other = [other_core(block) for block in above]
    held = multiply(held, below + below_other, 8)
    held = multiply(held, above + above_other, 16)
    far_top, far_bottom, held = lax.optimization_barrier((far_top, far_bottom, held))
    far = [far_top, far_bottom]
    far_other = [other_core(block) for block in far]
    held = multiply(held, far, 24)
    partial_rows = multiply(held, far_other, 28)
    partial_rows, wide_rows = lax.optimization_barrier((partial_rows, wide_rows))
    summed = lax.psum_scatter(partial_rows, "tensor", scatter_dimension=0, tiled=False)
    late, late_slope = quantize_own(wide_rows, table, place, dp, width)
    q_own = lax.all_to_all(
        late.reshape(dp, own, width), "dp", split_axis=0, concat_axis=0, tiled=True
    )
    early, early_slope = quantize(wide_rows, table, place, dp, width)
    q_early = lax.all_to_all(early, "dp", split_axis=0, concat_axis=0, tiled=True)
    summed, q_early, q_own = lax.optimization_barrier((summed, q_early, q_own))
    homed = lax.all_to_all(
        summed.reshape(dp, STEP, width), "dp", split_axis=0, concat_axis=0, tiled=True
    )
    q_late = lax.all_gather(q_own, "tensor", axis=1, tiled=True)
    mixed = finish(homed, (early_slope, late_slope), table, members)
    grad_input = lax.all_to_all(mixed, "tensor", split_axis=0, concat_axis=0, tiled=True)
    arrived = near + near_other + below + below_other + above + above_other + far + far_other
    weight_sum = gradient(None, 0, sources, q_early, arrived)
    weight_sum = gradient(weight_sum, 1, sources, q_late, arrived)
    return (grad_input.reshape(tokens, features), weight_sum)


def solution(mesh):
    return jax.shard_map(
        shards,
        mesh=mesh,
        in_specs=(P("dp", "tensor"), P("dp", "tensor"), P("dp", "tensor")),
        out_specs=(P("dp", "tensor"), P("dp", "tensor")),
        check_vma=False,
    )
```

```python
import functools
import math

import jax
import jax.numpy as jnp
import numpy as np
from jax import lax
from jax.experimental import pallas as pl
from jax.experimental.pallas import tpu as pltpu
from jax.sharding import PartitionSpec as P

BLOCK = 1024
WIDTH = 16384
TABLE = 256
LANES = 128
VMEM_BYTES = 16 * 1024 * 1024
HALVES = [slice(start, start + LANES) for start in range(0, TABLE, LANES)]
NORM = 1.0 / math.sqrt(WIDTH)
SIDE = 4
STEP = 16
OFFSETS = (0, -1, 1, -2)

levels = 127.0
ripple = 0.5
epsilon = 1e-06


def hadamard_table(length):
    table = np.ones((1, 1), np.float32)
    while table.shape[0] < length:
        table = np.block([[table, table], [table, -table]])
    return jnp.asarray(table, jnp.bfloat16)


def fit(odd, terms):
    nodes = 0.5 * np.cos(np.pi * (np.arange(400) + 0.5) / 800.0)
    squares = nodes * nodes
    values = np.sin(2.0 * np.pi * nodes) / nodes if odd else np.cos(2.0 * np.pi * nodes)
    scaled = np.polynomial.chebyshev.Chebyshev.fit(squares, values, terms - 1, domain=[0.0, 0.25])
    return [float(c) for c in scaled.convert(kind=np.polynomial.Polynomial).coef]


SINE = fit(True, 6)
COSINE = fit(False, 7)


def horner(coefficients, square):
    total = jnp.full_like(square, coefficients[-1])
    for coefficient in coefficients[-2::-1]:
        total = total * square + coefficient
    return total


def butterfly(parts):
    distance = 1
    while distance < len(parts):
        mixed = list(parts)
        for low in range(len(parts)):
            if not low & distance:
                mixed[low] = parts[low] + parts[low | distance]
                mixed[low | distance] = parts[low] - parts[low | distance]
        parts = mixed
        distance *= 2
    return parts


def levels_of(largest):
    rows = largest.shape[0]
    peak = jnp.max(largest, axis=1, keepdims=True) * NORM
    scale = (peak + epsilon) / levels
    inverse = jnp.broadcast_to(NORM / scale, (rows, LANES))
    depth = jnp.broadcast_to((ripple / (2.0 * math.pi)) * scale, (rows, LANES))
    return inverse, depth


def remainder(value, inverse):
    turns = value * inverse
    return turns - jnp.round(turns)


def quantized_of(value, inverse, depth):
    rest = remainder(value, inverse)
    return value * NORM - depth * (rest * horner(SINE, rest * rest))


def slope_of(value, inverse):
    rest = remainder(value, inverse)
    return 1.0 - ripple * horner(COSINE, rest * rest)


def mix(rows, table, inner, spans):
    chunks = inner.shape[0]
    for c in range(chunks):
        inner[c] = jnp.dot(
            rows[:, c * TABLE : (c + 1) * TABLE], table, preferred_element_type=jnp.float32
        )
    return [mix_group(inner, group) for group in spans]


def mix_group(inner, spans):
    chunks = inner.shape[0]
    rows = spans[0].stop - spans[0].start
    for span in spans:
        for lanes in HALVES:
            parts = butterfly([inner[c, span, lanes] for c in range(chunks)])
            for c in range(chunks):
                inner[c, span, lanes] = parts[c]
    largest = jnp.zeros((rows, LANES), jnp.float32)
    for c in range(chunks):
        for lanes in HALVES:
            parts = butterfly([inner[c, span, lanes] for span in spans])
            for span, part in zip(spans, parts):
                inner[c, span, lanes] = part
                largest = jnp.maximum(largest, jnp.abs(part))
    return largest


def quantize_kernel(rows_ref, table_ref, quantized_ref, inner):
    members, count, features = rows_ref.shape
    width = quantized_ref.shape[2]
    chunks, per_shard, per_width = features // TABLE, features // width, width // TABLE
    groups = [
        [slice(t * count + g, t * count + g + STEP) for t in range(members)]
        for g in range(0, count, STEP)
    ]
    rows = rows_ref[...].reshape(members * count, features)
    found = mix(rows, table_ref[...], inner, groups)
    for g, (spans, largest) in enumerate(zip(groups, found)):
        inverse, depth = levels_of(largest)
        here = slice(g * STEP, (g + 1) * STEP)
        for t, span in enumerate(spans):
            for c in range(chunks):
                for l, lanes in enumerate(HALVES):
                    start = (c % per_width) * TABLE + l * LANES
                    block = t * per_shard + c // per_width
                    quantized_ref[block, here, start : start + LANES] = quantized_of(
                        inner[c, span, lanes], inverse, depth
                    ).astype(jnp.bfloat16)


def quantize(rows, table, dp, width):
    members, tokens, features = rows.shape
    tokens, count = tokens // 2, 2 * STEP
    return pl.pallas_call(
        quantize_kernel,
        grid=(tokens // count,),
        in_specs=[
            pl.BlockSpec((members, count, features), lambda i: (0, i, 0)),
            pl.BlockSpec((TABLE, TABLE), lambda i: (0, 0)),
        ],
        out_specs=pl.BlockSpec((dp, count, width), lambda i: (0, i, 0)),
        scratch_shapes=[pltpu.VMEM((features // TABLE, members * count, TABLE), jnp.float32)],
        out_shape=jax.ShapeDtypeStruct((dp, tokens, width), jnp.bfloat16),
        compiler_params=pltpu.CompilerParams(vmem_limit_bytes=VMEM_BYTES),
        cost_estimate=pl.CostEstimate(
            flops=2 * tokens * WIDTH * BLOCK, bytes_accessed=4 * tokens * WIDTH, transcendentals=0
        ),
    )(rows, table)


def quantize_own_kernel(place, mine_ref, spread_ref, table_ref, quantized_ref, slope_ref, inner):
    devices, _, width = slope_ref.shape
    own = quantized_ref.shape[0] // devices
    members, _, features = mine_ref.shape
    per_shard, per_width = devices // members, width // TABLE
    spans = [slice(t * STEP, (t + 1) * STEP) for t in range(members)]

    def blocks():
        for block in range(devices):
            for k in range(per_width):
                for l, lanes in enumerate(HALVES):
                    t, c = block // per_shard, block % per_shard * per_width + k
                    start = k * TABLE + l * LANES
                    yield block, t, c, lanes, slice(start, start + LANES)

    flat = lambda ref: ref[...].reshape(members * STEP, features)
    (largest,) = mix(flat(mine_ref), table_ref[...], inner, [spans])
    inverse, _ = levels_of(largest)
    for block, t, c, lanes, columns in blocks():
        slope_ref[block, :, columns] = slope_of(inner[c, spans[t], lanes], inverse)
    (largest,) = mix(flat(spread_ref), table_ref[...], inner, [spans])
    upper = place[0] % 2 == 1
    inverse, depth = levels_of(jnp.where(upper, largest[own:], largest[:own]))
    shift = pl.multiple_of(place[0] % 2 * own, own)
    held = {}
    for block, t, c, lanes, columns in blocks():
        rows = pl.ds(pl.multiple_of(t * STEP + shift, own), own)
        value = quantized_of(inner[c, rows, lanes], inverse, depth)
        if block % 2 == 0:
            held[columns.start] = value
        else:
            quantized_ref[(block - 1) * own : (block + 1) * own, columns] = jnp.concatenate(
                [held[columns.start], value], axis=0
            ).astype(jnp.bfloat16)


def quantize_own(rows, table, place, dp, width):
    members, tokens, features = rows.shape
    own, half = STEP // 2, tokens // 2 // STEP
    shape = (members, STEP, features)
    return pl.pallas_call(
        quantize_own_kernel,
        grid_spec=pltpu.PrefetchScalarGridSpec(
            num_scalar_prefetch=1,
            grid=(1,),
            in_specs=[
                pl.BlockSpec(shape, lambda i, place: (0, place[0], 0)),
                pl.BlockSpec(shape, lambda i, place: (0, half + place[0] // 2, 0)),
                pl.BlockSpec((TABLE, TABLE), lambda i, place: (0, 0)),
            ],
            out_specs=[
                pl.BlockSpec((dp * own, width), lambda i, place: (0, 0)),
                pl.BlockSpec((dp, STEP, width), lambda i, place: (0, 0, 0)),
            ],
            scratch_shapes=[pltpu.VMEM((features // TABLE, members * STEP, TABLE), jnp.float32)],
        ),
        out_shape=[
            jax.ShapeDtypeStruct((dp * own, width), jnp.bfloat16),
            jax.ShapeDtypeStruct((dp, STEP, width), jnp.float32),
        ],
        compiler_params=pltpu.CompilerParams(vmem_limit_bytes=VMEM_BYTES),
        cost_estimate=pl.CostEstimate(
            flops=2 * STEP * WIDTH * BLOCK, bytes_accessed=8 * STEP * WIDTH, transcendentals=0
        ),
    )(place, rows, rows, table)


def product_kernel(count, slots, sources, *refs):
    pieces, weight_ref = refs[: 2 * count], refs[2 * count]
    out_ref, early_ref, late_ref, results, out_sems, row_sems = refs[-6:]
    members, tokens = out_ref.shape[0], out_ref.shape[0] * STEP
    half = early_ref.shape[1]
    stores = []
    for n in range(count):
        for k in range(4):
            piece, first = pieces[2 * n + k // 2], k % 2 * tokens
            source = sources[slots[n] + k]
            for h, ref in enumerate((early_ref, late_ref)):
                stores.append(
                    pltpu.make_async_copy(
                        piece.at[pl.ds(first + h * half, half), :],
                        ref.at[source],
                        row_sems.at[n, k, h],
                    )
                )
                stores[-1].start()
    for n in range(count):
        result = lax.dot_general(
            jnp.concatenate([pieces[2 * n][...], pieces[2 * n + 1][...]], axis=0),
            weight_ref[...],
            (((1,), (1,)), ((), ())),
            preferred_element_type=jnp.float32,
        ).astype(results.dtype)
        for k in range(4):
            for t in range(members):
                start = k * tokens + t * STEP
                results[n, k, t] = result[start : start + STEP]
            place = pl.multiple_of(sources[slots[n] + k] * STEP, STEP)
            stores.append(
                pltpu.make_async_copy(
                    results.at[n, k], out_ref.at[:, pl.ds(place, STEP), :], out_sems.at[n, k]
                )
            )
            stores[-1].start()
    for store in stores:
        store.wait()


def product(held, pieces, slots, weight, sources, members, dp):
    count, rows = len(pieces) // 2, pieces[0].shape[0]
    width, depth = weight.shape
    half = members * STEP // 2
    shapes = [(members, dp * STEP, width), (dp, half, depth), (dp, half, depth)]
    earlier = [] if held is None else list(held)
    return pl.pallas_call(
        functools.partial(product_kernel, count, slots),
        in_specs=[pl.BlockSpec(memory_space=pltpu.SMEM)]
        + [pl.BlockSpec(memory_space=pltpu.VMEM)] * (2 * count + 1)
        + [pl.BlockSpec(memory_space=pltpu.HBM)] * len(earlier),
        out_specs=[pl.BlockSpec(memory_space=pltpu.HBM)] * 3,
        out_shape=[jax.ShapeDtypeStruct(shape, jnp.bfloat16) for shape in shapes],
        scratch_shapes=[
            pltpu.VMEM((count, 4, members, STEP, width), jnp.bfloat16),
            pltpu.SemaphoreType.DMA((count, 4)),
            pltpu.SemaphoreType.DMA((count, 4, 2)),
        ],
        input_output_aliases={2 * count + 2 + n: n for n in range(len(earlier))},
        compiler_params=pltpu.CompilerParams(vmem_limit_bytes=VMEM_BYTES),
        cost_estimate=pl.CostEstimate(
            flops=4 * count * rows * depth * width,
            bytes_accessed=4 * count * rows * (depth + width),
            transcendentals=0,
        ),
    )(sources, *pieces, weight, *earlier)


def gradient(quantized, rows):
    return lax.dot_general(
        quantized.reshape(-1, quantized.shape[2]),
        rows.reshape(-1, rows.shape[2]),
        (((0,), (0,)), ((), ())),
        preferred_element_type=jnp.float32,
    )


def chip_core(x, y, core):
    return (x % SIDE * SIDE + y % SIDE) * 2 + core


def route(turn, sign):
    pairs = []
    for x in range(SIDE):
        for y in range(SIDE):
            for core in range(2):
                along = (sign, 0) if core == turn else (0, sign)
                pairs.append(
                    (chip_core(x, y, core), chip_core(x + along[0], y + along[1], core))
                )
    return pairs


def send(block, turn, sign):
    return lax.ppermute(block, "dp", route(turn, sign))


def other_core(block):
    return lax.ppermute(block, "dp", [(d, d ^ 1) for d in range(2 * SIDE * SIDE)])


def sources_table():
    table = []
    for x in range(SIDE):
        for y in range(SIDE):
            for core in range(2):
                found = []
                for outer in OFFSETS:
                    for sender in (core, 1 - core):
                        for inner in OFFSETS:
                            along = (inner, outer) if sender == 0 else (outer, inner)
                            found.append(chip_core(x + along[0], y + along[1], sender))
                table.append(found)
    return np.asarray(table, np.int32)


def finish_kernel(summed_ref, slope_ref, table_ref, out_ref, inner):
    devices, step, width = summed_ref.shape
    members, per_width = out_ref.shape[0], width // TABLE
    per_shard = devices // members
    upstream = (summed_ref[...].astype(jnp.float32) * slope_ref[...]).astype(jnp.bfloat16)
    upstream = upstream.reshape(devices * step, width)
    for c in range(per_width):
        inner[c] = jnp.dot(
            upstream[:, c * TABLE : (c + 1) * TABLE],
            table_ref[...],
            preferred_element_type=jnp.float32,
        )
    span = lambda d: slice(d * step, (d + 1) * step)
    for l in range(TABLE // LANES):
        lanes = slice(l * LANES, (l + 1) * LANES)
        for t in range(members):
            near = [(c, span(t * per_shard + k)) for k in range(per_shard) for c in range(per_width)]
            parts = butterfly([inner[c, rows, lanes] for c, rows in near])
            for (c, rows), part in zip(near, parts):
                inner[c, rows, lanes] = part
        for k in range(per_shard):
            for c in range(per_width):
                far = [span(t * per_shard + k) for t in range(members)]
                parts = butterfly([inner[c, rows, lanes] for rows in far])
                start = (k * per_width + c) * TABLE + l * LANES
                for t in range(members):
                    out_ref[t, :, start : start + LANES] = (parts[t] * NORM).astype(out_ref.dtype)


def finish(summed, slope, table, members):
    devices, step, width = summed.shape
    return pl.pallas_call(
        finish_kernel,
        out_shape=jax.ShapeDtypeStruct((members, step, WIDTH // members), jnp.bfloat16),
        scratch_shapes=[pltpu.VMEM((width // TABLE, devices * step, TABLE), jnp.float32)],
        compiler_params=pltpu.CompilerParams(vmem_limit_bytes=VMEM_BYTES),
        cost_estimate=pl.CostEstimate(
            flops=2 * step * WIDTH * BLOCK, bytes_accessed=8 * step * WIDTH, transcendentals=0
        ),
    )(summed, slope, table)


def shards(activations, weight, grad_out):
    dp = lax.axis_size("dp")
    members = lax.axis_size("tensor")
    tokens, features = activations.shape
    width = weight.shape[0]
    place = lax.axis_index("tensor").astype(jnp.int32).reshape(1)
    sources = jnp.asarray(sources_table())[lax.axis_index("dp")]
    table = hadamard_table(TABLE)
    own, half = STEP // 2, tokens // 2
    wide_rows = lax.all_gather(activations, "tensor", axis=0, tiled=False)

    def multiply(held, pieces, slot):
        slots = [slot + 4 * n for n in range(len(pieces) // 2)]
        return product(held, pieces, slots, weight, sources, members, dp)

    below, above = send(grad_out, 0, 1), send(grad_out, 0, -1)
    top = jnp.concatenate([grad_out, below], axis=0)
    below_top, above_top = send(top, 1, 1), send(top, 1, -1)
    far = [send(below[:half], 0, 1), send(above[half:], 0, -1)]
    bottom = jnp.concatenate([above, *far], axis=0)
    below_bottom, above_bottom = send(bottom, 1, 1), send(bottom, 1, -1)
    far_top = send(below_top, 1, 1)
    near = [top, bottom]
    near_other = [other_core(block) for block in near]
    held = multiply(None, near + near_other, 0)
    below_bottom, above_bottom, held = lax.optimization_barrier(
        (below_bottom, above_bottom, held)
    )
    far_bottom = send(above_bottom, 1, -1)
    below, above = [below_top, below_bottom], [above_top, above_bottom]
    below_other = [other_core(block) for block in below]
    above_other = [other_core(block) for block in above]
    held = multiply(held, below + below_other, 8)
    held = multiply(held, above + above_other, 16)
    far_top, far_bottom, held = lax.optimization_barrier((far_top, far_bottom, held))
    far = [far_top, far_bottom]
    far_other = [other_core(block) for block in far]
    held = multiply(held, far, 24)
    partial_rows, rows_early, rows_late = multiply(held, far_other, 28)
    partial_rows, wide_rows = lax.optimization_barrier((partial_rows, wide_rows))
    summed = lax.psum_scatter(partial_rows, "tensor", scatter_dimension=0, tiled=False)
    late, slope = quantize_own(wide_rows, table, place, dp, width)
    q_own = lax.all_to_all(
        late.reshape(dp, own, width), "dp", split_axis=0, concat_axis=0, tiled=True
    )
    early = quantize(wide_rows, table, dp, width)
    q_early = lax.all_to_all(early, "dp", split_axis=0, concat_axis=0, tiled=True)
    summed, q_early, q_own = lax.optimization_barrier((summed, q_early, q_own))
    homed = lax.all_to_all(
        summed.reshape(dp, STEP, width), "dp", split_axis=0, concat_axis=0, tiled=True
    )
    q_late = lax.all_gather(q_own, "tensor", axis=1, tiled=True)
    mixed = finish(homed, slope, table, members)
    grad_input = lax.all_to_all(mixed, "tensor", split_axis=0, concat_axis=0, tiled=True)
    early_sum = gradient(q_early, rows_early)
    early_sum, q_late = lax.optimization_barrier((early_sum, q_late))
    weight_sum = early_sum + gradient(q_late, rows_late)
    return (grad_input.reshape(tokens, features), weight_sum)


def solution(mesh):
    return jax.shard_map(
        shards,
        mesh=mesh,
        in_specs=(P("dp", "tensor"), P("dp", "tensor"), P("dp", "tensor")),
        out_specs=(P("dp", "tensor"), P("dp", "tensor")),
        check_vma=False,
    )
```

```python
import math

import jax
import jax.numpy as jnp
import numpy as np
from jax import lax
from jax.experimental import pallas as pl
from jax.experimental.pallas import tpu as pltpu
from jax.sharding import PartitionSpec as P

BLOCK = 1024
WIDTH = 16384
TABLE = 256
LANES = 128
VMEM_BYTES = 60 * 1024 * 1024
LITTLE_VMEM = 16 * 1024 * 1024
NORM = 1.0 / math.sqrt(WIDTH)
SIDE = 4
STEP = 16
OFFSETS = (0, -1, 1, -2)

levels = 127.0
ripple = 0.5
epsilon = 1e-06


def hadamard_table(length):
    table = np.ones((1, 1), np.float32)
    while table.shape[0] < length:
        table = np.block([[table, table], [table, -table]])
    return jnp.asarray(table, jnp.bfloat16)


def fit(odd, terms):
    nodes = 0.5 * np.cos(np.pi * (np.arange(400) + 0.5) / 800.0)
    squares = nodes * nodes
    values = np.sin(2.0 * np.pi * nodes) / nodes if odd else np.cos(2.0 * np.pi * nodes)
    scaled = np.polynomial.chebyshev.Chebyshev.fit(squares, values, terms - 1, domain=[0.0, 0.25])
    return [float(c) for c in scaled.convert(kind=np.polynomial.Polynomial).coef]


SINE = fit(True, 6)
COSINE = fit(False, 7)


def horner(coefficients, square):
    total = jnp.full_like(square, coefficients[-1])
    for coefficient in coefficients[-2::-1]:
        total = total * square + coefficient
    return total


def butterfly(parts):
    distance = 1
    while distance < len(parts):
        mixed = list(parts)
        for low in range(len(parts)):
            if not low & distance:
                mixed[low] = parts[low] + parts[low | distance]
                mixed[low | distance] = parts[low] - parts[low | distance]
        parts = mixed
        distance *= 2
    return parts


def quantize_kernel(place, rows_ref, table_ref, quantized_ref, slope_ref, inner, mixed):
    members, count, features = rows_ref.shape
    step, width = slope_ref.shape[1:]
    chunks, per_shard, per_width = features // TABLE, features // width, width // TABLE
    rows = rows_ref[...].reshape(members * count, features)
    for c in range(chunks):
        inner[c] = jnp.dot(
            rows[:, c * TABLE : (c + 1) * TABLE],
            table_ref[...],
            preferred_element_type=jnp.float32,
        )
    halves = [slice(l * LANES, (l + 1) * LANES) for l in range(TABLE // LANES)]
    for group in range(count // step):
        spans = [
            slice(t * count + group * step, t * count + (group + 1) * step)
            for t in range(members)
        ]
        here = slice(group * step, (group + 1) * step)
        for span in spans:
            for lanes in halves:
                parts = butterfly([inner[c, span, lanes] for c in range(chunks)])
                for c in range(chunks):
                    inner[c, span, lanes] = parts[c]
        largest = jnp.zeros((step, LANES), jnp.float32)
        for c in range(chunks):
            for lanes in halves:
                parts = butterfly([inner[c, span, lanes] for span in spans])
                for span, part in zip(spans, parts):
                    mixed[c, span, lanes] = part
                    largest = jnp.maximum(largest, jnp.abs(part))
        peak = jnp.max(largest, axis=1, keepdims=True) * NORM
        scale = (peak + epsilon) / levels
        inverse = jnp.broadcast_to(NORM / scale, (step, LANES))
        depth = jnp.broadcast_to((ripple / (2.0 * math.pi)) * scale, (step, LANES))

        def remainder(value):
            turns = value * inverse
            return turns - jnp.round(turns)

        def places():
            for t, span in enumerate(spans):
                for c in range(chunks):
                    for l, lanes in enumerate(halves):
                        start = (c % per_width) * TABLE + l * LANES
                        yield t * per_shard + c // per_width, start, mixed[c, span, lanes]

        for block, start, value in places():
            rest = remainder(value)
            sine = rest * horner(SINE, rest * rest)
            quantized_ref[block, here, start : start + LANES] = (
                value * NORM - depth * sine
            ).astype(jnp.bfloat16)

        @pl.when(pl.program_id(0) * (count // step) + group == place[0])
        def _():
            for block, start, value in places():
                rest = remainder(value)
                slope_ref[block, :, start : start + LANES] = 1.0 - ripple * horner(
                    COSINE, rest * rest
                )


def quantize(rows, table, place, dp, width):
    members, tokens, features = rows.shape
    step = tokens // members
    count = 2 * step
    return pl.pallas_call(
        quantize_kernel,
        grid_spec=pltpu.PrefetchScalarGridSpec(
            num_scalar_prefetch=1,
            grid=(tokens // count,),
            in_specs=[
                pl.BlockSpec((members, count, features), lambda i, place: (0, i, 0)),
                pl.BlockSpec((TABLE, TABLE), lambda i, place: (0, 0)),
            ],
            out_specs=[
                pl.BlockSpec((dp, count, width), lambda i, place: (0, i, 0)),
                pl.BlockSpec((dp, step, width), lambda i, place: (0, 0, 0)),
            ],
            scratch_shapes=[
                pltpu.VMEM((features // TABLE, members * count, TABLE), jnp.float32),
                pltpu.VMEM((features // TABLE, members * count, TABLE), jnp.float32),
            ],
        ),
        out_shape=[
            jax.ShapeDtypeStruct((dp, tokens, width), jnp.bfloat16),
            jax.ShapeDtypeStruct((dp, step, width), jnp.float32),
        ],
        compiler_params=pltpu.CompilerParams(vmem_limit_bytes=VMEM_BYTES),
        cost_estimate=pl.CostEstimate(
            flops=2 * tokens * WIDTH * BLOCK, bytes_accessed=4 * tokens * WIDTH, transcendentals=0
        ),
    )(place, rows, table)


def product_kernel(*refs):
    weight_ref, out_ref = refs[-2:]
    pieces = [ref for ref in refs[:-2] if len(ref.shape) == 2]
    members, step = out_ref.shape[0], STEP
    done = 0
    for piece_ref in pieces:
        rows, depth = piece_ref.shape
        result = lax.dot_general(
            piece_ref[...],
            weight_ref[...],
            (((1,), (1,)), ((), ())),
            preferred_element_type=jnp.float32,
        ).astype(out_ref.dtype)
        for k in range(rows // (members * step)):
            for t in range(members):
                start = (k * members + t) * step
                out_ref[t, done * step : (done + 1) * step, :] = result[start : start + step]
            done += 1


def product(held, pieces, weight, position, members, total):
    rows = sum(piece.shape[0] for piece in pieces)
    width, depth = weight.shape
    whole = [pl.BlockSpec(memory_space=pltpu.VMEM)] * (len(pieces) + 1)
    earlier = [] if held is None else [held]
    return pl.pallas_call(
        product_kernel,
        grid=(1,),
        in_specs=[pl.BlockSpec(memory_space=pl.ANY)] * len(earlier) + whole,
        out_specs=pl.BlockSpec((members, rows // members, width), lambda i: (0, position, 0)),
        out_shape=jax.ShapeDtypeStruct((members, total // members, width), jnp.bfloat16),
        input_output_aliases={0: 0} if earlier else {},
        compiler_params=pltpu.CompilerParams(vmem_limit_bytes=LITTLE_VMEM),
        cost_estimate=pl.CostEstimate(
            flops=2 * rows * depth * width,
            bytes_accessed=2 * rows * (depth + width),
            transcendentals=0,
        ),
    )(*earlier, *pieces, weight)


def order_kernel(sources, rows_ref, out_ref):
    for slot in range(rows_ref.shape[0]):
        out_ref[sources[slot]] = rows_ref[slot]


def order(rows, sources):
    return pl.pallas_call(
        order_kernel,
        in_specs=[
            pl.BlockSpec(memory_space=pltpu.SMEM),
            pl.BlockSpec(memory_space=pltpu.VMEM),
        ],
        out_specs=pl.BlockSpec(memory_space=pltpu.VMEM),
        out_shape=jax.ShapeDtypeStruct(rows.shape, rows.dtype),
        compiler_params=pltpu.CompilerParams(vmem_limit_bytes=VMEM_BYTES),
    )(sources, rows)


def gradient_kernel(sources, quantized_ref, *refs):
    out_ref = refs[-1]
    pieces = refs[:-1]
    tokens = quantized_ref.shape[1]
    slot = 0
    for number, piece_ref in enumerate(pieces):
        count = piece_ref.shape[0] // tokens
        block = jnp.concatenate(
            [quantized_ref[sources[slot + k]] for k in range(count)], axis=0
        )
        slot += count
        term = lax.dot_general(
            block, piece_ref[...], (((0,), (0,)), ((), ())), preferred_element_type=jnp.float32
        )
        out_ref[...] = term if number == 0 else out_ref[...] + term


def gradient(sources, quantized, pieces):
    width, depth = quantized.shape[2], pieces[0].shape[1]
    rows = sum(piece.shape[0] for piece in pieces)
    return pl.pallas_call(
        gradient_kernel,
        in_specs=[pl.BlockSpec(memory_space=pltpu.SMEM)]
        + [pl.BlockSpec(memory_space=pltpu.VMEM)] * (len(pieces) + 1),
        out_specs=pl.BlockSpec(memory_space=pltpu.VMEM),
        out_shape=jax.ShapeDtypeStruct((width, depth), jnp.float32),
        compiler_params=pltpu.CompilerParams(vmem_limit_bytes=VMEM_BYTES),
        cost_estimate=pl.CostEstimate(
            flops=2 * rows * depth * width,
            bytes_accessed=2 * rows * (depth + width) + 4 * width * depth,
            transcendentals=0,
        ),
    )(sources, quantized, *pieces)


def chip_core(x, y, core):
    return (x % SIDE * SIDE + y % SIDE) * 2 + core


def route(turn, sign):
    pairs = []
    for x in range(SIDE):
        for y in range(SIDE):
            for core in range(2):
                along = (sign, 0) if core == turn else (0, sign)
                pairs.append(
                    (chip_core(x, y, core), chip_core(x + along[0], y + along[1], core))
                )
    return pairs


def send(block, turn, sign):
    return lax.ppermute(block, "dp", route(turn, sign))


def other_core(block):
    return lax.ppermute(block, "dp", [(d, d ^ 1) for d in range(2 * SIDE * SIDE)])


def sources_table():
    table = []
    for x in range(SIDE):
        for y in range(SIDE):
            for core in range(2):
                found = []
                for outer in OFFSETS:
                    for sender in (core, 1 - core):
                        for inner in OFFSETS:
                            along = (inner, outer) if sender == 0 else (outer, inner)
                            found.append(chip_core(x + along[0], y + along[1], sender))
                table.append(found)
    return np.asarray(table, np.int32)


def finish_kernel(summed_ref, slope_ref, table_ref, out_ref, inner):
    devices, step, width = summed_ref.shape
    members, per_width = out_ref.shape[0], width // TABLE
    per_shard = devices // members
    upstream = (summed_ref[...].astype(jnp.float32) * slope_ref[...]).astype(jnp.bfloat16)
    upstream = upstream.reshape(devices * step, width)
    for c in range(per_width):
        inner[c] = jnp.dot(
            upstream[:, c * TABLE : (c + 1) * TABLE],
            table_ref[...],
            preferred_element_type=jnp.float32,
        )
    span = lambda d: slice(d * step, (d + 1) * step)
    for l in range(TABLE // LANES):
        lanes = slice(l * LANES, (l + 1) * LANES)
        for t in range(members):
            near = [(c, span(t * per_shard + k)) for k in range(per_shard) for c in range(per_width)]
            parts = butterfly([inner[c, rows, lanes] for c, rows in near])
            for (c, rows), part in zip(near, parts):
                inner[c, rows, lanes] = part
        for k in range(per_shard):
            for c in range(per_width):
                far = [span(t * per_shard + k) for t in range(members)]
                parts = butterfly([inner[c, rows, lanes] for rows in far])
                start = (k * per_width + c) * TABLE + l * LANES
                for t in range(members):
                    out_ref[t, :, start : start + LANES] = (parts[t] * NORM).astype(out_ref.dtype)


def finish(summed, slope, table, members):
    devices, step, width = summed.shape
    return pl.pallas_call(
        finish_kernel,
        out_shape=jax.ShapeDtypeStruct((members, step, WIDTH // members), jnp.bfloat16),
        scratch_shapes=[pltpu.VMEM((width // TABLE, devices * step, TABLE), jnp.float32)],
        compiler_params=pltpu.CompilerParams(vmem_limit_bytes=LITTLE_VMEM),
        cost_estimate=pl.CostEstimate(
            flops=2 * step * WIDTH * BLOCK, bytes_accessed=8 * step * WIDTH, transcendentals=0
        ),
    )(summed, slope, table)


def shards(activations, weight, grad_out):
    dp = lax.axis_size("dp")
    members = lax.axis_size("tensor")
    tokens, features = activations.shape
    width = weight.shape[0]
    place = lax.axis_index("tensor").astype(jnp.int32).reshape(1)
    sources = jnp.asarray(sources_table())[lax.axis_index("dp")]
    table = hadamard_table(TABLE)
    wide_rows = lax.all_gather(activations, "tensor", axis=0, tiled=False)
    total = dp * tokens

    def multiply(held, pieces, position):
        return product(held, pieces, weight, position, members, total)

    half = tokens // 2
    below, above = send(grad_out, 0, 1), send(grad_out, 0, -1)
    top = jnp.concatenate([grad_out, below], axis=0)
    below_top, above_top = send(top, 1, 1), send(top, 1, -1)
    far = [send(below[:half], 0, 1), send(above[half:], 0, -1)]
    bottom = jnp.concatenate([above, *far], axis=0)
    below_bottom, above_bottom = send(bottom, 1, 1), send(bottom, 1, -1)
    far_top = send(below_top, 1, 1)
    near = [top, bottom]
    near_other = [other_core(block) for block in near]
    held = multiply(None, near + near_other, 0)
    below_bottom, above_bottom, held = lax.optimization_barrier(
        (below_bottom, above_bottom, held)
    )
    far_bottom = send(above_bottom, 1, -1)
    below, above = [below_top, below_bottom], [above_top, above_bottom]
    below_other = [other_core(block) for block in below]
    above_other = [other_core(block) for block in above]
    held = multiply(held, below + below_other, 1)
    held = multiply(held, above + above_other, 2)
    far_top, far_bottom, held = lax.optimization_barrier((far_top, far_bottom, held))
    far = [far_top, far_bottom]
    far_other = [other_core(block) for block in far]
    held = multiply(held, far, 6)
    partial_rows = multiply(held, far_other, 7)
    partial_rows, wide_rows = lax.optimization_barrier((partial_rows, wide_rows))
    summed = lax.psum_scatter(partial_rows, "tensor", scatter_dimension=0, tiled=False)
    quantized, slope = quantize(wide_rows, table, place, dp, width)
    q_block = lax.all_to_all(quantized, "dp", split_axis=0, concat_axis=0, tiled=True)
    ordered = order(summed.reshape(dp, tokens // members, width), sources)
    ordered, q_block = lax.optimization_barrier((ordered, q_block))
    homed = lax.all_to_all(ordered, "dp", split_axis=0, concat_axis=0, tiled=True)
    mixed = finish(homed, slope, table, members)
    grad_input = lax.all_to_all(mixed, "tensor", split_axis=0, concat_axis=0, tiled=True)
    arrived = near + near_other + below + below_other + above + above_other + far + far_other
    weight_sum = gradient(sources, q_block, arrived)
    return (grad_input.reshape(tokens, features), weight_sum)


def solution(mesh):
    return jax.shard_map(
        shards,
        mesh=mesh,
        in_specs=(P("dp", "tensor"), P("dp", "tensor"), P("dp", "tensor")),
        out_specs=(P("dp", "tensor"), P("dp", "tensor")),
        check_vma=False,
    )
```

```python
import functools
import math

import jax
import jax.numpy as jnp
import numpy as np
from jax import lax
from jax.experimental import pallas as pl
from jax.experimental.pallas import tpu as pltpu
from jax.sharding import PartitionSpec as P

BLOCK = 1024
WIDTH = 16384
TABLE = 256
LANES = 128
VMEM_BYTES = 60 * 1024 * 1024
LITTLE_VMEM = 16 * 1024 * 1024
HALVES = [slice(start, start + LANES) for start in range(0, TABLE, LANES)]
NORM = 1.0 / math.sqrt(WIDTH)
SIDE = 4
STEP = 16
OFFSETS = (0, -1, 1, -2)

levels = 127.0
ripple = 0.5
epsilon = 1e-06


def hadamard_table(length):
    table = np.ones((1, 1), np.float32)
    while table.shape[0] < length:
        table = np.block([[table, table], [table, -table]])
    return jnp.asarray(table, jnp.bfloat16)


def fit(odd, terms):
    nodes = 0.5 * np.cos(np.pi * (np.arange(400) + 0.5) / 800.0)
    squares = nodes * nodes
    values = np.sin(2.0 * np.pi * nodes) / nodes if odd else np.cos(2.0 * np.pi * nodes)
    scaled = np.polynomial.chebyshev.Chebyshev.fit(squares, values, terms - 1, domain=[0.0, 0.25])
    return [float(c) for c in scaled.convert(kind=np.polynomial.Polynomial).coef]


SINE = fit(True, 6)
COSINE = fit(False, 7)


def horner(coefficients, square):
    total = jnp.full_like(square, coefficients[-1])
    for coefficient in coefficients[-2::-1]:
        total = total * square + coefficient
    return total


def butterfly(parts):
    distance = 1
    while distance < len(parts):
        mixed = list(parts)
        for low in range(len(parts)):
            if not low & distance:
                mixed[low] = parts[low] + parts[low | distance]
                mixed[low | distance] = parts[low] - parts[low | distance]
        parts = mixed
        distance *= 2
    return parts


def levels_of(largest):
    rows = largest.shape[0]
    peak = jnp.max(largest, axis=1, keepdims=True) * NORM
    scale = (peak + epsilon) / levels
    inverse = jnp.broadcast_to(NORM / scale, (rows, LANES))
    depth = jnp.broadcast_to((ripple / (2.0 * math.pi)) * scale, (rows, LANES))
    return inverse, depth


def remainder(value, inverse):
    turns = value * inverse
    return turns - jnp.round(turns)


def quantized_of(value, inverse, depth):
    rest = remainder(value, inverse)
    return value * NORM - depth * (rest * horner(SINE, rest * rest))


def slope_of(value, inverse):
    rest = remainder(value, inverse)
    return 1.0 - ripple * horner(COSINE, rest * rest)


def mix(rows, table, inner, spans):
    chunks = inner.shape[0]
    for c in range(chunks):
        inner[c] = jnp.dot(
            rows[:, c * TABLE : (c + 1) * TABLE], table, preferred_element_type=jnp.float32
        )
    return [mix_group(inner, group) for group in spans]


def mix_group(inner, spans):
    chunks = inner.shape[0]
    rows = spans[0].stop - spans[0].start
    for span in spans:
        for lanes in HALVES:
            parts = butterfly([inner[c, span, lanes] for c in range(chunks)])
            for c in range(chunks):
                inner[c, span, lanes] = parts[c]
    largest = jnp.zeros((rows, LANES), jnp.float32)
    for c in range(chunks):
        for lanes in HALVES:
            parts = butterfly([inner[c, span, lanes] for span in spans])
            for span, part in zip(spans, parts):
                inner[c, span, lanes] = part
                largest = jnp.maximum(largest, jnp.abs(part))
    return largest


def quantize_kernel(rows_ref, table_ref, quantized_ref, inner):
    members, count, features = rows_ref.shape
    width = quantized_ref.shape[2]
    chunks, per_shard, per_width = features // TABLE, features // width, width // TABLE
    groups = [
        [slice(t * count + g, t * count + g + STEP) for t in range(members)]
        for g in range(0, count, STEP)
    ]
    rows = rows_ref[...].reshape(members * count, features)
    found = mix(rows, table_ref[...], inner, groups)
    for g, (spans, largest) in enumerate(zip(groups, found)):
        inverse, depth = levels_of(largest)
        here = slice(g * STEP, (g + 1) * STEP)
        for t, span in enumerate(spans):
            for c in range(chunks):
                for l, lanes in enumerate(HALVES):
                    start = (c % per_width) * TABLE + l * LANES
                    block = t * per_shard + c // per_width
                    quantized_ref[block, here, start : start + LANES] = quantized_of(
                        inner[c, span, lanes], inverse, depth
                    ).astype(jnp.bfloat16)


def quantize(rows, table, dp, width):
    members, tokens, features = rows.shape
    count = 2 * STEP
    return pl.pallas_call(
        quantize_kernel,
        grid=(tokens // count,),
        in_specs=[
            pl.BlockSpec((members, count, features), lambda i: (0, i, 0)),
            pl.BlockSpec((TABLE, TABLE), lambda i: (0, 0)),
        ],
        out_specs=pl.BlockSpec((dp, count, width), lambda i: (0, i, 0)),
        scratch_shapes=[pltpu.VMEM((features // TABLE, members * count, TABLE), jnp.float32)],
        out_shape=jax.ShapeDtypeStruct((dp, tokens, width), jnp.bfloat16),
        compiler_params=pltpu.CompilerParams(vmem_limit_bytes=VMEM_BYTES),
        cost_estimate=pl.CostEstimate(
            flops=2 * tokens * WIDTH * BLOCK, bytes_accessed=4 * tokens * WIDTH, transcendentals=0
        ),
    )(rows, table)


def slope_kernel(place, rows_ref, table_ref, slope_ref, inner):
    members, _, features = rows_ref.shape
    devices, _, width = slope_ref.shape
    per_shard, per_width = devices // members, width // TABLE
    spans = [slice(t * STEP, (t + 1) * STEP) for t in range(members)]
    rows = rows_ref[...].reshape(members * STEP, features)
    (largest,) = mix(rows, table_ref[...], inner, [spans])
    inverse, _ = levels_of(largest)
    for block in range(devices):
        for k in range(per_width):
            for l, lanes in enumerate(HALVES):
                c = block % per_shard * per_width + k
                start = k * TABLE + l * LANES
                slope_ref[block, :, start : start + LANES] = slope_of(
                    inner[c, spans[block // per_shard], lanes], inverse
                )


def slopes(rows, table, place, dp, width):
    members, tokens, features = rows.shape
    return pl.pallas_call(
        slope_kernel,
        grid_spec=pltpu.PrefetchScalarGridSpec(
            num_scalar_prefetch=1,
            grid=(1,),
            in_specs=[
                pl.BlockSpec((members, STEP, features), lambda i, place: (0, place[0], 0)),
                pl.BlockSpec((TABLE, TABLE), lambda i, place: (0, 0)),
            ],
            out_specs=pl.BlockSpec((dp, STEP, width), lambda i, place: (0, 0, 0)),
            scratch_shapes=[pltpu.VMEM((features // TABLE, members * STEP, TABLE), jnp.float32)],
        ),
        out_shape=jax.ShapeDtypeStruct((dp, STEP, width), jnp.float32),
        compiler_params=pltpu.CompilerParams(vmem_limit_bytes=VMEM_BYTES),
        cost_estimate=pl.CostEstimate(
            flops=2 * STEP * WIDTH * BLOCK, bytes_accessed=8 * STEP * WIDTH, transcendentals=0
        ),
    )(place, rows, table)


def product_kernel(count, position, *refs):
    pieces, weight_ref = refs[:count], refs[count]
    out_ref, results, sems = refs[-3:]
    members = out_ref.shape[0]
    stores = []
    for n, piece_ref in enumerate(pieces):
        slots = piece_ref.shape[0] // (members * STEP)
        result = lax.dot_general(
            piece_ref[...],
            weight_ref[...],
            (((1,), (1,)), ((), ())),
            preferred_element_type=jnp.float32,
        ).astype(out_ref.dtype)
        for k in range(slots):
            for t in range(members):
                start = (k * members + t) * STEP
                results[n, t, k * STEP : (k + 1) * STEP, :] = result[start : start + STEP]
        place = (position * count + n) * slots * STEP
        stores.append(
            pltpu.make_async_copy(
                results.at[n], out_ref.at[:, pl.ds(place, slots * STEP), :], sems.at[n]
            )
        )
        stores[-1].start()
    for store in stores:
        store.wait()


def product(held, pieces, weight, position, members, total):
    count, rows = len(pieces), pieces[0].shape[0]
    width, depth = weight.shape
    earlier = [] if held is None else [held]
    return pl.pallas_call(
        functools.partial(product_kernel, count, position),
        in_specs=[pl.BlockSpec(memory_space=pltpu.VMEM)] * (count + 1)
        + [pl.BlockSpec(memory_space=pltpu.HBM)] * len(earlier),
        out_specs=pl.BlockSpec(memory_space=pltpu.HBM),
        out_shape=jax.ShapeDtypeStruct((members, total // members, width), jnp.bfloat16),
        scratch_shapes=[
            pltpu.VMEM((count, members, rows // members, width), jnp.bfloat16),
            pltpu.SemaphoreType.DMA((count,)),
        ],
        input_output_aliases={count + 1: 0} if earlier else {},
        compiler_params=pltpu.CompilerParams(vmem_limit_bytes=LITTLE_VMEM),
        cost_estimate=pl.CostEstimate(
            flops=2 * count * rows * depth * width,
            bytes_accessed=2 * count * rows * (depth + width),
            transcendentals=0,
        ),
    )(*pieces, weight, *earlier)


def order_kernel(sources, rows_ref, out_ref):
    for slot in range(rows_ref.shape[0]):
        out_ref[sources[slot]] = rows_ref[slot]


def order(rows, sources):
    return pl.pallas_call(
        order_kernel,
        in_specs=[
            pl.BlockSpec(memory_space=pltpu.SMEM),
            pl.BlockSpec(memory_space=pltpu.VMEM),
        ],
        out_specs=pl.BlockSpec(memory_space=pltpu.VMEM),
        out_shape=jax.ShapeDtypeStruct(rows.shape, rows.dtype),
        compiler_params=pltpu.CompilerParams(vmem_limit_bytes=VMEM_BYTES),
    )(sources, rows)


def gradient_kernel(sources, quantized_ref, *refs):
    out_ref = refs[-1]
    pieces = refs[:-1]
    tokens = quantized_ref.shape[1]
    slot = 0
    for number, piece_ref in enumerate(pieces):
        count = piece_ref.shape[0] // tokens
        block = jnp.concatenate(
            [quantized_ref[sources[slot + k]] for k in range(count)], axis=0
        )
        slot += count
        term = lax.dot_general(
            block, piece_ref[...], (((0,), (0,)), ((), ())), preferred_element_type=jnp.float32
        )
        out_ref[...] = term if number == 0 else out_ref[...] + term


def gradient(sources, quantized, pieces):
    width, depth = quantized.shape[2], pieces[0].shape[1]
    rows = sum(piece.shape[0] for piece in pieces)
    return pl.pallas_call(
        gradient_kernel,
        in_specs=[pl.BlockSpec(memory_space=pltpu.SMEM)]
        + [pl.BlockSpec(memory_space=pltpu.VMEM)] * (len(pieces) + 1),
        out_specs=pl.BlockSpec(memory_space=pltpu.VMEM),
        out_shape=jax.ShapeDtypeStruct((width, depth), jnp.float32),
        compiler_params=pltpu.CompilerParams(vmem_limit_bytes=VMEM_BYTES),
        cost_estimate=pl.CostEstimate(
            flops=2 * rows * depth * width,
            bytes_accessed=2 * rows * (depth + width) + 4 * width * depth,
            transcendentals=0,
        ),
    )(sources, quantized, *pieces)


def chip_core(x, y, core):
    return (x % SIDE * SIDE + y % SIDE) * 2 + core


def route(turn, sign):
    pairs = []
    for x in range(SIDE):
        for y in range(SIDE):
            for core in range(2):
                along = (sign, 0) if core == turn else (0, sign)
                pairs.append(
                    (chip_core(x, y, core), chip_core(x + along[0], y + along[1], core))
                )
    return pairs


def send(block, turn, sign):
    return lax.ppermute(block, "dp", route(turn, sign))


def other_core(block):
    return lax.ppermute(block, "dp", [(d, d ^ 1) for d in range(2 * SIDE * SIDE)])


def sources_table():
    table = []
    for x in range(SIDE):
        for y in range(SIDE):
            for core in range(2):
                found = []
                for outer in OFFSETS:
                    for sender in (core, 1 - core):
                        for inner in OFFSETS:
                            along = (inner, outer) if sender == 0 else (outer, inner)
                            found.append(chip_core(x + along[0], y + along[1], sender))
                table.append(found)
    return np.asarray(table, np.int32)


def finish_kernel(summed_ref, slope_ref, table_ref, out_ref, inner):
    devices, step, width = summed_ref.shape
    members, per_width = out_ref.shape[0], width // TABLE
    per_shard = devices // members
    upstream = (summed_ref[...].astype(jnp.float32) * slope_ref[...]).astype(jnp.bfloat16)
    upstream = upstream.reshape(devices * step, width)
    for c in range(per_width):
        inner[c] = jnp.dot(
            upstream[:, c * TABLE : (c + 1) * TABLE],
            table_ref[...],
            preferred_element_type=jnp.float32,
        )
    span = lambda d: slice(d * step, (d + 1) * step)
    for l in range(TABLE // LANES):
        lanes = slice(l * LANES, (l + 1) * LANES)
        for t in range(members):
            near = [(c, span(t * per_shard + k)) for k in range(per_shard) for c in range(per_width)]
            parts = butterfly([inner[c, rows, lanes] for c, rows in near])
            for (c, rows), part in zip(near, parts):
                inner[c, rows, lanes] = part
        for k in range(per_shard):
            for c in range(per_width):
                far = [span(t * per_shard + k) for t in range(members)]
                parts = butterfly([inner[c, rows, lanes] for rows in far])
                start = (k * per_width + c) * TABLE + l * LANES
                for t in range(members):
                    out_ref[t, :, start : start + LANES] = (parts[t] * NORM).astype(out_ref.dtype)


def finish(summed, slope, table, members):
    devices, step, width = summed.shape
    return pl.pallas_call(
        finish_kernel,
        out_shape=jax.ShapeDtypeStruct((members, step, WIDTH // members), jnp.bfloat16),
        scratch_shapes=[pltpu.VMEM((width // TABLE, devices * step, TABLE), jnp.float32)],
        compiler_params=pltpu.CompilerParams(vmem_limit_bytes=LITTLE_VMEM),
        cost_estimate=pl.CostEstimate(
            flops=2 * step * WIDTH * BLOCK, bytes_accessed=8 * step * WIDTH, transcendentals=0
        ),
    )(summed, slope, table)


def shards(activations, weight, grad_out):
    dp = lax.axis_size("dp")
    members = lax.axis_size("tensor")
    tokens, features = activations.shape
    width = weight.shape[0]
    place = lax.axis_index("tensor").astype(jnp.int32).reshape(1)
    sources = jnp.asarray(sources_table())[lax.axis_index("dp")]
    table = hadamard_table(TABLE)
    wide_rows = lax.all_gather(activations, "tensor", axis=0, tiled=False)
    total = dp * tokens

    def multiply(held, pieces, position):
        return product(held, pieces, weight, position, members, total)

    half = tokens // 2
    below, above = send(grad_out, 0, 1), send(grad_out, 0, -1)
    top = jnp.concatenate([grad_out, below], axis=0)
    below_top, above_top = send(top, 1, 1), send(top, 1, -1)
    far = [send(below[:half], 0, 1), send(above[half:], 0, -1)]
    bottom = jnp.concatenate([above, *far], axis=0)
    below_bottom, above_bottom = send(bottom, 1, 1), send(bottom, 1, -1)
    far_top = send(below_top, 1, 1)
    near = [top, bottom]
    near_other = [other_core(block) for block in near]
    held = multiply(None, near + near_other, 0)
    below_bottom, above_bottom, held = lax.optimization_barrier(
        (below_bottom, above_bottom, held)
    )
    far_bottom = send(above_bottom, 1, -1)
    below, above = [below_top, below_bottom], [above_top, above_bottom]
    below_other = [other_core(block) for block in below]
    above_other = [other_core(block) for block in above]
    held = multiply(held, below + below_other, 1)
    held = multiply(held, above + above_other, 2)
    far_top, far_bottom, held = lax.optimization_barrier((far_top, far_bottom, held))
    far = [far_top, far_bottom]
    far_other = [other_core(block) for block in far]
    held = multiply(held, far, 6)
    partial_rows = multiply(held, far_other, 7)
    partial_rows, wide_rows = lax.optimization_barrier((partial_rows, wide_rows))
    summed = lax.psum_scatter(partial_rows, "tensor", scatter_dimension=0, tiled=False)
    quantized = quantize(wide_rows, table, dp, width)
    q_block = lax.all_to_all(quantized, "dp", split_axis=0, concat_axis=0, tiled=True)
    summed, wide_rows = lax.optimization_barrier((summed, wide_rows))
    slope = slopes(wide_rows, table, place, dp, width)
    ordered = order(summed.reshape(dp, tokens // members, width), sources)
    ordered, q_block, slope = lax.optimization_barrier((ordered, q_block, slope))
    homed = lax.all_to_all(ordered, "dp", split_axis=0, concat_axis=0, tiled=True)
    mixed = finish(homed, slope, table, members)
    grad_input = lax.all_to_all(mixed, "tensor", split_axis=0, concat_axis=0, tiled=True)
    arrived = near + near_other + below + below_other + above + above_other + far + far_other
    weight_sum = gradient(sources, q_block, arrived)
    return (grad_input.reshape(tokens, features), weight_sum)


def solution(mesh):
    return jax.shard_map(
        shards,
        mesh=mesh,
        in_specs=(P("dp", "tensor"), P("dp", "tensor"), P("dp", "tensor")),
        out_specs=(P("dp", "tensor"), P("dp", "tensor")),
        check_vma=False,
    )
```

```python
import functools
import math

import jax
import jax.numpy as jnp
import numpy as np
from jax import lax
from jax.experimental import pallas as pl
from jax.experimental.pallas import tpu as pltpu
from jax.sharding import PartitionSpec as P

BLOCK = 1024
WIDTH = 16384
TABLE = 256
LANES = 128
VMEM_BYTES = 60 * 1024 * 1024
LITTLE_VMEM = 16 * 1024 * 1024
HALVES = [slice(start, start + LANES) for start in range(0, TABLE, LANES)]
NORM = 1.0 / math.sqrt(WIDTH)
SIDE = 4
STEP = 16
OFFSETS = (0, -1, 1, -2)

levels = 127.0
ripple = 0.5
epsilon = 1e-06


def hadamard_table(length):
    table = np.ones((1, 1), np.float32)
    while table.shape[0] < length:
        table = np.block([[table, table], [table, -table]])
    return jnp.asarray(table, jnp.bfloat16)


def fit(odd, terms):
    nodes = 0.5 * np.cos(np.pi * (np.arange(400) + 0.5) / 800.0)
    squares = nodes * nodes
    values = np.sin(2.0 * np.pi * nodes) / nodes if odd else np.cos(2.0 * np.pi * nodes)
    scaled = np.polynomial.chebyshev.Chebyshev.fit(squares, values, terms - 1, domain=[0.0, 0.25])
    return [float(c) for c in scaled.convert(kind=np.polynomial.Polynomial).coef]


SINE = [ripple / (2.0 * math.pi) * c for c in fit(True, 5)]
COSINE = fit(False, 7)


def horner(coefficients, square):
    total = jnp.full_like(square, coefficients[-1])
    for coefficient in coefficients[-2::-1]:
        total = total * square + coefficient
    return total


def butterfly(parts):
    distance = 1
    while distance < len(parts):
        mixed = list(parts)
        for low in range(len(parts)):
            if not low & distance:
                mixed[low] = parts[low] + parts[low | distance]
                mixed[low | distance] = parts[low] - parts[low | distance]
        parts = mixed
        distance *= 2
    return parts


def levels_of(largest):
    rows = largest.shape[0]
    peak = jnp.max(largest, axis=1, keepdims=True) * NORM
    scale = (peak + epsilon) / levels
    inverse = jnp.broadcast_to(NORM / scale, (rows, LANES))
    return inverse, jnp.broadcast_to(scale, (rows, LANES))


def remainder(value, inverse):
    turns = value * inverse
    return turns - jnp.round(turns)


def quantized_of(value, inverse, scale):
    turns = value * inverse
    rest = turns - jnp.round(turns)
    return scale * (turns - rest * horner(SINE, rest * rest))


def slope_of(value, inverse):
    rest = remainder(value, inverse)
    return 1.0 - ripple * horner(COSINE, rest * rest)


def mix(rows, table, inner, spans):
    chunks = inner.shape[0]
    for c in range(chunks):
        inner[c] = jnp.dot(
            rows[:, c * TABLE : (c + 1) * TABLE], table, preferred_element_type=jnp.float32
        )
    return [mix_group(inner, group) for group in spans]


def mix_group(inner, spans):
    chunks = inner.shape[0]
    rows = spans[0].stop - spans[0].start
    for span in spans:
        for lanes in HALVES:
            parts = butterfly([inner[c, span, lanes] for c in range(chunks)])
            for c in range(chunks):
                inner[c, span, lanes] = parts[c]
    largest = jnp.zeros((rows, LANES), jnp.float32)
    for c in range(chunks):
        for lanes in HALVES:
            parts = butterfly([inner[c, span, lanes] for span in spans])
            for span, part in zip(spans, parts):
                inner[c, span, lanes] = part
                largest = jnp.maximum(largest, jnp.abs(part))
    return largest


def quantize_kernel(rows_ref, table_ref, quantized_ref, inner):
    members, count, features = rows_ref.shape
    width = quantized_ref.shape[2]
    chunks, per_shard, per_width = features // TABLE, features // width, width // TABLE
    groups = [
        [slice(t * count + g, t * count + g + STEP) for t in range(members)]
        for g in range(0, count, STEP)
    ]
    rows = rows_ref[...].reshape(members * count, features)
    found = mix(rows, table_ref[...], inner, groups)
    for g, (spans, largest) in enumerate(zip(groups, found)):
        inverse, scale = levels_of(largest)
        here = slice(g * STEP, (g + 1) * STEP)
        for t, span in enumerate(spans):
            for c in range(chunks):
                for l, lanes in enumerate(HALVES):
                    start = (c % per_width) * TABLE + l * LANES
                    block = t * per_shard + c // per_width
                    quantized_ref[block, here, start : start + LANES] = quantized_of(
                        inner[c, span, lanes], inverse, scale
                    ).astype(jnp.bfloat16)


def quantize(rows, table, dp, width):
    members, tokens, features = rows.shape
    count = 2 * STEP
    return pl.pallas_call(
        quantize_kernel,
        grid=(tokens // count,),
        in_specs=[
            pl.BlockSpec((members, count, features), lambda i: (0, i, 0)),
            pl.BlockSpec((TABLE, TABLE), lambda i: (0, 0)),
        ],
        out_specs=pl.BlockSpec((dp, count, width), lambda i: (0, i, 0)),
        scratch_shapes=[pltpu.VMEM((features // TABLE, members * count, TABLE), jnp.float32)],
        out_shape=jax.ShapeDtypeStruct((dp, tokens, width), jnp.bfloat16),
        compiler_params=pltpu.CompilerParams(vmem_limit_bytes=VMEM_BYTES),
        cost_estimate=pl.CostEstimate(
            flops=2 * tokens * WIDTH * BLOCK, bytes_accessed=4 * tokens * WIDTH, transcendentals=0
        ),
    )(rows, table)


def slope_kernel(place, rows_ref, table_ref, slope_ref, inner):
    members, _, features = rows_ref.shape
    devices, _, width = slope_ref.shape
    per_shard, per_width = devices // members, width // TABLE
    spans = [slice(t * STEP, (t + 1) * STEP) for t in range(members)]
    rows = rows_ref[...].reshape(members * STEP, features)
    (largest,) = mix(rows, table_ref[...], inner, [spans])
    inverse, _ = levels_of(largest)
    for block in range(devices):
        for k in range(per_width):
            for l, lanes in enumerate(HALVES):
                c = block % per_shard * per_width + k
                start = k * TABLE + l * LANES
                slope_ref[block, :, start : start + LANES] = slope_of(
                    inner[c, spans[block // per_shard], lanes], inverse
                ).astype(slope_ref.dtype)


def slopes(rows, table, place, dp, width):
    members, tokens, features = rows.shape
    return pl.pallas_call(
        slope_kernel,
        grid_spec=pltpu.PrefetchScalarGridSpec(
            num_scalar_prefetch=1,
            grid=(1,),
            in_specs=[
                pl.BlockSpec((members, STEP, features), lambda i, place: (0, place[0], 0)),
                pl.BlockSpec((TABLE, TABLE), lambda i, place: (0, 0)),
            ],
            out_specs=pl.BlockSpec((dp, STEP, width), lambda i, place: (0, 0, 0)),
            scratch_shapes=[pltpu.VMEM((features // TABLE, members * STEP, TABLE), jnp.float32)],
        ),
        out_shape=jax.ShapeDtypeStruct((dp, STEP, width), jnp.bfloat16),
        compiler_params=pltpu.CompilerParams(vmem_limit_bytes=VMEM_BYTES),
        cost_estimate=pl.CostEstimate(
            flops=2 * STEP * WIDTH * BLOCK, bytes_accessed=8 * STEP * WIDTH, transcendentals=0
        ),
    )(place, rows, table)


def product_kernel(count, position, *refs):
    pieces, weight_ref = refs[:count], refs[count]
    out_ref, results, sems = refs[-3:]
    members = out_ref.shape[0]
    stores = []
    for n, piece_ref in enumerate(pieces):
        slots = piece_ref.shape[0] // (members * STEP)
        result = lax.dot_general(
            piece_ref[...],
            weight_ref[...],
            (((1,), (1,)), ((), ())),
            preferred_element_type=jnp.float32,
        ).astype(out_ref.dtype)
        for k in range(slots):
            for t in range(members):
                start = (k * members + t) * STEP
                results[n, t, k * STEP : (k + 1) * STEP, :] = result[start : start + STEP]
        place = (position * count + n) * slots * STEP
        stores.append(
            pltpu.make_async_copy(
                results.at[n], out_ref.at[:, pl.ds(place, slots * STEP), :], sems.at[n]
            )
        )
        stores[-1].start()
    for store in stores:
        store.wait()


def product(held, pieces, weight, position, members, total):
    count, rows = len(pieces), pieces[0].shape[0]
    width, depth = weight.shape
    earlier = [] if held is None else [held]
    return pl.pallas_call(
        functools.partial(product_kernel, count, position),
        in_specs=[pl.BlockSpec(memory_space=pltpu.VMEM)] * (count + 1)
        + [pl.BlockSpec(memory_space=pltpu.HBM)] * len(earlier),
        out_specs=pl.BlockSpec(memory_space=pltpu.HBM),
        out_shape=pltpu.HBM((members, total // members, width), jnp.bfloat16),
        scratch_shapes=[
            pltpu.VMEM((count, members, rows // members, width), jnp.bfloat16),
            pltpu.SemaphoreType.DMA((count,)),
        ],
        input_output_aliases={count + 1: 0} if earlier else {},
        compiler_params=pltpu.CompilerParams(vmem_limit_bytes=LITTLE_VMEM),
        cost_estimate=pl.CostEstimate(
            flops=2 * count * rows * depth * width,
            bytes_accessed=2 * count * rows * (depth + width),
            transcendentals=0,
        ),
    )(*pieces, weight, *earlier)


def order_kernel(sources, rows_ref, out_ref):
    for slot in range(rows_ref.shape[0]):
        out_ref[sources[slot]] = rows_ref[slot]


def order(rows, sources):
    return pl.pallas_call(
        order_kernel,
        in_specs=[
            pl.BlockSpec(memory_space=pltpu.SMEM),
            pl.BlockSpec(memory_space=pltpu.VMEM),
        ],
        out_specs=pl.BlockSpec(memory_space=pltpu.VMEM),
        out_shape=jax.ShapeDtypeStruct(rows.shape, rows.dtype),
        compiler_params=pltpu.CompilerParams(vmem_limit_bytes=VMEM_BYTES),
    )(sources, rows)


def gradient_kernel(sources, quantized_ref, *refs):
    out_ref = refs[-1]
    pieces = refs[:-1]
    tokens = quantized_ref.shape[1]
    slot = 0
    for number, piece_ref in enumerate(pieces):
        count = piece_ref.shape[0] // tokens
        block = jnp.concatenate(
            [quantized_ref[sources[slot + k]] for k in range(count)], axis=0
        )
        slot += count
        term = lax.dot_general(
            block, piece_ref[...], (((0,), (0,)), ((), ())), preferred_element_type=jnp.float32
        )
        out_ref[...] = term if number == 0 else out_ref[...] + term


def gradient(sources, quantized, pieces):
    width, depth = quantized.shape[2], pieces[0].shape[1]
    rows = sum(piece.shape[0] for piece in pieces)
    return pl.pallas_call(
        gradient_kernel,
        in_specs=[pl.BlockSpec(memory_space=pltpu.SMEM)]
        + [pl.BlockSpec(memory_space=pltpu.VMEM)] * (len(pieces) + 1),
        out_specs=pl.BlockSpec(memory_space=pltpu.VMEM),
        out_shape=jax.ShapeDtypeStruct((width, depth), jnp.float32),
        compiler_params=pltpu.CompilerParams(vmem_limit_bytes=VMEM_BYTES),
        cost_estimate=pl.CostEstimate(
            flops=2 * rows * depth * width,
            bytes_accessed=2 * rows * (depth + width) + 4 * width * depth,
            transcendentals=0,
        ),
    )(sources, quantized, *pieces)


def chip_core(x, y, core):
    return (x % SIDE * SIDE + y % SIDE) * 2 + core


def route(turn, sign):
    pairs = []
    for x in range(SIDE):
        for y in range(SIDE):
            for core in range(2):
                along = (sign, 0) if core == turn else (0, sign)
                pairs.append(
                    (chip_core(x, y, core), chip_core(x + along[0], y + along[1], core))
                )
    return pairs


def send(block, turn, sign):
    return lax.ppermute(block, "dp", route(turn, sign))


def other_core(block):
    return lax.ppermute(block, "dp", [(d, d ^ 1) for d in range(2 * SIDE * SIDE)])


def sources_table():
    table = []
    for x in range(SIDE):
        for y in range(SIDE):
            for core in range(2):
                found = []
                for outer in OFFSETS:
                    for sender in (core, 1 - core):
                        for inner in OFFSETS:
                            along = (inner, outer) if sender == 0 else (outer, inner)
                            found.append(chip_core(x + along[0], y + along[1], sender))
                table.append(found)
    return np.asarray(table, np.int32)


def finish_kernel(summed_ref, slope_ref, table_ref, out_ref, inner):
    devices, step, width = summed_ref.shape
    members, per_width = out_ref.shape[0], width // TABLE
    per_shard = devices // members
    upstream = summed_ref[...].astype(jnp.float32) * slope_ref[...].astype(jnp.float32)
    upstream = upstream.astype(jnp.bfloat16)
    upstream = upstream.reshape(devices * step, width)
    for c in range(per_width):
        inner[c] = jnp.dot(
            upstream[:, c * TABLE : (c + 1) * TABLE],
            table_ref[...],
            preferred_element_type=jnp.float32,
        )
    span = lambda d: slice(d * step, (d + 1) * step)
    for l in range(TABLE // LANES):
        lanes = slice(l * LANES, (l + 1) * LANES)
        for t in range(members):
            near = [(c, span(t * per_shard + k)) for k in range(per_shard) for c in range(per_width)]
            parts = butterfly([inner[c, rows, lanes] for c, rows in near])
            for (c, rows), part in zip(near, parts):
                inner[c, rows, lanes] = part
        for k in range(per_shard):
            for c in range(per_width):
                far = [span(t * per_shard + k) for t in range(members)]
                parts = butterfly([inner[c, rows, lanes] for rows in far])
                start = (k * per_width + c) * TABLE + l * LANES
                for t in range(members):
                    out_ref[t, :, start : start + LANES] = (parts[t] * NORM).astype(out_ref.dtype)


def finish(summed, slope, table, members):
    devices, step, width = summed.shape
    return pl.pallas_call(
        finish_kernel,
        out_shape=jax.ShapeDtypeStruct((members, step, WIDTH // members), jnp.bfloat16),
        scratch_shapes=[pltpu.VMEM((width // TABLE, devices * step, TABLE), jnp.float32)],
        compiler_params=pltpu.CompilerParams(vmem_limit_bytes=LITTLE_VMEM),
        cost_estimate=pl.CostEstimate(
            flops=2 * step * WIDTH * BLOCK, bytes_accessed=8 * step * WIDTH, transcendentals=0
        ),
    )(summed, slope, table)


def shards(activations, weight, grad_out):
    dp = lax.axis_size("dp")
    members = lax.axis_size("tensor")
    tokens, features = activations.shape
    width = weight.shape[0]
    place = lax.axis_index("tensor").astype(jnp.int32).reshape(1)
    sources = jnp.asarray(sources_table())[lax.axis_index("dp")]
    table = hadamard_table(TABLE)
    wide_rows = lax.all_gather(activations, "tensor", axis=0, tiled=False)
    total = dp * tokens

    def multiply(held, pieces, position):
        return product(held, pieces, weight, position, members, total)

    half = tokens // 2
    below, above = send(grad_out, 0, 1), send(grad_out, 0, -1)
    top = jnp.concatenate([grad_out, below], axis=0)
    below_top, above_top = send(top, 1, 1), send(top, 1, -1)
    far = [send(below[:half], 0, 1), send(above[half:], 0, -1)]
    bottom = jnp.concatenate([above, *far], axis=0)
    below_bottom, above_bottom = send(bottom, 1, 1), send(bottom, 1, -1)
    far_top = send(below_top, 1, 1)
    near = [top, bottom]
    near_other = [other_core(block) for block in near]
    held = multiply(None, near + near_other, 0)
    below_bottom, above_bottom, held = lax.optimization_barrier(
        (below_bottom, above_bottom, held)
    )
    far_bottom = send(above_bottom, 1, -1)
    below, above = [below_top, below_bottom], [above_top, above_bottom]
    below_other = [other_core(block) for block in below]
    above_other = [other_core(block) for block in above]
    held = multiply(held, below + below_other, 1)
    held = multiply(held, above + above_other, 2)
    far_top, far_bottom, held = lax.optimization_barrier((far_top, far_bottom, held))
    far = [far_top, far_bottom]
    far_other = [other_core(block) for block in far]
    held = multiply(held, far, 6)
    partial_rows = multiply(held, far_other, 7)
    partial_rows, wide_rows = lax.optimization_barrier((partial_rows, wide_rows))
    summed = lax.psum_scatter(partial_rows, "tensor", scatter_dimension=0, tiled=False)
    quantized = quantize(wide_rows, table, dp, width)
    q_block = lax.all_to_all(quantized, "dp", split_axis=0, concat_axis=0, tiled=True)
    summed, wide_rows = lax.optimization_barrier((summed, wide_rows))
    slope = slopes(wide_rows, table, place, dp, width)
    ordered = order(summed.reshape(dp, tokens // members, width), sources)
    ordered, q_block, slope = lax.optimization_barrier((ordered, q_block, slope))
    homed = lax.all_to_all(ordered, "dp", split_axis=0, concat_axis=0, tiled=True)
    mixed = finish(homed, slope, table, members)
    grad_input = lax.all_to_all(mixed, "tensor", split_axis=0, concat_axis=0, tiled=True)
    arrived = near + near_other + below + below_other + above + above_other + far + far_other
    weight_sum = gradient(sources, q_block, arrived)
    return (grad_input.reshape(tokens, features), weight_sum)


def solution(mesh):
    return jax.shard_map(
        shards,
        mesh=mesh,
        in_specs=(P("dp", "tensor"), P("dp", "tensor"), P("dp", "tensor")),
        out_specs=(P("dp", "tensor"), P("dp", "tensor")),
        check_vma=False,
    )
```

```python
import functools
import math

import jax
import jax.numpy as jnp
import numpy as np
from jax import lax
from jax.experimental import pallas as pl
from jax.experimental.pallas import tpu as pltpu
from jax.sharding import PartitionSpec as P

BLOCK = 1024
WIDTH = 16384
TABLE = 256
LANES = 128
VMEM_BYTES = 60 * 1024 * 1024
LITTLE_VMEM = 16 * 1024 * 1024
HALVES = [slice(start, start + LANES) for start in range(0, TABLE, LANES)]
NORM = 1.0 / math.sqrt(WIDTH)
SIDE = 4
STEP = 16
OFFSETS = (0, -1, 1, -2)

levels = 127.0
ripple = 0.5
epsilon = 1e-06


def hadamard_table(length):
    table = np.ones((1, 1), np.float32)
    while table.shape[0] < length:
        table = np.block([[table, table], [table, -table]])
    return jnp.asarray(table, jnp.bfloat16)


def fit(odd, terms):
    nodes = 0.5 * np.cos(np.pi * (np.arange(400) + 0.5) / 800.0)
    squares = nodes * nodes
    values = np.sin(2.0 * np.pi * nodes) / nodes if odd else np.cos(2.0 * np.pi * nodes)
    scaled = np.polynomial.chebyshev.Chebyshev.fit(squares, values, terms - 1, domain=[0.0, 0.25])
    return [float(c) for c in scaled.convert(kind=np.polynomial.Polynomial).coef]


SINE = [ripple / (2.0 * math.pi) * c for c in fit(True, 5)]
COSINE = fit(False, 7)


def horner(coefficients, square):
    total = jnp.full_like(square, coefficients[-1])
    for coefficient in coefficients[-2::-1]:
        total = total * square + coefficient
    return total


def butterfly(parts):
    distance = 1
    while distance < len(parts):
        mixed = list(parts)
        for low in range(len(parts)):
            if not low & distance:
                mixed[low] = parts[low] + parts[low | distance]
                mixed[low | distance] = parts[low] - parts[low | distance]
        parts = mixed
        distance *= 2
    return parts


def levels_of(largest):
    rows = largest.shape[0]
    peak = jnp.max(largest, axis=1, keepdims=True) * NORM
    scale = (peak + epsilon) / levels
    inverse = jnp.broadcast_to(NORM / scale, (rows, LANES))
    return inverse, jnp.broadcast_to(scale, (rows, LANES))


def remainder(value, inverse):
    turns = value * inverse
    return turns - jnp.round(turns)


def quantized_of(value, inverse, scale):
    turns = value * inverse
    rest = turns - jnp.round(turns)
    return scale * (turns - rest * horner(SINE, rest * rest))


def slope_of(value, inverse):
    rest = remainder(value, inverse)
    return 1.0 - ripple * horner(COSINE, rest * rest)


def mix(rows, table, inner, spans):
    chunks = inner.shape[0]
    for c in range(chunks):
        inner[c] = jnp.dot(
            rows[:, c * TABLE : (c + 1) * TABLE], table, preferred_element_type=jnp.float32
        )
    return [mix_group(inner, group) for group in spans]


def mix_group(inner, spans):
    chunks = inner.shape[0]
    rows = spans[0].stop - spans[0].start
    for span in spans:
        for lanes in HALVES:
            parts = butterfly([inner[c, span, lanes] for c in range(chunks)])
            for c in range(chunks):
                inner[c, span, lanes] = parts[c]
    largest = jnp.zeros((rows, LANES), jnp.float32)
    for c in range(chunks):
        for lanes in HALVES:
            parts = butterfly([inner[c, span, lanes] for span in spans])
            for span, part in zip(spans, parts):
                inner[c, span, lanes] = part
                largest = jnp.maximum(largest, jnp.abs(part))
    return largest


def quantize_kernel(rows_ref, table_ref, quantized_ref, inner):
    members, count, features = rows_ref.shape
    width = quantized_ref.shape[2]
    chunks, per_shard, per_width = features // TABLE, features // width, width // TABLE
    groups = [
        [slice(t * count + g, t * count + g + STEP) for t in range(members)]
        for g in range(0, count, STEP)
    ]
    rows = rows_ref[...].reshape(members * count, features)
    found = mix(rows, table_ref[...], inner, groups)
    for g, (spans, largest) in enumerate(zip(groups, found)):
        inverse, scale = levels_of(largest)
        here = slice(g * STEP, (g + 1) * STEP)
        for t, span in enumerate(spans):
            for c in range(chunks):
                for l, lanes in enumerate(HALVES):
                    start = (c % per_width) * TABLE + l * LANES
                    block = t * per_shard + c // per_width
                    quantized_ref[block, here, start : start + LANES] = quantized_of(
                        inner[c, span, lanes], inverse, scale
                    ).astype(jnp.bfloat16)


def quantize(rows, table, dp, width):
    members, tokens, features = rows.shape
    count = 2 * STEP
    return pl.pallas_call(
        quantize_kernel,
        grid=(tokens // count,),
        in_specs=[
            pl.BlockSpec((members, count, features), lambda i: (0, i, 0)),
            pl.BlockSpec((TABLE, TABLE), lambda i: (0, 0)),
        ],
        out_specs=pl.BlockSpec((dp, count, width), lambda i: (0, i, 0)),
        scratch_shapes=[pltpu.VMEM((features // TABLE, members * count, TABLE), jnp.float32)],
        out_shape=jax.ShapeDtypeStruct((dp, tokens, width), jnp.bfloat16),
        compiler_params=pltpu.CompilerParams(vmem_limit_bytes=VMEM_BYTES),
        cost_estimate=pl.CostEstimate(
            flops=2 * tokens * WIDTH * BLOCK, bytes_accessed=4 * tokens * WIDTH, transcendentals=0
        ),
    )(rows, table)


def slope_kernel(place, rows_ref, table_ref, slope_ref, inner):
    members, _, features = rows_ref.shape
    devices, _, width = slope_ref.shape
    per_shard, per_width = devices // members, width // TABLE
    spans = [slice(t * STEP, (t + 1) * STEP) for t in range(members)]
    rows = rows_ref[...].reshape(members * STEP, features)
    (largest,) = mix(rows, table_ref[...], inner, [spans])
    inverse, _ = levels_of(largest)
    for block in range(devices):
        for k in range(per_width):
            for l, lanes in enumerate(HALVES):
                c = block % per_shard * per_width + k
                start = k * TABLE + l * LANES
                slope_ref[block, :, start : start + LANES] = slope_of(
                    inner[c, spans[block // per_shard], lanes], inverse
                ).astype(slope_ref.dtype)


def slopes(rows, table, place, dp, width):
    members, tokens, features = rows.shape
    return pl.pallas_call(
        slope_kernel,
        grid_spec=pltpu.PrefetchScalarGridSpec(
            num_scalar_prefetch=1,
            grid=(1,),
            in_specs=[
                pl.BlockSpec((members, STEP, features), lambda i, place: (0, place[0], 0)),
                pl.BlockSpec((TABLE, TABLE), lambda i, place: (0, 0)),
            ],
            out_specs=pl.BlockSpec((dp, STEP, width), lambda i, place: (0, 0, 0)),
            scratch_shapes=[pltpu.VMEM((features // TABLE, members * STEP, TABLE), jnp.float32)],
        ),
        out_shape=jax.ShapeDtypeStruct((dp, STEP, width), jnp.bfloat16),
        compiler_params=pltpu.CompilerParams(vmem_limit_bytes=VMEM_BYTES),
        cost_estimate=pl.CostEstimate(
            flops=2 * STEP * WIDTH * BLOCK, bytes_accessed=8 * STEP * WIDTH, transcendentals=0
        ),
    )(place, rows, table)


def product_kernel(count, positions, *refs):
    pieces, weight_ref = refs[:count], refs[count]
    out_ref, results, sems = refs[-3:]
    members = out_ref.shape[0]
    stores = []
    for n, piece_ref in enumerate(pieces):
        slots = piece_ref.shape[0] // (members * STEP)
        result = lax.dot_general(
            piece_ref[...],
            weight_ref[...],
            (((1,), (1,)), ((), ())),
            preferred_element_type=jnp.float32,
        ).astype(out_ref.dtype)
        for k in range(slots):
            for t in range(members):
                start = (k * members + t) * STEP
                results[n, t, k * STEP : (k + 1) * STEP, :] = result[start : start + STEP]
        place = positions[n] * slots * STEP
        stores.append(
            pltpu.make_async_copy(
                results.at[n], out_ref.at[:, pl.ds(place, slots * STEP), :], sems.at[n]
            )
        )
        stores[-1].start()
    for store in stores:
        store.wait()


def product(held, pieces, weight, positions, members, total):
    count, rows = len(pieces), pieces[0].shape[0]
    width, depth = weight.shape
    earlier = [] if held is None else [held]
    return pl.pallas_call(
        functools.partial(product_kernel, count, positions),
        in_specs=[pl.BlockSpec(memory_space=pltpu.VMEM)] * (count + 1)
        + [pl.BlockSpec(memory_space=pltpu.HBM)] * len(earlier),
        out_specs=pl.BlockSpec(memory_space=pltpu.HBM),
        out_shape=pltpu.HBM((members, total // members, width), jnp.bfloat16),
        scratch_shapes=[
            pltpu.VMEM((count, members, rows // members, width), jnp.bfloat16),
            pltpu.SemaphoreType.DMA((count,)),
        ],
        input_output_aliases={count + 1: 0} if earlier else {},
        compiler_params=pltpu.CompilerParams(vmem_limit_bytes=LITTLE_VMEM),
        cost_estimate=pl.CostEstimate(
            flops=2 * count * rows * depth * width,
            bytes_accessed=2 * count * rows * (depth + width),
            transcendentals=0,
        ),
    )(*pieces, weight, *earlier)


def order_kernel(sources, rows_ref, out_ref):
    for slot in range(rows_ref.shape[0]):
        out_ref[sources[slot]] = rows_ref[slot]


def order(rows, sources):
    return pl.pallas_call(
        order_kernel,
        in_specs=[
            pl.BlockSpec(memory_space=pltpu.SMEM),
            pl.BlockSpec(memory_space=pltpu.VMEM),
        ],
        out_specs=pl.BlockSpec(memory_space=pltpu.VMEM),
        out_shape=jax.ShapeDtypeStruct(rows.shape, rows.dtype),
        compiler_params=pltpu.CompilerParams(vmem_limit_bytes=VMEM_BYTES),
    )(sources, rows)


def gradient_kernel(sources, quantized_ref, *refs):
    out_ref = refs[-1]
    pieces = refs[:-1]
    tokens = quantized_ref.shape[1]
    slot = 0
    for number, piece_ref in enumerate(pieces):
        count = piece_ref.shape[0] // tokens
        block = jnp.concatenate(
            [quantized_ref[sources[slot + k]] for k in range(count)], axis=0
        )
        slot += count
        term = lax.dot_general(
            block, piece_ref[...], (((0,), (0,)), ((), ())), preferred_element_type=jnp.float32
        )
        out_ref[...] = term if number == 0 else out_ref[...] + term


def gradient(sources, quantized, pieces):
    width, depth = quantized.shape[2], pieces[0].shape[1]
    rows = sum(piece.shape[0] for piece in pieces)
    return pl.pallas_call(
        gradient_kernel,
        in_specs=[pl.BlockSpec(memory_space=pltpu.SMEM)]
        + [pl.BlockSpec(memory_space=pltpu.VMEM)] * (len(pieces) + 1),
        out_specs=pl.BlockSpec(memory_space=pltpu.VMEM),
        out_shape=jax.ShapeDtypeStruct((width, depth), jnp.float32),
        compiler_params=pltpu.CompilerParams(vmem_limit_bytes=VMEM_BYTES),
        cost_estimate=pl.CostEstimate(
            flops=2 * rows * depth * width,
            bytes_accessed=2 * rows * (depth + width) + 4 * width * depth,
            transcendentals=0,
        ),
    )(sources, quantized, *pieces)


def chip_core(x, y, core):
    return (x % SIDE * SIDE + y % SIDE) * 2 + core


def route(turn, sign):
    pairs = []
    for x in range(SIDE):
        for y in range(SIDE):
            for core in range(2):
                along = (sign, 0) if core == turn else (0, sign)
                pairs.append(
                    (chip_core(x, y, core), chip_core(x + along[0], y + along[1], core))
                )
    return pairs


def send(block, turn, sign):
    return lax.ppermute(block, "dp", route(turn, sign))


def other_core(block):
    return lax.ppermute(block, "dp", [(d, d ^ 1) for d in range(2 * SIDE * SIDE)])


def sources_table():
    table = []
    for x in range(SIDE):
        for y in range(SIDE):
            for core in range(2):
                found = []
                for outer in OFFSETS:
                    for sender in (core, 1 - core):
                        for inner in OFFSETS:
                            along = (inner, outer) if sender == 0 else (outer, inner)
                            found.append(chip_core(x + along[0], y + along[1], sender))
                table.append(found)
    return np.asarray(table, np.int32)


def finish_kernel(summed_ref, slope_ref, table_ref, out_ref, inner):
    devices, step, width = summed_ref.shape
    members, per_width = out_ref.shape[0], width // TABLE
    per_shard = devices // members
    upstream = summed_ref[...].astype(jnp.float32) * slope_ref[...].astype(jnp.float32)
    upstream = upstream.astype(jnp.bfloat16)
    upstream = upstream.reshape(devices * step, width)
    for c in range(per_width):
        inner[c] = jnp.dot(
            upstream[:, c * TABLE : (c + 1) * TABLE],
            table_ref[...],
            preferred_element_type=jnp.float32,
        )
    span = lambda d: slice(d * step, (d + 1) * step)
    for l in range(TABLE // LANES):
        lanes = slice(l * LANES, (l + 1) * LANES)
        for t in range(members):
            near = [(c, span(t * per_shard + k)) for k in range(per_shard) for c in range(per_width)]
            parts = butterfly([inner[c, rows, lanes] for c, rows in near])
            for (c, rows), part in zip(near, parts):
                inner[c, rows, lanes] = part
        for k in range(per_shard):
            for c in range(per_width):
                far = [span(t * per_shard + k) for t in range(members)]
                parts = butterfly([inner[c, rows, lanes] for rows in far])
                start = (k * per_width + c) * TABLE + l * LANES
                for t in range(members):
                    out_ref[t, :, start : start + LANES] = (parts[t] * NORM).astype(out_ref.dtype)


def finish(summed, slope, table, members):
    devices, step, width = summed.shape
    return pl.pallas_call(
        finish_kernel,
        out_shape=jax.ShapeDtypeStruct((members, step, WIDTH // members), jnp.bfloat16),
        scratch_shapes=[pltpu.VMEM((width // TABLE, devices * step, TABLE), jnp.float32)],
        compiler_params=pltpu.CompilerParams(vmem_limit_bytes=LITTLE_VMEM),
        cost_estimate=pl.CostEstimate(
            flops=2 * step * WIDTH * BLOCK, bytes_accessed=8 * step * WIDTH, transcendentals=0
        ),
    )(summed, slope, table)


def shards(activations, weight, grad_out):
    dp = lax.axis_size("dp")
    members = lax.axis_size("tensor")
    tokens, features = activations.shape
    width = weight.shape[0]
    place = lax.axis_index("tensor").astype(jnp.int32).reshape(1)
    sources = jnp.asarray(sources_table())[lax.axis_index("dp")]
    table = hadamard_table(TABLE)
    wide_rows = lax.all_gather(activations, "tensor", axis=0, tiled=False)
    total = dp * tokens

    def multiply(held, pieces, positions):
        return product(held, pieces, weight, positions, members, total)

    half = tokens // 2
    below, above = send(grad_out, 0, 1), send(grad_out, 0, -1)
    top = jnp.concatenate([grad_out, below], axis=0)
    below_top, above_top = send(top, 1, 1), send(top, 1, -1)
    far = [send(below[:half], 0, 1), send(above[half:], 0, -1)]
    bottom = jnp.concatenate([above, *far], axis=0)
    below_bottom, above_bottom = send(bottom, 1, 1), send(bottom, 1, -1)
    far_top = send(below_top, 1, 1)
    near = [top, bottom]
    near_other = [other_core(block) for block in near]
    held = multiply(None, near + near_other, range(0, 4))
    below_bottom, above_bottom, held = lax.optimization_barrier(
        (below_bottom, above_bottom, held)
    )
    far_bottom = send(above_bottom, 1, -1)
    below, above = [below_top, below_bottom], [above_top, above_bottom]
    below_other = [other_core(block) for block in below]
    above_other = [other_core(block) for block in above]
    held = multiply(held, below + below_other, range(4, 8))
    held = multiply(held, above + above_other, range(8, 12))
    far_top, held = lax.optimization_barrier((far_top, held))
    top_other = other_core(far_top)
    held = multiply(held, [far_top, top_other], (12, 14))
    far_bottom, held = lax.optimization_barrier((far_bottom, held))
    bottom_other = other_core(far_bottom)
    held = multiply(held, [far_bottom], (13,))
    partial_rows = multiply(held, [bottom_other], (15,))
    far, far_other = [far_top, far_bottom], [top_other, bottom_other]
    partial_rows, wide_rows = lax.optimization_barrier((partial_rows, wide_rows))
    summed = lax.psum_scatter(partial_rows, "tensor", scatter_dimension=0, tiled=False)
    quantized = quantize(wide_rows, table, dp, width)
    q_block = lax.all_to_all(quantized, "dp", split_axis=0, concat_axis=0, tiled=True)
    summed, wide_rows = lax.optimization_barrier((summed, wide_rows))
    slope = slopes(wide_rows, table, place, dp, width)
    ordered = order(summed.reshape(dp, tokens // members, width), sources)
    ordered, q_block, slope = lax.optimization_barrier((ordered, q_block, slope))
    homed = lax.all_to_all(ordered, "dp", split_axis=0, concat_axis=0, tiled=True)
    mixed = finish(homed, slope, table, members)
    grad_input = lax.all_to_all(mixed, "tensor", split_axis=0, concat_axis=0, tiled=True)
    arrived = near + near_other + below + below_other + above + above_other + far + far_other
    weight_sum = gradient(sources, q_block, arrived)
    return (grad_input.reshape(tokens, features), weight_sum)


def solution(mesh):
    return jax.shard_map(
        shards,
        mesh=mesh,
        in_specs=(P("dp", "tensor"), P("dp", "tensor"), P("dp", "tensor")),
        out_specs=(P("dp", "tensor"), P("dp", "tensor")),
        check_vma=False,
    )
```

```python
import functools
import math

import jax
import jax.numpy as jnp
import numpy as np
from jax import lax
from jax.experimental import pallas as pl
from jax.experimental.pallas import tpu as pltpu
from jax.sharding import PartitionSpec as P

BLOCK = 1024
WIDTH = 16384
TABLE = 256
LANES = 128
VMEM_BYTES = 60 * 1024 * 1024
LITTLE_VMEM = 16 * 1024 * 1024
HALVES = [slice(start, start + LANES) for start in range(0, TABLE, LANES)]
NORM = 1.0 / math.sqrt(WIDTH)
SIDE = 4
STEP = 16
OFFSETS = (0, -1, 1, -2)

levels = 127.0
ripple = 0.5
epsilon = 1e-06


def hadamard_table(length):
    table = np.ones((1, 1), np.float32)
    while table.shape[0] < length:
        table = np.block([[table, table], [table, -table]])
    return jnp.asarray(table, jnp.bfloat16)


def fit(odd, terms):
    nodes = 0.5 * np.cos(np.pi * (np.arange(400) + 0.5) / 800.0)
    squares = nodes * nodes
    values = np.sin(2.0 * np.pi * nodes) / nodes if odd else np.cos(2.0 * np.pi * nodes)
    scaled = np.polynomial.chebyshev.Chebyshev.fit(squares, values, terms - 1, domain=[0.0, 0.25])
    return [float(c) for c in scaled.convert(kind=np.polynomial.Polynomial).coef]


SINE = [ripple / (2.0 * math.pi) * c for c in fit(True, 5)]
COSINE = fit(False, 7)


def horner(coefficients, square):
    total = jnp.full_like(square, coefficients[-1])
    for coefficient in coefficients[-2::-1]:
        total = total * square + coefficient
    return total


def butterfly(parts):
    distance = 1
    while distance < len(parts):
        mixed = list(parts)
        for low in range(len(parts)):
            if not low & distance:
                mixed[low] = parts[low] + parts[low | distance]
                mixed[low | distance] = parts[low] - parts[low | distance]
        parts = mixed
        distance *= 2
    return parts


def levels_of(largest):
    rows = largest.shape[0]
    peak = jnp.max(largest, axis=1, keepdims=True) * NORM
    scale = (peak + epsilon) / levels
    inverse = jnp.broadcast_to(NORM / scale, (rows, LANES))
    return inverse, jnp.broadcast_to(scale, (rows, LANES))


def remainder(value, inverse):
    turns = value * inverse
    return turns - jnp.round(turns)


def quantized_of(value, inverse, scale):
    turns = value * inverse
    rest = turns - jnp.round(turns)
    return scale * (turns - rest * horner(SINE, rest * rest))


def slope_of(value, inverse):
    rest = remainder(value, inverse)
    return 1.0 - ripple * horner(COSINE, rest * rest)


def mix(rows, table, inner, spans):
    chunks = inner.shape[0]
    for c in range(chunks):
        inner[c] = jnp.dot(
            rows[:, c * TABLE : (c + 1) * TABLE], table, preferred_element_type=jnp.float32
        )
    return [mix_group(inner, group) for group in spans]


def mix_group(inner, spans):
    chunks = inner.shape[0]
    rows = spans[0].stop - spans[0].start
    for span in spans:
        for lanes in HALVES:
            parts = butterfly([inner[c, span, lanes] for c in range(chunks)])
            for c in range(chunks):
                inner[c, span, lanes] = parts[c]
    largest = jnp.zeros((rows, LANES), jnp.float32)
    for c in range(chunks):
        for lanes in HALVES:
            parts = butterfly([inner[c, span, lanes] for span in spans])
            for span, part in zip(spans, parts):
                inner[c, span, lanes] = part
                largest = jnp.maximum(largest, jnp.abs(part))
    return largest


def quantize_kernel(rows_ref, table_ref, quantized_ref, inner):
    members, count, features = rows_ref.shape
    width = quantized_ref.shape[2]
    chunks, per_shard, per_width = features // TABLE, features // width, width // TABLE
    groups = [
        [slice(t * count + g, t * count + g + STEP) for t in range(members)]
        for g in range(0, count, STEP)
    ]
    rows = rows_ref[...].reshape(members * count, features)
    found = mix(rows, table_ref[...], inner, groups)
    for g, (spans, largest) in enumerate(zip(groups, found)):
        inverse, scale = levels_of(largest)
        here = slice(g * STEP, (g + 1) * STEP)
        for t, span in enumerate(spans):
            for c in range(chunks):
                for l, lanes in enumerate(HALVES):
                    start = (c % per_width) * TABLE + l * LANES
                    block = t * per_shard + c // per_width
                    quantized_ref[block, here, start : start + LANES] = quantized_of(
                        inner[c, span, lanes], inverse, scale
                    ).astype(jnp.bfloat16)


def quantize(rows, table, dp, width):
    members, tokens, features = rows.shape
    count = 2 * STEP
    return pl.pallas_call(
        quantize_kernel,
        grid=(tokens // count,),
        in_specs=[
            pl.BlockSpec((members, count, features), lambda i: (0, i, 0)),
            pl.BlockSpec((TABLE, TABLE), lambda i: (0, 0)),
        ],
        out_specs=pl.BlockSpec((dp, count, width), lambda i: (0, i, 0)),
        scratch_shapes=[pltpu.VMEM((features // TABLE, members * count, TABLE), jnp.float32)],
        out_shape=jax.ShapeDtypeStruct((dp, tokens, width), jnp.bfloat16),
        compiler_params=pltpu.CompilerParams(vmem_limit_bytes=VMEM_BYTES),
        cost_estimate=pl.CostEstimate(
            flops=2 * tokens * WIDTH * BLOCK, bytes_accessed=4 * tokens * WIDTH, transcendentals=0
        ),
    )(rows, table)


def slope_kernel(place, rows_ref, table_ref, slope_ref, inner):
    members, _, features = rows_ref.shape
    devices, _, width = slope_ref.shape
    per_shard, per_width = devices // members, width // TABLE
    spans = [slice(t * STEP, (t + 1) * STEP) for t in range(members)]
    rows = rows_ref[...].reshape(members * STEP, features)
    (largest,) = mix(rows, table_ref[...], inner, [spans])
    inverse, _ = levels_of(largest)
    for block in range(devices):
        for k in range(per_width):
            for l, lanes in enumerate(HALVES):
                c = block % per_shard * per_width + k
                start = k * TABLE + l * LANES
                slope_ref[block, :, start : start + LANES] = slope_of(
                    inner[c, spans[block // per_shard], lanes], inverse
                ).astype(slope_ref.dtype)


def slopes(rows, table, place, dp, width):
    members, tokens, features = rows.shape
    return pl.pallas_call(
        slope_kernel,
        grid_spec=pltpu.PrefetchScalarGridSpec(
            num_scalar_prefetch=1,
            grid=(1,),
            in_specs=[
                pl.BlockSpec((members, STEP, features), lambda i, place: (0, place[0], 0)),
                pl.BlockSpec((TABLE, TABLE), lambda i, place: (0, 0)),
            ],
            out_specs=pl.BlockSpec((dp, STEP, width), lambda i, place: (0, 0, 0)),
            scratch_shapes=[pltpu.VMEM((features // TABLE, members * STEP, TABLE), jnp.float32)],
        ),
        out_shape=jax.ShapeDtypeStruct((dp, STEP, width), jnp.bfloat16),
        compiler_params=pltpu.CompilerParams(vmem_limit_bytes=VMEM_BYTES),
        cost_estimate=pl.CostEstimate(
            flops=2 * STEP * WIDTH * BLOCK, bytes_accessed=8 * STEP * WIDTH, transcendentals=0
        ),
    )(place, rows, table)


def product_kernel(count, position, *refs):
    pieces, weight_ref = refs[:count], refs[count]
    out_ref, results, sems = refs[-3:]
    members = out_ref.shape[0]
    stores = []
    for n, piece_ref in enumerate(pieces):
        slots = piece_ref.shape[0] // (members * STEP)
        result = lax.dot_general(
            piece_ref[...],
            weight_ref[...],
            (((1,), (1,)), ((), ())),
            preferred_element_type=jnp.float32,
        ).astype(out_ref.dtype)
        for k in range(slots):
            for t in range(members):
                start = (k * members + t) * STEP
                results[n, t, k * STEP : (k + 1) * STEP, :] = result[start : start + STEP]
        place = (position * count + n) * slots * STEP
        stores.append(
            pltpu.make_async_copy(
                results.at[n], out_ref.at[:, pl.ds(place, slots * STEP), :], sems.at[n]
            )
        )
        stores[-1].start()
    for store in stores:
        store.wait()


def product(held, pieces, weight, position, members, total):
    count, rows = len(pieces), pieces[0].shape[0]
    width, depth = weight.shape
    earlier = [] if held is None else [held]
    return pl.pallas_call(
        functools.partial(product_kernel, count, position),
        in_specs=[pl.BlockSpec(memory_space=pltpu.VMEM)] * (count + 1)
        + [pl.BlockSpec(memory_space=pltpu.HBM)] * len(earlier),
        out_specs=pl.BlockSpec(memory_space=pltpu.HBM),
        out_shape=pltpu.HBM((members, total // members, width), jnp.bfloat16),
        scratch_shapes=[
            pltpu.VMEM((count, members, rows // members, width), jnp.bfloat16),
            pltpu.SemaphoreType.DMA((count,)),
        ],
        input_output_aliases={count + 1: 0} if earlier else {},
        compiler_params=pltpu.CompilerParams(vmem_limit_bytes=LITTLE_VMEM),
        cost_estimate=pl.CostEstimate(
            flops=2 * count * rows * depth * width,
            bytes_accessed=2 * count * rows * (depth + width),
            transcendentals=0,
        ),
    )(*pieces, weight, *earlier)


def order_kernel(sources, rows_ref, out_ref):
    for slot in range(rows_ref.shape[0]):
        out_ref[sources[slot]] = rows_ref[slot]


def order(rows, sources):
    return pl.pallas_call(
        order_kernel,
        in_specs=[
            pl.BlockSpec(memory_space=pltpu.SMEM),
            pl.BlockSpec(memory_space=pltpu.VMEM),
        ],
        out_specs=pl.BlockSpec(memory_space=pltpu.VMEM),
        out_shape=jax.ShapeDtypeStruct(rows.shape, rows.dtype),
        compiler_params=pltpu.CompilerParams(vmem_limit_bytes=VMEM_BYTES),
    )(sources, rows)


def gradient_kernel(sources, quantized_ref, *refs):
    out_ref = refs[-1]
    pieces = refs[:-1]
    tokens = quantized_ref.shape[1]
    slot = 0
    for number, piece_ref in enumerate(pieces):
        count = piece_ref.shape[0] // tokens
        block = jnp.concatenate(
            [quantized_ref[sources[slot + k]] for k in range(count)], axis=0
        )
        slot += count
        term = lax.dot_general(
            block, piece_ref[...], (((0,), (0,)), ((), ())), preferred_element_type=jnp.float32
        )
        out_ref[...] = term if number == 0 else out_ref[...] + term


def gradient(sources, quantized, pieces):
    width, depth = quantized.shape[2], pieces[0].shape[1]
    rows = sum(piece.shape[0] for piece in pieces)
    return pl.pallas_call(
        gradient_kernel,
        in_specs=[pl.BlockSpec(memory_space=pltpu.SMEM)]
        + [pl.BlockSpec(memory_space=pltpu.VMEM)] * (len(pieces) + 1),
        out_specs=pl.BlockSpec(memory_space=pltpu.VMEM),
        out_shape=jax.ShapeDtypeStruct((width, depth), jnp.float32),
        compiler_params=pltpu.CompilerParams(vmem_limit_bytes=VMEM_BYTES),
        cost_estimate=pl.CostEstimate(
            flops=2 * rows * depth * width,
            bytes_accessed=2 * rows * (depth + width) + 4 * width * depth,
            transcendentals=0,
        ),
    )(sources, quantized, *pieces)


def chip_core(x, y, core):
    return (x % SIDE * SIDE + y % SIDE) * 2 + core


def route(turn, sign):
    pairs = []
    for x in range(SIDE):
        for y in range(SIDE):
            for core in range(2):
                along = (sign, 0) if core == turn else (0, sign)
                pairs.append(
                    (chip_core(x, y, core), chip_core(x + along[0], y + along[1], core))
                )
    return pairs


def send(block, turn, sign):
    return lax.ppermute(block, "dp", route(turn, sign))


def other_core(block):
    return lax.ppermute(block, "dp", [(d, d ^ 1) for d in range(2 * SIDE * SIDE)])


def sources_table():
    table = []
    for x in range(SIDE):
        for y in range(SIDE):
            for core in range(2):
                found = []
                for outer in OFFSETS:
                    for sender in (core, 1 - core):
                        for inner in OFFSETS:
                            along = (inner, outer) if sender == 0 else (outer, inner)
                            found.append(chip_core(x + along[0], y + along[1], sender))
                table.append(found)
    return np.asarray(table, np.int32)


def finish_kernel(summed_ref, slope_ref, table_ref, out_ref, inner):
    devices, step, width = summed_ref.shape
    members, per_width = out_ref.shape[0], width // TABLE
    per_shard = devices // members
    upstream = summed_ref[...].astype(jnp.float32) * slope_ref[...].astype(jnp.float32)
    upstream = upstream.astype(jnp.bfloat16)
    upstream = upstream.reshape(devices * step, width)
    for c in range(per_width):
        inner[c] = jnp.dot(
            upstream[:, c * TABLE : (c + 1) * TABLE],
            table_ref[...],
            preferred_element_type=jnp.float32,
        )
    span = lambda d: slice(d * step, (d + 1) * step)
    for l in range(TABLE // LANES):
        lanes = slice(l * LANES, (l + 1) * LANES)
        for t in range(members):
            near = [(c, span(t * per_shard + k)) for k in range(per_shard) for c in range(per_width)]
            parts = butterfly([inner[c, rows, lanes] for c, rows in near])
            for (c, rows), part in zip(near, parts):
                inner[c, rows, lanes] = part
        for k in range(per_shard):
            for c in range(per_width):
                far = [span(t * per_shard + k) for t in range(members)]
                parts = butterfly([inner[c, rows, lanes] for rows in far])
                start = (k * per_width + c) * TABLE + l * LANES
                for t in range(members):
                    out_ref[t, :, start : start + LANES] = (parts[t] * NORM).astype(out_ref.dtype)


def finish(summed, slope, table, members):
    devices, step, width = summed.shape
    return pl.pallas_call(
        finish_kernel,
        out_shape=jax.ShapeDtypeStruct((members, step, WIDTH // members), jnp.bfloat16),
        scratch_shapes=[pltpu.VMEM((width // TABLE, devices * step, TABLE), jnp.float32)],
        compiler_params=pltpu.CompilerParams(vmem_limit_bytes=LITTLE_VMEM),
        cost_estimate=pl.CostEstimate(
            flops=2 * step * WIDTH * BLOCK, bytes_accessed=8 * step * WIDTH, transcendentals=0
        ),
    )(summed, slope, table)


def shards(activations, weight, grad_out):
    dp = lax.axis_size("dp")
    members = lax.axis_size("tensor")
    tokens, features = activations.shape
    width = weight.shape[0]
    place = lax.axis_index("tensor").astype(jnp.int32).reshape(1)
    sources = jnp.asarray(sources_table())[lax.axis_index("dp")]
    table = hadamard_table(TABLE)
    wide_rows = lax.all_gather(activations, "tensor", axis=0, tiled=False)
    total = dp * tokens

    def multiply(held, pieces, position):
        return product(held, pieces, weight, position, members, total)

    below, above = send(grad_out, 0, 1), send(grad_out, 0, -1)
    top = jnp.concatenate([grad_out, below], axis=0)
    below_top, above_top = send(top, 1, 1), send(top, 1, -1)
    bottom = jnp.concatenate([above, send(grad_out, 0, 2)], axis=0)
    below_bottom, above_bottom = send(bottom, 1, 1), send(bottom, 1, -1)
    far_top = send(below_top, 1, 1)
    near = [top, bottom]
    near_other = [other_core(block) for block in near]
    held = multiply(None, near + near_other, 0)
    below_bottom, above_bottom, held = lax.optimization_barrier(
        (below_bottom, above_bottom, held)
    )
    far_bottom = send(above_bottom, 1, -1)
    below, above = [below_top, below_bottom], [above_top, above_bottom]
    below_other = [other_core(block) for block in below]
    above_other = [other_core(block) for block in above]
    held = multiply(held, below + below_other, 1)
    held = multiply(held, above + above_other, 2)
    far_top, far_bottom, held = lax.optimization_barrier((far_top, far_bottom, held))
    far = [far_top, far_bottom]
    far_other = [other_core(block) for block in far]
    held = multiply(held, far, 6)
    partial_rows = multiply(held, far_other, 7)
    partial_rows, wide_rows = lax.optimization_barrier((partial_rows, wide_rows))
    summed = lax.psum_scatter(partial_rows, "tensor", scatter_dimension=0, tiled=False)
    quantized = quantize(wide_rows, table, dp, width)
    q_block = lax.all_to_all(quantized, "dp", split_axis=0, concat_axis=0, tiled=True)
    summed, wide_rows = lax.optimization_barrier((summed, wide_rows))
    slope = slopes(wide_rows, table, place, dp, width)
    ordered = order(summed.reshape(dp, tokens // members, width), sources)
    ordered, q_block, slope = lax.optimization_barrier((ordered, q_block, slope))
    homed = lax.all_to_all(ordered, "dp", split_axis=0, concat_axis=0, tiled=True)
    mixed = finish(homed, slope, table, members)
    grad_input = lax.all_to_all(mixed, "tensor", split_axis=0, concat_axis=0, tiled=True)
    arrived = near + near_other + below + below_other + above + above_other + far + far_other
    weight_sum = gradient(sources, q_block, arrived)
    return (grad_input.reshape(tokens, features), weight_sum)


def solution(mesh):
    return jax.shard_map(
        shards,
        mesh=mesh,
        in_specs=(P("dp", "tensor"), P("dp", "tensor"), P("dp", "tensor")),
        out_specs=(P("dp", "tensor"), P("dp", "tensor")),
        check_vma=False,
    )
```
